32 devices in a mesh: seq: 4 (over y, core), fsdp: 8 (over z, x).
Axes of the slice: x: 2, y: 2, z: 4, core: 2. Of those that a mesh axis runs over, the one named last changes fastest.
Arguments:
- inputs: bfloat16 [16384, 1024], P(('seq', 'fsdp')), may hold values from -6 to 6
- cotangent: bfloat16 [16384, 1024], P(('seq', 'fsdp')), may hold values from -6 to 6
- lengths: int32 [8, 8], replicated, may hold values from 1 to 1792, 2048 in all within a row
- mixer_weight: float32 [3, 1024, 1024], P(None, 'fsdp'), may hold values from -0.1875 to 0.1875
- strength_weight: float32 [1024, 8], P('fsdp'), may hold values from -0.1875 to 0.1875
- filter_weight: float32 [3, 4, 1024], P(None, None, 'fsdp'), may hold values from -2.5 to 2.5
- norm_gain: float32 [2, 1024], P(None, 'fsdp'), may hold values from 0.5 to 1.5
- head_gain: float32 [128], P('fsdp'), may hold values from 0.5 to 1.5
- output_weight: float32 [1024, 1024], P('fsdp'), may hold values from -0.1875 to 0.1875
- gate_up_weight: float32 [2, 1024, 2816], P(None, 'fsdp'), may hold values from -0.1875 to 0.1875
- down_weight: float32 [2816, 1024], P(None, 'fsdp'), may hold values from -0.109375 to 0.109375
- mixer_moment: float32 [3, 1024, 1024], P(None, 'fsdp'), may hold values from -64 to 64, as said below
- strength_moment: float32 [1024, 8], P('fsdp'), may hold values from -80 to 80
- filter_moment: float32 [3, 4, 1024], P(None, None, 'fsdp'), may hold values from -160 to 160
- gain_moment: float32 [2, 1024], P(None, 'fsdp'), may hold values from -384 to 384
- head_gain_moment: float32 [128], P('fsdp'), may hold values from -768 to 768
- output_moment: float32 [1024, 1024], P('fsdp'), may hold values from -1280 to 1280, as said below
- gate_up_moment: float32 [2, 1024, 2816], P(None, 'fsdp'), may hold values from -384 to 384, as said below
- down_moment: float32 [2816, 1024], P(None, 'fsdp'), may hold values from -640 to 640, as said below
Outputs:
- block_output: float32 [16384, 1024], P(('seq', 'fsdp'))
- input_grad: float32 [16384, 1024], P(('seq', 'fsdp'))
- new_mixer_moment: float32 [3, 1024, 1024], P(None, 'fsdp')
- new_mixer_weight: float32 [3, 1024, 1024], P(None, 'fsdp')
- new_strength_moment: float32 [1024, 8], P('fsdp')
- new_strength_weight: float32 [1024, 8], P('fsdp')
- new_filter_moment: float32 [3, 4, 1024], P(None, None, 'fsdp')
- new_filter_weight: float32 [3, 4, 1024], P(None, None, 'fsdp')
- new_gain_moment: float32 [2, 1024], P(None, 'fsdp')
- new_norm_gain: float32 [2, 1024], P(None, 'fsdp')
- new_head_gain_moment: float32 [128], P('fsdp')
- new_head_gain: float32 [128], P('fsdp')
- new_output_moment: float32 [1024, 1024], P('fsdp')
- new_output_weight: float32 [1024, 1024], P('fsdp')
- new_gate_up_moment: float32 [2, 1024, 2816], P(None, 'fsdp')
- new_gate_up_weight: float32 [2, 1024, 2816], P(None, 'fsdp')
- new_down_moment: float32 [2816, 1024], P(None, 'fsdp')
- new_down_weight: float32 [2816, 1024], P(None, 'fsdp')
The draws below stay inside these ranges and needn't reach their ends.
Inputs may be any that keep to these rules, and one draw needn't show every extreme that they name: `lengths`: each row lists one stream's documents in order; a row sums to 2048, and its longest document has exactly 1792 positions. `mixer_moment`: momentum entries of the query, key and value projections. `output_moment`: momentum entries of the output projection. `gate_up_moment`: momentum entries of the gate and up projections. `down_moment`: momentum entries of the down projection.
All inputs are finite; a program needn't handle non-finite values.
Results may differ from the reference program's by a relative error of at most 0.02.
The reference program's roundings to bfloat16 on the way count: a program that leaves them out, or rounds other values in their place, can miss the bound.
Values may be sent and summed in bfloat16 or wider, within the bound.
A program may use at most 320 MiB of HBM per device.

```python
import math
import jax
import jax.numpy as jnp
import numpy as np
from jax import lax

D = 1024
H = 8
HD = 128
FF = 2816
CONV = 4
SPAN = 64
NDOC = 8
NS_STEPS = 3
TOK_DEV = 512
GROUP_TOK = 2048
TOKENS = 16384
LONGEST = 1792
N_SEQ = 4
N_FSDP = 8


def spread_entries(key, noise_draw, scale_factor, spread):
    row_key, col_key = jax.random.split(key)
    leading = noise_draw.shape[:-2]
    row_total = noise_draw.shape[-2]
    col_total = noise_draw.shape[-1]
    log_spread = math.log(spread)
    row_scale = jnp.exp(jax.random.uniform(row_key, leading + (row_total, 1), jnp.float32) * log_spread)
    col_scale = jnp.exp(jax.random.uniform(col_key, leading + (1, col_total), jnp.float32) * log_spread)
    mean_square = (spread * spread - 1.0) / (2.0 * log_spread)
    return jnp.clip(noise_draw * row_scale * col_scale / mean_square, -10.0, 10.0) * scale_factor


def draw_mixer_moment(key, part):
    key = jax.random.fold_in(key, 11)
    noise_key, scale_key = jax.random.split(key)
    shape_tuple = (3, D, D)
    noise_draw = jax.random.normal(noise_key, shape_tuple, jnp.float32)
    spread = 10.0
    return spread_entries(scale_key, noise_draw, 0.05 * TOKENS ** 0.5, spread)


def draw_output_moment(key, part):
    key = jax.random.fold_in(key, 12)
    noise_key, scale_key = jax.random.split(key)
    shape_tuple = (D, D)
    noise_draw = jax.random.normal(noise_key, shape_tuple, jnp.float32)
    spread = 10.0
    return spread_entries(scale_key, noise_draw, TOKENS ** 0.5, spread)


def draw_gate_up_moment(key, part):
    key = jax.random.fold_in(key, 13)
    noise_key, scale_key = jax.random.split(key)
    shape_tuple = (2, D, FF)
    noise_draw = jax.random.normal(noise_key, shape_tuple, jnp.float32)
    spread = 10.0
    return spread_entries(scale_key, noise_draw, 0.3 * TOKENS ** 0.5, spread)


def draw_down_moment(key, part):
    key = jax.random.fold_in(key, 14)
    noise_key, scale_key = jax.random.split(key)
    shape_tuple = (FF, D)
    noise_draw = jax.random.normal(noise_key, shape_tuple, jnp.float32)
    spread = 10.0
    return spread_entries(scale_key, noise_draw, 0.5 * TOKENS ** 0.5, spread)


def shard_levels(key, shape, pieces, least, top_value):
    gain, own = 1.0, jax.random.fold_in(key, 6)
    for dim, parts in pieces:
        heights = jnp.exp(jax.random.uniform(jax.random.fold_in(own, dim), (parts,), jnp.float32, least / len(pieces), top_value / len(pieces)))
        gain = gain * jnp.repeat(heights, shape[dim] // parts).reshape([-1 if axis == dim else 1 for axis in range(len(shape))])
    return gain


def split_up(number_of, total, limit, skew):
    portions = [(1 << 20) // math.isqrt(standing ** skew) + 1 for standing in range(2, number_of + 1)]
    spare, given = total - limit - (number_of - 1), [1] * (number_of - 1)
    while spare > 0:
        movable = [i for i in range(number_of - 1) if given[i] < limit]
        pool, left = sum([portions[i] for i in movable]), spare
        for i in movable:
            addition = min(limit - given[i], max(1, left * portions[i] // pool), spare)
            given[i] = given[i] + addition
            spare = spare - addition
    return np.array([limit] + given)


def uneven(stream_key, amount, total, bound, lean):
    if amount == 2:
        one = jax.random.randint(stream_key, (), max(1, total - bound), min(bound, total - 1) + 1)
        return jnp.stack([one, total - one])
    tallies = jnp.asarray(split_up(amount, total, bound, lean), jnp.int32)
    twos = (amount - 1) // 2
    source_of, receiver = tallies[1:1 + 2 * twos:2], tallies[2:2 + 2 * twos:2]
    slack = jnp.minimum(source_of - 1, bound - receiver)
    moved = jax.random.randint(jax.random.fold_in(stream_key, 1), (twos,), 0, 1 << 20) % (slack + 1)
    tallies = tallies.at[1:1 + 2 * twos:2].set(source_of - moved).at[2:2 + 2 * twos:2].set(receiver + moved)
    return tallies[jax.random.permutation(jax.random.fold_in(stream_key, 2), amount)]


def scatter_about(stream_key, extent, deviation, limit, cuts=(), kind=jnp.bfloat16):
    entries = jax.random.normal(stream_key, extent, jnp.float32) * deviation
    if len(cuts) > 0:
        entries = shard_levels(stream_key, extent, cuts, -0.22, 0.18) * entries
    return jnp.clip(entries, min=-limit, max=limit).astype(kind)


def setup_inputs(seed: int = 0) -> dict:
    keys = jax.random.split(jax.random.key(seed), 20)
    inputs = scatter_about(keys[0], (TOKENS, D), 1.0, 6.0, ((0, 32),))
    cotangent = scatter_about(keys[1], (TOKENS, D), 1.0, 6.0, ((0, 32),))
    lengths = jax.vmap(lambda own: uneven(own, NDOC, GROUP_TOK, LONGEST, 2))(jax.random.split(keys[2], N_FSDP)).reshape((N_FSDP, NDOC)).astype(jnp.int32)
    mixer_weight = scatter_about(keys[3], (3, D, D), D ** -0.5, 0.1875, ((1, 8),), jnp.float32)
    strength_weight = scatter_about(keys[4], (D, H), D ** -0.5, 0.1875, ((0, 8),), jnp.float32)
    filter_weight = scatter_about(keys[5], (3, CONV, D), 0.5, 2.5, ((2, 8),), jnp.float32)
    norm_gain = jnp.clip(1.0 + 0.1 * jax.random.normal(keys[6], (2, D), jnp.float32), 0.5, 1.5)
    head_gain = jnp.clip(1.0 + 0.1 * jax.random.normal(keys[7], (HD,), jnp.float32), 0.5, 1.5)
    output_weight = scatter_about(keys[8], (D, D), D ** -0.5, 0.1875, ((0, 8),), jnp.float32)
    gate_up_weight = scatter_about(keys[9], (2, D, FF), D ** -0.5, 0.1875, ((1, 8),), jnp.float32)
    down_weight = scatter_about(keys[10], (FF, D), FF ** -0.5, 0.109375, ((1, 8),), jnp.float32)
    mixer_moment = draw_mixer_moment(jax.random.fold_in(keys[19], 71), 0)
    strength_moment = scatter_about(keys[12], (D, H), (0.1 * TOKENS ** 0.5), 80.0, ((0, 8),), jnp.float32)
    filter_moment = scatter_about(keys[13], (3, CONV, D), (0.2 * TOKENS ** 0.5), 160.0, ((2, 8),), jnp.float32)
    gain_moment = scatter_about(keys[14], (2, D), (0.5 * TOKENS ** 0.5), 384.0, ((1, 8),), jnp.float32)
    head_gain_moment = scatter_about(keys[15], (HD,), (1.0 * TOKENS ** 0.5), 768.0, ((0, 8),), jnp.float32)
    output_moment = draw_output_moment(jax.random.fold_in(keys[19], 71), 0)
    gate_up_moment = draw_gate_up_moment(jax.random.fold_in(keys[19], 71), 0)
    down_moment = draw_down_moment(jax.random.fold_in(keys[19], 71), 0)
    return dict(inputs=inputs, cotangent=cotangent, lengths=lengths, mixer_weight=mixer_weight, strength_weight=strength_weight, filter_weight=filter_weight, norm_gain=norm_gain, head_gain=head_gain, output_weight=output_weight, gate_up_weight=gate_up_weight, down_weight=down_weight, mixer_moment=mixer_moment, strength_moment=strength_moment, filter_moment=filter_moment, gain_moment=gain_moment, head_gain_moment=head_gain_moment, output_moment=output_moment, gate_up_moment=gate_up_moment, down_moment=down_moment)


norm_eps = 1e-06
head_eps = 0.001
momentum_decay = 0.9
matrix_rate = 1.0
filter_rate = 0.01
gain_rate = 0.001
strength_rate = 0.001
coef_linear = 3.4445
coef_cubic = -4.775
coef_quintic = 2.0315

@jax.custom_vjp
def low(v):
    return lax.optimization_barrier(v.astype(jnp.bfloat16)).astype(jnp.float32)

@jax.custom_vjp
def low_back(v):
    return v

def low_keep(v):
    return (low(v), None)

def low_pass(kept, grad):
    return (grad,)

def back_keep(v):
    return (v, None)

def back_low(kept, grad):
    return (low(grad),)
low.defvjp(low_keep, low_pass)
low_back.defvjp(back_keep, back_low)

def rms_scale(values, gain_vector):
    return values * lax.rsqrt(lax.optimization_barrier(jnp.mean(values * values, axis=-1, keepdims=True)) + norm_eps) * gain_vector

def head_rms(values, gain_vector):
    return values * lax.rsqrt(lax.optimization_barrier(jnp.mean(values * values, axis=-1, keepdims=True)) + head_eps) * gain_vector

def unit_rows(values):
    return values * lax.rsqrt(lax.optimization_barrier(jnp.sum(values * values, axis=-1, keepdims=True)) + norm_eps)

def token_piece(extended, filters, logits, valid_mask):
    row_count = logits.shape[0]
    filter_len = filters.shape[1]
    summed = jnp.zeros((row_count,) + extended.shape[1:], jnp.float32)
    for lag_index in range(filter_len):
        offset = filter_len - 1 - lag_index
        summed = summed + valid_mask[lag_index][:, None, None] * extended[offset:offset + row_count] * filters[:, lag_index, :][None]
    activated = jax.nn.silu(summed)
    heads_view = activated.reshape(row_count, 3, -1, HD)
    query_rows = unit_rows(heads_view[:, 0]) * HD ** (-0.5)
    key_rows = unit_rows(heads_view[:, 1])
    mixed = jnp.stack([query_rows, key_rows, heads_view[:, 2]], axis=1).reshape(row_count, 3, -1)
    return (mixed, jax.nn.sigmoid(logits))

def delta_block(state_in, block_items):

    def token_step(carry_state, token_items):
        query_row, key_row, value_row, strength_row, start_flag = token_items
        carry_state = carry_state * (1.0 - start_flag)
        update = strength_row[:, None] * (value_row - jnp.einsum('hvk,hk->hv', carry_state, key_row, precision=lax.Precision.HIGHEST))
        carry_state = carry_state + update[:, :, None] * key_row[:, None, :]
        return (carry_state, jnp.einsum('hvk,hk->hv', carry_state, query_row, precision=lax.Precision.HIGHEST))
    return lax.scan(token_step, state_in, block_items)

def stream_forward(stream, lengths_row, params):
    mixer_low, strength_low, filter_low, gain_low, head_gain_low, output_low, gate_up_low, down_low = params
    highest = lax.Precision.HIGHEST
    positions = jnp.arange(GROUP_TOK, dtype=jnp.int32)
    doc_ends = jnp.cumsum(lengths_row).astype(jnp.int32)
    passed = (positions[:, None] >= doc_ends[None, :]).astype(jnp.int32)
    doc_first = lax.optimization_barrier(jnp.sum(passed * lengths_row[None, :], axis=1)).astype(jnp.int32)
    valid_mask = jnp.stack([(positions - lag_index >= doc_first).astype(jnp.float32) for lag_index in range(CONV)])
    normed = low(rms_scale(stream, gain_low[0]))
    projected = low_back(low(jnp.einsum('td,jde->tje', normed, mixer_low, precision=highest)))
    logits = low_back(jnp.dot(normed, strength_low, precision=highest))
    extended = jnp.concatenate([jnp.zeros((CONV - 1, 3, D), jnp.float32), projected], axis=0)
    mixed, strength = token_piece(extended, filter_low, logits, valid_mask)
    mixed = low_back(low(mixed))
    strength = low_back(low(strength))
    start_flag = (positions == doc_first).astype(jnp.float32)
    block_count = GROUP_TOK // SPAN
    heads_view = mixed.reshape(block_count, SPAN, 3, H, HD)
    block_items = (heads_view[:, :, 0], heads_view[:, :, 1], heads_view[:, :, 2], strength.reshape(block_count, SPAN, H), start_flag.reshape(block_count, SPAN))
    ignored, delta_out = lax.scan(jax.checkpoint(delta_block), jnp.zeros((H, HD, HD), jnp.float32), block_items)
    head_normed = low_back(low(head_rms(delta_out.reshape(GROUP_TOK, H, HD), head_gain_low).reshape(GROUP_TOK, D)))
    attention = low_back(jnp.dot(head_normed, output_low, precision=highest))
    residual = stream + attention
    normed_two = low(rms_scale(residual, gain_low[1]))
    gate_up_value = jnp.einsum('td,jdf->jtf', normed_two, gate_up_low, precision=highest)
    gate_value = low_back(gate_up_value[0])
    up_value = low_back(gate_up_value[1])
    hidden = low(jax.nn.silu(gate_value) * up_value)
    return residual + low_back(jnp.dot(hidden, down_low, precision=highest))

def orthogonalize(matrix):
    highest = lax.Precision.HIGHEST
    current = matrix / (jnp.sqrt(jnp.sum(matrix * matrix)) + 1e-07)
    for sweep_index in range(NS_STEPS):
        square = jnp.dot(current, current.T, precision=highest)
        mapped = coef_cubic * square + coef_quintic * jnp.dot(square, square, precision=highest)
        current = coef_linear * current + jnp.dot(mapped, current, precision=highest)
    return current

def reference(inputs, cotangent, lengths, mixer_weight, strength_weight, filter_weight, norm_gain, head_gain, output_weight, gate_up_weight, down_weight, mixer_moment, strength_moment, filter_moment, gain_moment, head_gain_moment, output_moment, gate_up_moment, down_moment):
    weights = (mixer_weight, strength_weight, filter_weight, norm_gain, head_gain, output_weight, gate_up_weight, down_weight)

    def whole_forward(rows_in, *params):
        rounded = tuple((low(param_array) for param_array in params))
        grouped = rows_in.reshape(N_SEQ, N_FSDP, TOK_DEV, D).transpose(1, 0, 2, 3).reshape(N_FSDP, GROUP_TOK, D)

        def one_stream(stream_pair):
            return stream_forward(stream_pair[0], stream_pair[1], rounded)
        streams_out = lax.map(jax.checkpoint(one_stream), (grouped, lengths))
        return streams_out.reshape(N_FSDP, N_SEQ, TOK_DEV, D).transpose(1, 0, 2, 3).reshape(TOKENS, D)
    block_output, pullback = jax.vjp(whole_forward, inputs.astype(jnp.float32), *weights)
    gradients = pullback(cotangent.astype(jnp.float32))
    input_grad = gradients[0]
    moments = (mixer_moment, strength_moment, filter_moment, gain_moment, head_gain_moment, output_moment, gate_up_moment, down_moment)
    fresh = tuple((momentum_decay * prior + gradient for prior, gradient in zip(moments, gradients[1:])))
    new_mixer = mixer_weight - matrix_rate * jnp.stack([orthogonalize(fresh[0][matrix_index]) for matrix_index in range(3)])
    new_output = output_weight - matrix_rate * orthogonalize(fresh[5])
    new_gate_up = gate_up_weight - matrix_rate * jnp.stack([orthogonalize(fresh[6][matrix_index]) for matrix_index in range(2)])
    new_down = down_weight - matrix_rate * orthogonalize(fresh[7].T).T
    new_strength = strength_weight - strength_rate * fresh[1]
    new_filter = filter_weight - filter_rate * fresh[2]
    new_gain = norm_gain - gain_rate * fresh[3]
    new_head = head_gain - gain_rate * fresh[4]
    return (block_output, input_grad, fresh[0], new_mixer, fresh[1], new_strength, fresh[2], new_filter, fresh[3], new_gain, fresh[4], new_head, fresh[5], new_output, fresh[6], new_gate_up, fresh[7], new_down)
```

```python
from functools import partial

import jax
import jax.numpy as jnp
from jax import lax
from jax.experimental import pallas as pl
from jax.experimental.pallas import tpu as pltpu
from jax.sharding import PartitionSpec as P

HD = 128
CONV = 4
BLOCK = 128
GROUP = 8
RIM = 16
NS_STEPS = 3

norm_eps = 1e-06
head_eps = 0.001
momentum_decay = 0.9
matrix_rate = 1.0
filter_rate = 0.01
gain_rate = 0.001
strength_rate = 0.001
coef_linear = 3.4445
coef_cubic = -4.775
coef_quintic = 2.0315

LOW = jnp.bfloat16
FULL = jnp.float32


def halves(values):
    top = values.astype(LOW)
    return (top, (values - top.astype(FULL)).astype(LOW))


def product(left, right, dims=(1, 0)):
    left = left if isinstance(left, tuple) else (left,)
    right = right if isinstance(right, tuple) else (right,)
    total = None
    for i, a in enumerate(left):
        for j, b in enumerate(right):
            if i + j < 2:
                term = lax.dot_general(
                    a, b, (((dims[0],), (dims[1],)), ((), ())), preferred_element_type=FULL
                )
                total = term if total is None else total + term
    return total


def low_product(left, right, dims=(1, 0)):
    return product(left.astype(LOW), right.astype(LOW), dims)


def lanes(values, head):
    return values[:, head * HD : (head + 1) * HD]


def unit_scale(values):
    return lax.rsqrt(jnp.sum(values * values, axis=-1, keepdims=True) + norm_eps)


def block_ids():
    rows = lax.broadcasted_iota(jnp.int32, (BLOCK, BLOCK), 0)
    cols = lax.broadcasted_iota(jnp.int32, (BLOCK, BLOCK), 1)
    return rows, cols


def short_conv(current, previous, taps, meta):
    joined = jnp.concatenate([previous, current], axis=0)
    total = None
    shifted = []
    for lag in range(CONV):
        moved = joined if lag == 0 else pltpu.roll(joined, lag, 0)
        moved = moved[RIM:] * meta[:, lag : lag + 1]
        shifted.append(moved)
        term = moved * taps[lag : lag + 1, :]
        total = term if total is None else total + term
    return total, shifted


def inverse(system, differ):
    rows, cols = block_ids()
    eye = jnp.where(rows == cols, 1.0, 0.0).astype(FULL)
    found = [eye - jnp.where((differ >> 0) == 1, one, 0.0) for one in system]
    level = 1
    while (1 << level) < BLOCK:
        picked = [jnp.where((differ >> level) == 1, one, 0.0).astype(LOW) for one in system]
        low = [one.astype(LOW) for one in found]
        inner = [product(a, b).astype(LOW) for a, b in zip(picked, low)]
        outer = [product(b, a) for a, b in zip(inner, low)]
        found = [a - b for a, b in zip(found, outer)]
        level += 1
    split = [halves(one) for one in found]
    wide = [halves(one) for one in system]
    error = [eye - a - product(b, c) for a, b, c in zip(found, wide, split)]
    return [a + product(b[0], c.astype(LOW)) for a, b, c in zip(found, split, error)]


def forward_kernel(
    proj_ref, prev_ref, rim_ref, taps_ref, strength_ref, strength_row_ref, meta_ref, meta_row_ref,
    mixed_ref, solve_ref, weight_ref, update_ref, drift_ref, out_ref, query_ref, state_ref, end_ref, transfer_ref,
    carry_ref,
):
    step = pl.program_id(1)
    rows, cols = block_ids()
    meta = meta_ref[...]
    carry, tail, segment = meta[:, 4:5], meta[:, 5:6], meta[:, 6:7]
    same = segment == meta_row_ref[0:1, :]
    strict = (rows > cols) & same
    inclusive = (rows >= cols) & same
    differ = rows ^ cols
    carry_last = carry[BLOCK - 1 : BLOCK, :]

    @pl.when(step == 0)
    def _():
        start = jnp.concatenate(
            [jnp.zeros((HD, HD), FULL), jnp.where(rows == cols, 1.0, 0.0).astype(FULL)], axis=1
        )
        for head in range(GROUP):
            carry_ref[head] = start

    first = step == 0
    parts = []
    for j in range(3):
        at = slice(j * GROUP * HD, (j + 1) * GROUP * HD)
        previous = jnp.where(first, rim_ref[:, at].astype(FULL), prev_ref[:, at].astype(FULL))
        conv, _ = short_conv(proj_ref[:, at].astype(FULL), previous, taps_ref[j], meta)
        parts.append(conv * jax.nn.sigmoid(conv))
    queries, keys, values = [], [], []
    for head in range(GROUP):
        query, key = lanes(parts[0], head), lanes(parts[1], head)
        queries.append((query * (unit_scale(query) * HD ** (-0.5))).astype(LOW))
        keys.append((key * unit_scale(key)).astype(LOW))
        values.append(lanes(parts[2], head).astype(LOW))
        mixed_ref[0, :, head * HD : (head + 1) * HD] = queries[head]
        mixed_ref[1, :, head * HD : (head + 1) * HD] = keys[head]
        mixed_ref[2, :, head * HD : (head + 1) * HD] = values[head]
    strength = strength_ref[0]
    strength_row = strength_row_ref[0]
    heads = range(GROUP)
    gram = [product(keys[h], keys[h], (1, 1)) for h in heads]
    system = [jnp.where(strict, strength[:, h : h + 1] * gram[h], 0.0) for h in heads]
    scores = [jnp.where(inclusive, product(queries[h], keys[h], (1, 1)), 0.0) for h in heads]
    solve = inverse(system, differ)
    carry_low, tail_low = carry.astype(LOW), tail.astype(LOW)
    carried_query = [queries[h] * carry_low for h in heads]
    tail_key = [keys[h] * tail_low for h in heads]
    right = [jnp.concatenate([values[h], keys[h] * carry_low], axis=1) for h in heads]
    solved = [product(halves(solve[h] * strength_row[h : h + 1, :]), right[h]) for h in heads]
    state = [carry_ref[h] for h in heads]
    state_parts = [halves(state[h]) for h in heads]
    passed = [product(halves(solved[h][:, HD:]), state_parts[h]) for h in heads]
    zero = jnp.zeros((BLOCK, HD), FULL)
    both = [
        jnp.concatenate([solved[h][:, :HD], zero], axis=1) - passed[h] for h in heads
    ]
    both_parts = [halves(both[h]) for h in heads]
    result = [
        product(carried_query[h], state_parts[h]) + product(halves(scores[h]), both_parts[h])
        for h in heads
    ]
    after = [
        carry_last * state[h] + product(tail_key[h], both_parts[h], (0, 0)) for h in heads
    ]
    for h in heads:
        solve_ref[0, h] = solve[h].astype(LOW)
        at = slice(h * HD, (h + 1) * HD)
        weight_ref[:, at] = solved[h][:, HD:].astype(LOW)
        update_ref[:, at] = both[h][:, :HD]
        drift_ref[:, at] = both[h][:, HD:].astype(LOW)
        out_ref[:, at] = result[h][:, :HD]
        query_ref[:, at] = result[h][:, HD:]
        state_ref[0, h] = state[h]
        carry_ref[h] = after[h]
        end_ref[h] = after[h][:, :HD]
        transfer_ref[h] = after[h][:, HD:]


def forward_blocks(projected, rim, taps, strength, meta, meta_row):
    total = projected.shape[0]
    width = projected.shape[1] // 3
    head_count = width // HD
    groups, steps = head_count // GROUP, total // BLOCK
    span = GROUP * HD
    grouped = strength.reshape(total, groups, GROUP)
    strength_col = grouped.transpose(1, 0, 2)
    strength_row = grouped.transpose(1, 2, 0)
    rows_of = lambda g, n: (n, g)
    shapes = (
        jax.ShapeDtypeStruct((3, total, width), LOW),
        jax.ShapeDtypeStruct((steps, head_count, BLOCK, BLOCK), LOW),
        jax.ShapeDtypeStruct((total, width), LOW),
        jax.ShapeDtypeStruct((total, width), FULL),
        jax.ShapeDtypeStruct((total, width), LOW),
        jax.ShapeDtypeStruct((total, width), FULL),
        jax.ShapeDtypeStruct((total, width), FULL),
        jax.ShapeDtypeStruct((steps, head_count, HD, 2 * HD), FULL),
        jax.ShapeDtypeStruct((head_count, HD, HD), FULL),
        jax.ShapeDtypeStruct((head_count, HD, HD), FULL),
    )
    wide = pl.BlockSpec((BLOCK, span), rows_of)
    ratio = BLOCK // RIM
    return pl.pallas_call(
        forward_kernel,
        grid=(groups, steps),
        in_specs=[
            pl.BlockSpec((BLOCK, 3 * span), rows_of),
            pl.BlockSpec((RIM, 3 * span), lambda g, n: (jnp.maximum(n * ratio - 1, 0), g)),
            pl.BlockSpec((RIM, 3 * span), lambda g, n: (0, g)),
            pl.BlockSpec((3, CONV, span), lambda g, n: (0, 0, g)),
            pl.BlockSpec((1, BLOCK, GROUP), lambda g, n: (g, n, 0)),
            pl.BlockSpec((1, GROUP, BLOCK), lambda g, n: (g, 0, n)),
            pl.BlockSpec((BLOCK, 8), lambda g, n: (n, 0)),
            pl.BlockSpec((8, BLOCK), lambda g, n: (0, n)),
        ],
        out_specs=(
            pl.BlockSpec((3, BLOCK, span), lambda g, n: (0, n, g)),
            pl.BlockSpec((1, GROUP, BLOCK, BLOCK), lambda g, n: (n, g, 0, 0)),
            wide,
            wide,
            wide,
            wide,
            wide,
            pl.BlockSpec((1, GROUP, HD, 2 * HD), lambda g, n: (n, g, 0, 0)),
            pl.BlockSpec((GROUP, HD, HD), lambda g, n: (g, 0, 0)),
            pl.BlockSpec((GROUP, HD, HD), lambda g, n: (g, 0, 0)),
        ),
        out_shape=shapes,
        scratch_shapes=[pltpu.VMEM((GROUP, HD, 2 * HD), FULL)],
        compiler_params=pltpu.CompilerParams(vmem_limit_bytes=48 << 20),
        cost_estimate=pl.CostEstimate(flops=8 << 30, bytes_accessed=24 << 20, transcendentals=0),
    )(projected, projected, rim, taps, strength_col, strength_row, meta, meta_row)


def out_kernel(local_ref, query_ref, state_ref, gain_ref, delta_ref, normed_ref):
    gain = gain_ref[0:1, :]
    for head in range(local_ref.shape[1] // HD):
        at = slice(head * HD, (head + 1) * HD)
        value = local_ref[:, at] + product(halves(query_ref[:, at]), halves(state_ref[head]))
        delta_ref[:, at] = value
        scale = lax.rsqrt(jnp.mean(value * value, axis=-1, keepdims=True) + head_eps)
        normed_ref[:, at] = (value * scale * gain).astype(LOW)


def head_outputs(local_out, effective, state_in, gain):
    total, width = local_out.shape
    rows = pl.BlockSpec((BLOCK, width), lambda n: (n, 0))
    return pl.pallas_call(
        out_kernel,
        grid=(total // BLOCK,),
        in_specs=[
            rows,
            rows,
            pl.BlockSpec(state_in.shape, lambda n: (0, 0, 0)),
            pl.BlockSpec((1, HD), lambda n: (0, 0)),
        ],
        out_specs=(rows, rows),
        out_shape=(
            jax.ShapeDtypeStruct((total, width), FULL),
            jax.ShapeDtypeStruct((total, width), LOW),
        ),
        compiler_params=pltpu.CompilerParams(vmem_limit_bytes=32 << 20),
    )(local_out, effective, state_in, gain)


def head_back_kernel(grad_ref, delta_ref, query_ref, gain_ref, upstream_ref, adjoint_ref, gain_grad_ref):
    step = pl.program_id(0)
    gain = gain_ref[0:1, :]

    @pl.when(step == 0)
    def _():
        adjoint_ref[...] = jnp.zeros_like(adjoint_ref)
        gain_grad_ref[...] = jnp.zeros_like(gain_grad_ref)

    gained = jnp.zeros((1, HD), FULL)
    for head in range(grad_ref.shape[1] // HD):
        at = slice(head * HD, (head + 1) * HD)
        value = delta_ref[:, at]
        grad = grad_ref[:, at].astype(FULL)
        scale = lax.rsqrt(jnp.mean(value * value, axis=-1, keepdims=True) + head_eps)
        unit = value * scale
        gained = gained + jnp.sum(grad * unit, axis=0, keepdims=True)
        grad = grad * gain
        back = scale * (grad - unit * jnp.mean(grad * unit, axis=-1, keepdims=True))
        low = back.astype(LOW)
        upstream_ref[:, at] = low
        adjoint_ref[head] += product(query_ref[:, at].astype(LOW), low, (0, 0))
    gain_grad_ref[...] += gained


def head_back(grad_normed, delta_out, effective, gain):
    total, width = delta_out.shape
    head_count = width // HD
    rows = pl.BlockSpec((BLOCK, width), lambda n: (n, 0))
    return pl.pallas_call(
        head_back_kernel,
        grid=(total // BLOCK,),
        in_specs=[rows, rows, rows, pl.BlockSpec((1, HD), lambda n: (0, 0))],
        out_specs=(
            rows,
            pl.BlockSpec((head_count, HD, HD), lambda n: (0, 0, 0)),
            pl.BlockSpec((1, HD), lambda n: (0, 0)),
        ),
        out_shape=(
            jax.ShapeDtypeStruct((total, width), LOW),
            jax.ShapeDtypeStruct((head_count, HD, HD), FULL),
            jax.ShapeDtypeStruct((1, HD), FULL),
        ),
        compiler_params=pltpu.CompilerParams(vmem_limit_bytes=32 << 20),
    )(grad_normed, delta_out, effective, gain)


def backward_kernel(
    proj_ref, prev_ref, rim_ref, taps_ref, strength_ref, meta_ref, meta_row_ref,
    mixed_ref, solve_ref, weight_ref, update_ref, drift_ref, upstream_ref, state_ref, enter_ref, leave_ref,
    grad_ref, strength_grad_ref, taps_grad_ref, edge_ref, lead_ref,
    adjoint_ref, spill_ref,
):
    turn = pl.program_id(1)
    last_turn = pl.num_programs(1) - 1
    rows, cols = block_ids()
    meta = meta_ref[...]
    carry, tail, segment = meta[:, 4:5], meta[:, 5:6], meta[:, 6:7]
    same = segment == meta_row_ref[0:1, :]
    strict = (rows > cols) & same
    inclusive = (rows >= cols) & same
    carry_last = carry[BLOCK - 1 : BLOCK, :]
    carry_low, tail_low = carry.astype(LOW), tail.astype(LOW)
    heads = range(GROUP)

    @pl.when(turn == 0)
    def _():
        for h in heads:
            adjoint_ref[h] = leave_ref[h]
        spill_ref[...] = jnp.zeros_like(spill_ref)
        taps_grad_ref[...] = jnp.zeros_like(taps_grad_ref)

    strength = strength_ref[0]
    at = [slice(h * HD, (h + 1) * HD) for h in heads]
    query = [mixed_ref[0, :, at[h]] for h in heads]
    key = [mixed_ref[1, :, at[h]] for h in heads]
    value = [mixed_ref[2, :, at[h]] for h in heads]
    upstream = [upstream_ref[:, at[h]] for h in heads]
    enter = [enter_ref[h].astype(LOW) for h in heads]
    state = [
        (state_ref[0, h, :, :HD] + product(state_ref[0, h, :, HD:].astype(LOW), enter[h])).astype(LOW)
        for h in heads
    ]
    update = [
        (update_ref[:, at[h]] + product(drift_ref[:, at[h]], enter[h])).astype(LOW) for h in heads
    ]
    gram = [product(key[h], key[h], (1, 1)) for h in heads]
    scores = [
        jnp.where(inclusive, product(query[h], key[h], (1, 1)), 0.0).astype(LOW) for h in heads
    ]
    tail_key = [key[h] * tail_low for h in heads]
    adjoint = [adjoint_ref[h] for h in heads]
    adjoint_low = [adjoint[h].astype(LOW) for h in heads]
    grad_update = [
        (product(scores[h], upstream[h], (0, 0)) + product(tail_key[h], adjoint_low[h])).astype(LOW)
        for h in heads
    ]
    for h in heads:
        adjoint_ref[h] = (
            carry_last * adjoint[h]
            + product(query[h] * carry_low, upstream[h], (0, 0))
            - product(weight_ref[:, at[h]], grad_update[h], (0, 0))
        )
    grad_right = [product(solve_ref[0, h], grad_update[h], (0, 0)) for h in heads]
    right_low = [grad_right[h].astype(LOW) for h in heads]
    grad_scores = [
        jnp.where(inclusive, product(upstream[h], update[h], (1, 1)), 0.0).astype(LOW) for h in heads
    ]
    grad_query = [
        carry * product(upstream[h], state[h], (1, 1)) + product(grad_scores[h], key[h]) for h in heads
    ]
    right_state = [product(right_low[h], state[h], (1, 1)) for h in heads]
    grad_system = [
        jnp.where(strict, -product(right_low[h], update[h], (1, 1)), 0.0) for h in heads
    ]
    beta = [strength[:, h : h + 1] for h in heads]
    grad_gram = [(beta[h] * grad_system[h]).astype(LOW) for h in heads]
    grad_key = [
        product(grad_scores[h], query[h], (0, 0))
        + tail * product(update[h], adjoint_low[h], (1, 1))
        - (beta[h] * carry) * right_state[h]
        + product(grad_gram[h], key[h])
        + product(grad_gram[h], key[h], (0, 0))
        for h in heads
    ]
    grad_value = [beta[h] * grad_right[h] for h in heads]
    columns = [
        jnp.sum(
            grad_right[h] * value[h].astype(FULL)
            - carry * right_state[h] * key[h].astype(FULL)
            + grad_system[h] * gram[h],
            axis=-1,
            keepdims=True,
        )
        for h in heads
    ]
    strength_grad_ref[0] = jnp.concatenate(columns, axis=1)

    def rounded(values):
        return values.astype(LOW).astype(FULL)

    first = turn == last_turn
    grads = (grad_query, grad_key, grad_value)
    span = GROUP * HD
    for j in range(3):
        at = slice(j * span, (j + 1) * span)
        previous = jnp.where(first, rim_ref[:, at].astype(FULL), prev_ref[:, at].astype(FULL))
        taps = taps_ref[j]
        conv, shifted = short_conv(proj_ref[:, at].astype(FULL), previous, taps, meta)
        gate = jax.nn.sigmoid(conv)
        active = conv * gate
        pieces = []
        for h in heads:
            grad = rounded(grads[j][h])
            if j < 2:
                raw = lanes(active, h)
                scale = unit_scale(raw)
                unit = raw * scale
                if j == 0:
                    grad = grad * HD ** (-0.5)
                grad = scale * (grad - unit * jnp.sum(unit * grad, axis=-1, keepdims=True))
            pieces.append(grad)
        grad_conv = jnp.concatenate(pieces, axis=1) * (gate * (1.0 + conv * (1.0 - gate)))
        total = None
        for lag in range(CONV):
            taps_grad_ref[j, lag : lag + 1, :] += jnp.sum(grad_conv * shifted[lag], axis=0, keepdims=True)
            spread = grad_conv * (meta[:, lag : lag + 1] * taps[lag : lag + 1, :])
            spread = jnp.concatenate([jnp.zeros((8, span), FULL), spread], axis=0)
            if lag:
                spread = pltpu.roll(spread, BLOCK + 8 - lag, 0)
            total = spread if total is None else total + spread
        bottom = total[BLOCK:] + spill_ref[j]
        spill_ref[j] = total[:8]
        grad_ref[:, at] = jnp.concatenate([total[8:BLOCK], bottom], axis=0).astype(LOW)

        @pl.when(turn == 0)
        def _():
            edge_ref[:, at] = bottom

        lead_ref[:, at] = total[:8]


def backward_blocks(
    projected, rim, taps, strength, meta, meta_row, mixed, solve, weight, update, drift, upstream,
    states, enter, leave,
):
    total, width = projected.shape[0], projected.shape[1] // 3
    head_count = width // HD
    groups, steps = head_count // GROUP, total // BLOCK
    span = GROUP * HD
    strength_col = strength.reshape(total, groups, GROUP).transpose(1, 0, 2)
    ratio = BLOCK // RIM
    back = lambda n: steps - 1 - n
    wide = pl.BlockSpec((BLOCK, span), lambda g, n: (back(n), g))
    deep = pl.BlockSpec((3, BLOCK, span), lambda g, n: (0, back(n), g))
    per_group = pl.BlockSpec((GROUP, HD, HD), lambda g, n: (g, 0, 0))
    flat = pl.BlockSpec((BLOCK, 3 * span), lambda g, n: (back(n), g))
    narrow = pl.BlockSpec((8, 3 * span), lambda g, n: (0, g))
    grads, strength_grad, taps_grad, edge, lead = pl.pallas_call(
        backward_kernel,
        grid=(groups, steps),
        in_specs=[
            flat,
            pl.BlockSpec((RIM, 3 * span), lambda g, n: (jnp.maximum(back(n) * ratio - 1, 0), g)),
            pl.BlockSpec((RIM, 3 * span), lambda g, n: (0, g)),
            pl.BlockSpec((3, CONV, span), lambda g, n: (0, 0, g)),
            pl.BlockSpec((1, BLOCK, GROUP), lambda g, n: (g, back(n), 0)),
            pl.BlockSpec((BLOCK, 8), lambda g, n: (back(n), 0)),
            pl.BlockSpec((8, BLOCK), lambda g, n: (0, back(n))),
            deep,
            pl.BlockSpec((1, GROUP, BLOCK, BLOCK), lambda g, n: (back(n), g, 0, 0)),
            wide,
            wide,
            wide,
            wide,
            pl.BlockSpec((1, GROUP, HD, 2 * HD), lambda g, n: (back(n), g, 0, 0)),
            per_group,
            per_group,
        ],
        out_specs=(
            flat,
            pl.BlockSpec((1, BLOCK, GROUP), lambda g, n: (g, back(n), 0)),
            pl.BlockSpec((3, CONV, span), lambda g, n: (0, 0, g)),
            narrow,
            narrow,
        ),
        out_shape=(
            jax.ShapeDtypeStruct((total, 3 * width), LOW),
            jax.ShapeDtypeStruct((groups, total, GROUP), FULL),
            jax.ShapeDtypeStruct((3, CONV, width), FULL),
            jax.ShapeDtypeStruct((8, 3 * width), FULL),
            jax.ShapeDtypeStruct((8, 3 * width), FULL),
        ),
        scratch_shapes=[pltpu.VMEM((GROUP, HD, HD), FULL), pltpu.VMEM((3, 8, span), FULL)],
        compiler_params=pltpu.CompilerParams(vmem_limit_bytes=48 << 20),
        cost_estimate=pl.CostEstimate(flops=4 << 30, bytes_accessed=24 << 20, transcendentals=0),
    )(
        projected, projected, rim, taps, strength_col, meta, meta_row, mixed, solve, weight, update,
        drift, upstream, states, enter, leave,
    )
    return grads, strength_grad.transpose(1, 0, 2).reshape(total, head_count), taps_grad, edge, lead


def fsdp_split(count):
    along = 4 if count % 4 == 0 else 1
    return along, count // along


def gather_kernel(along, across, seq_count, shard_ref, small_ref, full_ref, small_full_ref, local_sem, small_send,
                  small_recv, z_send, z_recv, x_send, x_recv, core_send, core_recv):
    count = along * across
    seq, mine = lax.axis_index("seq"), lax.axis_index("fsdp")
    core, z, x = lax.rem(seq, 2), lax.div(mine, across), lax.rem(mine, across)
    partner = seq + 1 - 2 * core
    rows = shard_ref.shape[0]
    half = rows // 2
    mesh_id = pl.DeviceIdType.MESH

    barrier = pltpu.get_barrier_semaphore()
    for d in range(1, count):
        pl.semaphore_signal(barrier, inc=1, device_id=(seq, lax.rem(mine + d, count)), device_id_type=mesh_id)
    pl.semaphore_signal(barrier, inc=1, device_id=(partner, mine), device_id_type=mesh_id)
    pl.semaphore_wait(barrier, count)

    def place(k, j):
        owner = lax.rem(z - k + along, along) * across + lax.rem(x - j + across, across)
        start = pl.multiple_of(owner * rows + core * half, 16)
        return full_ref.at[pl.ds(start, half), :]

    own_half = shard_ref.at[pl.ds(pl.multiple_of(core * half, 16), half), :]
    keep = pltpu.make_async_copy(
        shard_ref, full_ref.at[pl.ds(pl.multiple_of(mine * rows, 16), rows), :], local_sem.at[0]
    )
    keep.start()
    small_place = small_full_ref.at[:, pl.ds(pl.multiple_of(mine * 128, 128), 128)]
    keep_small = pltpu.make_async_copy(small_ref, small_place, local_sem.at[1])
    keep_small.start()

    def sent(source, target, send, recv, device):
        copy = pltpu.make_async_remote_copy(
            src_ref=source, dst_ref=target, send_sem=send, recv_sem=recv, device_id=device, device_id_type=mesh_id
        )
        copy.start()
        return copy

    def along_z(k):
        source = own_half if k == 1 else place(k - 1, 0)
        device = (seq, lax.rem(z + 1, along) * across + x)
        return sent(source, place(k - 1, 0), z_send.at[k - 1], z_recv.at[k - 1], device)

    def along_x(k, j):
        source = own_half if k == 0 else place(k, 0)
        at = k * (across - 1) + j - 1
        device = (seq, z * across + lax.rem(x + j, across))
        return sent(source, place(k, 0), x_send.at[at], x_recv.at[at], device)

    def to_core(k, j):
        at = k * across + j
        return sent(place(k, j), place(k, j), core_send.at[at], core_recv.at[at], (partner, mine))

    copies = []
    z_copies = {1: along_z(1)} if along > 1 else {}
    x_copies = {}
    for j in range(1, across):
        x_copies[0, j] = along_x(0, j)
    for d in range(1, count):
        copies.append(
            sent(small_ref, small_place, small_send.at[d - 1], small_recv.at[d - 1],
                 (seq, lax.rem(mine + d, count)))
        )
    core_copies = []
    for k in range(1, along):
        z_copies[k].wait_recv()
        if k + 1 < along:
            z_copies[k + 1] = along_z(k + 1)
        for j in range(1, across):
            x_copies[k, j] = along_x(k, j)
        core_copies.append(to_core(k, 0))
        for j in range(1, across):
            x_copies[k - 1, j].wait_recv()
            core_copies.append(to_core(k - 1, j))
    for j in range(1, across):
        x_copies[along - 1, j].wait_recv()
        core_copies.append(to_core(along - 1, j))
    keep.wait()
    keep_small.wait()
    for copy in list(z_copies.values()) + list(x_copies.values()):
        copy.wait_send()
    for copy in copies + core_copies:
        copy.wait()


def gathered_mixer(shard, small, seq_count, fsdp_count):
    along, across = fsdp_split(fsdp_count)
    rows, width = shard.shape
    dma = pltpu.SemaphoreType.DMA
    hold = pl.BlockSpec(memory_space=pl.ANY)
    links = max(along * (across - 1), 1)
    return pl.pallas_call(
        partial(gather_kernel, along, across, seq_count),
        in_specs=[hold, hold],
        out_specs=(hold, hold),
        out_shape=(
            jax.ShapeDtypeStruct((rows * fsdp_count, width), shard.dtype),
            jax.ShapeDtypeStruct((small.shape[0], fsdp_count * 128), small.dtype),
        ),
        scratch_shapes=[
            dma((2,)),
            dma((fsdp_count - 1,)),
            dma((fsdp_count - 1,)),
            dma((along,)),
            dma((along,)),
            dma((links,)),
            dma((links,)),
            dma((along * across,)),
            dma((along * across,)),
        ],
        compiler_params=pltpu.CompilerParams(collective_id=0, has_side_effects=True),
    )(shard, small)


def core_swapped(value):
    count = lax.axis_size("seq")
    return lax.ppermute(value, "seq", [(i, i + 1 - 2 * (i % 2)) for i in range(count)])


def chip_shifted(value, by):
    count = lax.axis_size("seq")
    return lax.ppermute(value, "seq", [(i, (i + 2 * by) % count) for i in range(count)])


def seq_blocks(value):
    chips = lax.axis_size("seq") // 2
    far = [chip_shifted(value, k) for k in range(1, chips)]
    found = []
    for one in [value] + far:
        found += [one, core_swapped(one)]
    return found


def seq_stacked(value):
    count, index = lax.axis_size("seq"), lax.axis_index("seq")
    core = index % 2
    result = jnp.zeros((count,) + value.shape, value.dtype)
    for place, one in enumerate(seq_blocks(value)):
        chip = (index // 2 - place // 2) % (count // 2)
        at = chip * 2 + (core if place % 2 == 0 else 1 - core)
        result = lax.dynamic_update_slice_in_dim(result, one[None], at, 0)
    return result


def low_dot(left, right, dims):
    return lax.dot_general(left, right, (((dims[0],), (dims[1],)), ((), ())), preferred_element_type=FULL)


def exchange_kernel(backward, seq_count, local_ref, transfer_ref, result_ref, other_local, other_transfer, chip_ref, sent_ref,
                    swap_send, swap_recv, chip_send, chip_recv, half_send, half_recv):
    seq, mine = lax.axis_index("seq"), lax.axis_index("fsdp")
    core, chip = lax.rem(seq, 2), lax.div(seq, 2)
    partner = seq + 1 - 2 * core
    chips = seq_count // 2
    heads = local_ref.shape[0]
    mesh_id = pl.DeviceIdType.MESH
    lead = core == (1 if backward else 0)
    dims = (0, 0) if backward else (1, 0)
    step = -1 if backward else 1

    for head in range(heads):
        chip_ref[head] = jnp.zeros((HD, HD), FULL)
    barrier = pltpu.get_barrier_semaphore()
    pl.semaphore_signal(barrier, inc=1, device_id=(partner, mine), device_id_type=mesh_id)
    for k in range(1, chips):
        other = lax.rem(seq + 2 * k, seq_count)
        pl.semaphore_signal(barrier, inc=1, device_id=(other, mine), device_id_type=mesh_id)
    pl.semaphore_wait(barrier, chips)

    swaps = [
        pltpu.make_async_remote_copy(
            src_ref=source, dst_ref=target, send_sem=swap_send.at[i], recv_sem=swap_recv.at[i],
            device_id=(partner, mine), device_id_type=mesh_id,
        )
        for i, (source, target) in enumerate(((local_ref, other_local), (transfer_ref, other_transfer)))
    ]
    for swap in swaps:
        swap.start()
    for swap in swaps:
        swap.wait()
    share = pl.ds(pl.multiple_of(core * (heads // 2), heads // 2), heads // 2)

    def applied(matrix, value):
        return product(halves(matrix), halves(value), dims)

    for i in range(chips - 1):
        source = chips - 1 - i if backward else i

        @pl.when(chip == source)
        def _():
            for head in range(heads):
                lead_local = jnp.where(lead, local_ref[head], other_local[head])
                trail_local = jnp.where(lead, other_local[head], local_ref[head])
                lead_transfer = jnp.where(lead, transfer_ref[head], other_transfer[head])
                trail_transfer = jnp.where(lead, other_transfer[head], transfer_ref[head])
                inner = lead_local if i == 0 else lead_local + applied(lead_transfer, chip_ref[head])
                sent_ref[head] = trail_local + applied(trail_transfer, inner)

        onward = pltpu.make_async_remote_copy(
            src_ref=sent_ref.at[share], dst_ref=chip_ref.at[share], send_sem=chip_send.at[i], recv_sem=chip_recv.at[i],
            device_id=(lax.rem(seq + 2 * step + seq_count, seq_count), mine), device_id_type=mesh_id,
        )
        half = pltpu.make_async_remote_copy(
            src_ref=chip_ref.at[share], dst_ref=chip_ref.at[share], send_sem=half_send.at[i], recv_sem=half_recv.at[i],
            device_id=(partner, mine), device_id_type=mesh_id,
        )

        @pl.when(chip == source)
        def _():
            onward.start()
            onward.wait_send()

        @pl.when(chip == source + step)
        def _():
            onward.wait_recv()
            half.start()
            half.wait()

    for head in range(heads):
        lead_local = jnp.where(lead, local_ref[head], other_local[head])
        lead_transfer = jnp.where(lead, transfer_ref[head], other_transfer[head])
        state = chip_ref[head]
        result_ref[head] = jnp.where(lead, state, lead_local + applied(lead_transfer, state))


def exchanged(local, transfer, backward, call_id):
    seq_count = lax.axis_size("seq")
    dma = pltpu.SemaphoreType.DMA
    vmem = pl.BlockSpec(memory_space=pltpu.VMEM)
    hops = max(seq_count // 2 - 1, 1)
    return pl.pallas_call(
        partial(exchange_kernel, backward, seq_count),
        in_specs=[vmem, vmem],
        out_specs=vmem,
        out_shape=jax.ShapeDtypeStruct(local.shape, FULL),
        scratch_shapes=[pltpu.VMEM(local.shape, FULL)] * 4 + [dma((2,))] * 2 + [dma((hops,))] * 4,
        compiler_params=pltpu.CompilerParams(collective_id=call_id, has_side_effects=True, vmem_limit_bytes=24 << 20),
    )(local, transfer)


def norm_back(unit, scale, gain, grad):
    gained = jnp.sum(grad * unit, axis=0)
    grad = grad * gain
    return scale * (grad - unit * jnp.mean(grad * unit, axis=-1, keepdims=True)), gained


def matrix_owners(fsdp_count):
    along, across = fsdp_split(fsdp_count)
    if along == 4 and across > 1:
        first, second = across, 2 * across + 1
        return [(0, first), (0, second), (1, first), (1, second), (1, first + 1), (0, first + 1), (1, second - 1)]
    return [(m % 2, m * fsdp_count // 7) for m in range(7)]


def remote(source, target, send, recv, device):
    return pltpu.make_async_remote_copy(
        src_ref=source, dst_ref=target, send_sem=send, recv_sem=recv, device_id=device,
        device_id_type=pl.DeviceIdType.MESH,
    )


class Place:
    def __init__(self, seq_count, count):
        self.seq_count, self.count, self.chips = seq_count, count, seq_count // 2
        self.seq, self.mine = lax.axis_index("seq"), lax.axis_index("fsdp")
        self.core, self.chip = lax.rem(self.seq, 2), lax.div(self.seq, 2)
        self.partner = (self.seq + 1 - 2 * self.core, self.mine)

    def fsdp(self, d):
        return lax.rem(self.mine + d, self.count)

    def next_seq(self, k):
        return (lax.rem(self.seq + k, self.seq_count), self.mine)

    def next_chip(self, k):
        return (lax.rem(self.seq + 2 * k, self.seq_count), self.mine)

    def greet(self, chips_too):
        barrier = pltpu.get_barrier_semaphore()
        others = [(self.seq, self.fsdp(d)) for d in range(1, self.count)]
        others += [self.next_seq(k) for k in range(1, self.seq_count)] if chips_too else [self.partner]
        for other in others:
            pl.semaphore_signal(barrier, inc=1, device_id=other, device_id_type=pl.DeviceIdType.MESH)
        pl.semaphore_wait(barrier, len(others))


def collect(here, owners, pieces, whole, send, recv, local_sem, core_send, core_recv):
    def piece(n, target, source):
        return remote(pieces.at[n], whole.at[source, here.core], send.at[n], recv.at[source], (here.seq, target))

    for n, (row, owner) in enumerate(owners):
        @pl.when((here.chip == row) & (here.mine != owner))
        def _():
            piece(n, owner, here.mine).start()

    def finish():
        for n, (row, owner) in enumerate(owners):
            @pl.when((here.chip == row) & (here.mine == owner))
            def _():
                keep = pltpu.make_async_copy(pieces.at[n], whole.at[here.mine, here.core], local_sem)
                keep.start()
                for d in range(1, here.count):
                    piece(n, here.fsdp(d), here.fsdp(d)).wait_recv()
                keep.wait()
                half = whole.at[:, here.core]
                swap = remote(half, half, core_send, core_recv, here.partner)
                swap.start()
                swap.wait()

        for n, (row, owner) in enumerate(owners):
            @pl.when((here.chip == row) & (here.mine != owner))
            def _():
                piece(n, owner, here.mine).wait_send()

    return finish


def hand_back(here, owners, rows, parts, local_sem, send, recv, chip_send, chip_recv, core_send, core_recv):
    def part(m):
        return parts.at[m, here.core]

    def piece(m, d):
        return remote(rows.at[here.fsdp(d)], part(m), send.at[d], recv.at[m], (here.seq, here.fsdp(d)))

    def onward(m, k):
        return remote(part(m), part(m), chip_send.at[m, k - 1], chip_recv.at[m], here.next_chip(k))

    def swap(m):
        return remote(part(m), part(m), core_send.at[m], core_recv.at[m], here.partner)

    for m, (row, owner) in enumerate(owners):
        @pl.when((here.chip == row) & (here.mine == owner))
        def _():
            for d in range(1, here.count):
                piece(m, d).start()
            keep = pltpu.make_async_copy(rows.at[here.mine], part(m), local_sem)
            keep.start()
            keep.wait()

    def finish():
        for m, (row, owner) in enumerate(owners):
            @pl.when((here.chip == row) & (here.mine != owner))
            def _():
                piece(m, 0).wait_recv()

            @pl.when(here.chip == row)
            def _():
                for k in range(1, here.chips):
                    onward(m, k).start()
                swap(m).start()

        for m, (row, owner) in enumerate(owners):
            @pl.when(here.chip != row)
            def _():
                onward(m, 1).wait_recv()
                swap(m).start()

        for m, (row, owner) in enumerate(owners):
            swap(m).wait()

            @pl.when(here.chip == row)
            def _():
                for k in range(1, here.chips):
                    onward(m, k).wait_send()

            @pl.when((here.chip == row) & (here.mine == owner))
            def _():
                for d in range(1, here.count):
                    piece(m, d).wait_send()

    return finish


def collect_sems(kinds, count):
    dma = pltpu.SemaphoreType.DMA
    return [dma((kinds,)), dma((count,)), dma, dma, dma]


def hand_back_sems(kinds, count, chips):
    dma = pltpu.SemaphoreType.DMA
    return [dma, dma((count,)), dma((kinds,)), dma((kinds, chips)), dma((kinds,)), dma((kinds,)), dma((kinds,))]


def middle_kernel(owners, seq_count, count, part_ref, prior_ref, small_ref, wide_ref, sum_ref, small_out, square_whole,
                  wide_whole, chip_ref, total_ref, piece_ref, place_ref, seq_ref, chip_send, chip_recv, half_sem,
                  place_send, place_recv, seq_send, seq_recv, *sems):
    here = Place(seq_count, count)
    width = piece_ref.shape[2]
    chip_ref[here.chip] = part_ref[...]
    place_ref[here.mine] = small_ref[here.mine]
    here.greet(True)
    small_copies = []
    for d in range(1, count):
        copy = remote(
            small_ref.at[here.fsdp(d)], place_ref.at[here.mine], place_send.at[d - 1], place_recv.at[here.mine],
            (here.seq, here.fsdp(d)),
        )
        copy.start()
        small_copies.append(copy)
    own = chip_ref.at[here.chip]
    onward = [
        remote(own, own, chip_send.at[k - 1], chip_recv.at[here.chip], here.next_chip(k)) for k in range(1, here.chips)
    ]
    for copy in onward:
        copy.start()
    finish_wide = collect(here, owners[:3], wide_ref, wide_whole, *sems[:5])
    for k in range(1, here.chips):
        source = lax.rem(here.chip + k, here.chips)
        other = chip_ref.at[source]
        remote(other, other, chip_send.at[k - 1], chip_recv.at[source], here.next_chip(k)).wait_recv()
    total = chip_ref[0].astype(FULL)
    for i in range(1, here.chips):
        total = total + chip_ref[i].astype(FULL)
    total_ref[...] = total
    fresh = (momentum_decay * prior_ref[...] + total).astype(LOW)
    span = GROUP * HD
    for g in range(width // span):
        for j in range(3):
            at = (3 * g + j) * span
            piece_ref[j, :, g * span : (g + 1) * span] = fresh[:, at : at + span]
    piece_ref[3] = fresh[:, 3 * width :]
    finish_square = collect(here, owners[3:], piece_ref, square_whole, *sems[5:])
    half_copy = remote(total_ref, sum_ref.at[here.core], half_sem.at[0], half_sem.at[1], here.partner)
    half_copy.start()
    keep = pltpu.make_async_copy(total_ref, sum_ref.at[here.core], half_sem.at[2])
    keep.start()
    for d in range(1, count):
        source = here.fsdp(d)
        other = place_ref.at[source]
        remote(other, other, place_send.at[d - 1], place_recv.at[source], (here.seq, source)).wait_recv()
    small = place_ref[0]
    for i in range(1, count):
        small = small + place_ref[i]
    seq_ref[here.seq] = small
    own = seq_ref.at[here.seq]
    for k in range(1, seq_count):
        copy = remote(own, own, seq_send.at[k - 1], seq_recv.at[here.seq], here.next_seq(k))
        copy.start()
        small_copies.append(copy)
    for k in range(1, seq_count):
        source = lax.rem(here.seq + k, seq_count)
        other = seq_ref.at[source]
        remote(other, other, seq_send.at[k - 1], seq_recv.at[source], here.next_seq(k)).wait_recv()
    small = seq_ref[0]
    for i in range(1, seq_count):
        small = small + seq_ref[i]
    small_out[...] = small
    finish_square()
    finish_wide()
    keep.wait()
    half_copy.wait()
    for copy in onward + small_copies:
        copy.wait_send()


def middle(part, prior, small, wide, owners, call_id, seq_count, count):
    half, columns = part.shape
    width = columns // 4
    chips = seq_count // 2
    dma = pltpu.SemaphoreType.DMA
    hold, vmem = pl.BlockSpec(memory_space=pl.ANY), pl.BlockSpec(memory_space=pltpu.VMEM)
    return pl.pallas_call(
        partial(middle_kernel, owners, seq_count, count),
        in_specs=[vmem, vmem, vmem, hold],
        out_specs=(hold, vmem, hold, hold),
        out_shape=(
            jax.ShapeDtypeStruct((2, half, columns), FULL),
            jax.ShapeDtypeStruct(small.shape[1:], FULL),
            jax.ShapeDtypeStruct((count, 2, half, width), LOW),
            jax.ShapeDtypeStruct((count, 2) + wide.shape[1:], LOW),
        ),
        scratch_shapes=[
            pltpu.VMEM((chips, half, columns), LOW),
            pltpu.VMEM((half, columns), FULL),
            pltpu.VMEM((4, half, width), LOW),
            pltpu.VMEM(small.shape, FULL),
            pltpu.VMEM((seq_count,) + small.shape[1:], FULL),
            dma((max(chips - 1, 1),)),
            dma((chips,)),
            dma((3,)),
            dma((count,)),
            dma((count,)),
            dma((seq_count,)),
            dma((seq_count,)),
        ]
        + collect_sems(3, count)
        + collect_sems(4, count),
        compiler_params=pltpu.CompilerParams(collective_id=call_id, has_side_effects=True, vmem_limit_bytes=24 << 20),
    )(part, prior, small, wide)


def hand_back_kernel(owners, seq_count, count, wide_ref, square_ref, wide_parts, square_parts, *sems):
    here = Place(seq_count, count)
    here.greet(True)
    finish_square = hand_back(here, owners[3:], square_ref, square_parts, *sems[7:])
    finish_wide = hand_back(here, owners[:3], wide_ref, wide_parts, *sems[:7])
    finish_square()
    finish_wide()


def handed_back(wide_rows, square_rows, owners, call_id, seq_count, count):
    hold = pl.BlockSpec(memory_space=pl.ANY)
    chips = seq_count // 2
    return pl.pallas_call(
        partial(hand_back_kernel, owners, seq_count, count),
        in_specs=[hold, hold],
        out_specs=(hold, hold),
        out_shape=(
            jax.ShapeDtypeStruct((3, 2) + wide_rows.shape[1:], LOW),
            jax.ShapeDtypeStruct((4, 2) + square_rows.shape[1:], LOW),
        ),
        scratch_shapes=hand_back_sems(3, count, chips) + hand_back_sems(4, count, chips),
        compiler_params=pltpu.CompilerParams(collective_id=call_id, has_side_effects=True),
    )(wide_rows, square_rows)


def tile_count(width, seq_count):
    return -(-(width // HD) // seq_count)


def prepare_kernel(seq_count, mixer_ref, output_ref, gate_up_ref, down_ref, strength_ref, filter_ref, gain_ref, head_ref,
                   square_ref, ff_ref, small_ref):
    shard, width = output_ref.shape
    span = GROUP * HD
    tiles = gate_up_ref.shape[2] // HD
    per = tile_count(gate_up_ref.shape[2], seq_count)
    seq = lax.axis_index("seq")
    for g in range(width // span):
        for j in range(3):
            at = (3 * g + j) * span
            square_ref[:, at : at + span] = mixer_ref[j, :, g * span : (g + 1) * span].astype(LOW)
    square_ref[:, 3 * width :] = output_ref[...].astype(LOW)
    for i in range(per):
        tile = i * seq_count + seq
        at = pl.ds(pl.multiple_of(jnp.minimum(tile, tiles - 1) * HD, HD), HD)
        kept = jnp.where(tile < tiles, 1.0, 0.0).astype(FULL)
        for j in range(2):
            to = (j * per + i) * HD
            ff_ref[:, to : to + HD] = (gate_up_ref[j, :, at] * kept).astype(LOW)
        to = (2 * per + i) * HD
        ff_ref[:, to : to + HD] = (down_ref[at, :] * kept).T.astype(LOW)
    small_ref[...] = jnp.zeros_like(small_ref)
    heads = strength_ref.shape[1]
    rows = [strength_ref[...].T] + [filter_ref[j] for j in range(3)] + [gain_ref[...]]
    at = 0
    for one in rows:
        small_ref[at : at + one.shape[0], :shard] = one.astype(LOW)
        at += one.shape[0]
    small_ref[at : at + 1, : head_ref.shape[1]] = head_ref[...].astype(LOW)


def prepared(mixer, output, gate_up, down, strength, filters, gain, head, seq_count):
    shard, width = output.shape
    columns = 3 * tile_count(gate_up.shape[2], seq_count) * HD
    vmem = pl.BlockSpec(memory_space=pltpu.VMEM)
    return pl.pallas_call(
        partial(prepare_kernel, seq_count),
        in_specs=[vmem] * 8,
        out_specs=(vmem,) * 3,
        out_shape=(
            jax.ShapeDtypeStruct((shard, 4 * width), LOW),
            jax.ShapeDtypeStruct((shard, columns), LOW),
            jax.ShapeDtypeStruct((32, 128), LOW),
        ),
        compiler_params=pltpu.CompilerParams(vmem_limit_bytes=40 << 20),
    )(mixer, output, gate_up, down, strength, filters, gain, head[None])


def wide_moment_kernel(seq_count, gate_up_ref, down_ref, stack_ref, gate_up_out, down_out, sent_ref, hold_ref):
    half = sent_ref.shape[1]
    tiles = gate_up_ref.shape[2] // HD
    per = stack_ref.shape[2] // (3 * HD)
    core = lax.rem(lax.axis_index("seq"), 2)
    mine = pl.ds(pl.multiple_of(core * half, half), half)
    for t in range(tiles):
        source, i = t % seq_count, t // seq_count
        at = slice(t * HD, (t + 1) * HD)
        for j in range(2):
            grad = stack_ref[source, :, (j * per + i) * HD : (j * per + i + 1) * HD].astype(FULL)
            gate_up_out[j, :, at] = momentum_decay * gate_up_ref[j, :, at] + grad
            sent_ref[j, :, at] = gate_up_out[j, mine, at].astype(LOW)
        grad = stack_ref[source, :, (2 * per + i) * HD : (2 * per + i + 1) * HD].astype(FULL)
        fresh = momentum_decay * down_ref[at, :] + grad.T
        down_out[at, :] = fresh
        hold_ref[...] = fresh.T
        sent_ref[2, :, at] = hold_ref[mine, :].astype(LOW)


def wide_moments(gate_up, down, stack, seq_count):
    shard, width = gate_up.shape[1:]
    vmem = pl.BlockSpec(memory_space=pltpu.VMEM)
    return pl.pallas_call(
        partial(wide_moment_kernel, seq_count),
        in_specs=[vmem] * 3,
        out_specs=(vmem,) * 3,
        out_shape=(
            jax.ShapeDtypeStruct(gate_up.shape, FULL),
            jax.ShapeDtypeStruct(down.shape, FULL),
            jax.ShapeDtypeStruct((3, shard // 2, width), LOW),
        ),
        scratch_shapes=[pltpu.VMEM((shard, HD), FULL)],
        compiler_params=pltpu.CompilerParams(vmem_limit_bytes=40 << 20),
    )(gate_up, down, stack)


def finish_kernel(
    wide_ref, square_ref, sum_ref, small_ref, mixer_w, output_w, gate_up_w, down_w, strength_w, filter_w, gain_w, head_w,
    mixer_m, output_m, strength_m, filter_m, gain_m, head_m,
    new_mixer_m, new_mixer_w, new_strength_m, new_strength_w, new_filter_m, new_filter_w, new_gain_m, new_gain_w,
    new_head_m, new_head_w, new_output_m, new_output_w, new_gate_up_w, new_down_w,
):
    shard, width = output_w.shape
    span = GROUP * HD
    for g in range(width // span):
        for j in range(3):
            at, to = (3 * g + j) * span, slice(g * span, (g + 1) * span)
            new_mixer_m[j, :, to] = momentum_decay * mixer_m[j, :, to] + sum_ref[:, at : at + span]
    for j in range(3):
        new_mixer_w[j] = mixer_w[j] - matrix_rate * square_ref[j].astype(FULL)
    new_output_m[...] = momentum_decay * output_m[...] + sum_ref[:, 3 * width :]
    new_output_w[...] = output_w[...] - matrix_rate * square_ref[3].astype(FULL)
    for j in range(2):
        new_gate_up_w[j] = gate_up_w[j] - matrix_rate * wide_ref[j].astype(FULL)
    for t in range(down_w.shape[0] // HD):
        at = slice(t * HD, (t + 1) * HD)
        new_down_w[at, :] = down_w[at, :] - matrix_rate * wide_ref[2, :, at].astype(FULL).T
    heads = strength_w.shape[1]
    fresh = momentum_decay * strength_m[...] + small_ref[:heads, :].T
    new_strength_m[...] = fresh
    new_strength_w[...] = strength_w[...] - strength_rate * fresh
    for j in range(3):
        fresh = momentum_decay * filter_m[j] + small_ref[heads + CONV * j : heads + CONV * (j + 1), :]
        new_filter_m[j] = fresh
        new_filter_w[j] = filter_w[j] - filter_rate * fresh
    at = heads + 3 * CONV
    fresh = momentum_decay * gain_m[...] + small_ref[at : at + 2, :]
    new_gain_m[...] = fresh
    new_gain_w[...] = gain_w[...] - gain_rate * fresh
    fresh = momentum_decay * head_m[...] + small_ref[at + 2 : at + 3, : head_m.shape[1]]
    new_head_m[...] = fresh
    new_head_w[...] = head_w[...] - gain_rate * fresh


def finished(wide, square, total, small, weights, moments):
    mixer_w, output_w, gate_up_w, down_w, strength_w, filter_w, gain_w, head_w = weights
    mixer_m, output_m, strength_m, filter_m, gain_m, head_m = moments
    pairs = [mixer_w, strength_w, filter_w, gain_w, head_w[None], output_w]
    shapes = [jax.ShapeDtypeStruct(one.shape, FULL) for pair in zip(pairs, pairs) for one in pair]
    shapes += [jax.ShapeDtypeStruct(one.shape, FULL) for one in (gate_up_w, down_w)]
    vmem = pl.BlockSpec(memory_space=pltpu.VMEM)
    return pl.pallas_call(
        finish_kernel,
        in_specs=[vmem] * 18,
        out_specs=(vmem,) * len(shapes),
        out_shape=tuple(shapes),
        compiler_params=pltpu.CompilerParams(vmem_limit_bytes=56 << 20),
    )(
        wide, square, total, small, mixer_w, output_w, gate_up_w, down_w, strength_w, filter_w, gain_w, head_w[None],
        mixer_m, output_m, strength_m, filter_m, gain_m, head_m[None],
    )


TILE = 256


def row_loop(rows, body):
    @pl.loop(0, rows // TILE)
    def _(i):
        body(pl.ds(pl.multiple_of(i * TILE, TILE), TILE))


def trace_of(square_ref):
    total = jnp.zeros((1, 1), FULL)
    for i in range(square_ref.shape[0] // TILE):
        tile = square_ref[i * TILE : (i + 1) * TILE, i * TILE : (i + 1) * TILE]
        rows = lax.broadcasted_iota(jnp.int32, (TILE, TILE), 0)
        cols = lax.broadcasted_iota(jnp.int32, (TILE, TILE), 1)
        total = total + jnp.sum(jnp.where(rows == cols, tile, 0.0), keepdims=True)
    return total


def pick_rows(count, half, source_ref, target_ref):
    core = lax.rem(lax.axis_index("seq"), 2)
    for f in range(count):
        at = pl.multiple_of(f * 2 * half + core * half, 16)
        target_ref[f * half : (f + 1) * half, :] = source_ref[pl.ds(at, half), :]


def orth_wide_kernel(
    count, half, whole_ref, out_ref, square_ref, middle_ref, mapped_ref, gathered_ref,
    square_low, mapped_low, first_low, second_low, rows_low, rows_own,
):
    size = whole_ref.shape[0]

    def start(at):
        square_ref[at, :] = product(whole_ref[at, :], whole_ref[...], (1, 1))

    row_loop(size, start)
    scale = 1.0 / (jnp.sqrt(trace_of(square_ref)) + 1e-07)

    def scaled(at):
        value = square_ref[at, :] * (scale * scale)
        square_ref[at, :] = value
        square_low[at, :] = value.astype(LOW)

    row_loop(size, scaled)
    level = 1.0
    gathered_low, spare_low = first_low, second_low
    for sweep in range(NS_STEPS):
        keep_ref = gathered_ref if sweep == 0 else mapped_ref

        def mapping(at):
            value = coef_cubic * square_ref[at, :] + coef_quintic * product(square_low[at, :], square_low[...])
            keep_ref[at, :] = value
            mapped_low[at, :] = value.astype(LOW)

        row_loop(size, mapping)
        if sweep == 0:
            def copy_low(at):
                gathered_low[at, :] = mapped_low[at, :]

            row_loop(size, copy_low)
        else:
            def gather(at):
                value = (
                    coef_linear * gathered_ref[at, :]
                    + level * mapped_ref[at, :]
                    + product(mapped_low[at, :], gathered_low[...])
                )
                gathered_ref[at, :] = value
                spare_low[at, :] = value.astype(LOW)

            row_loop(size, gather)
            gathered_low, spare_low = spare_low, gathered_low
        level = level * coef_linear
        if sweep < NS_STEPS - 1:
            def middle(at):
                value = coef_linear * square_ref[at, :] + product(mapped_low[at, :], square_low[...])
                middle_ref[at, :] = value
                spare_low[at, :] = value.astype(LOW)

            row_loop(size, middle)

            def squared(at):
                value = coef_linear * middle_ref[at, :] + product(spare_low[at, :], mapped_low[...])
                square_ref[at, :] = value
                square_low[at, :] = value.astype(LOW)

            row_loop(size, squared)
    pick_rows(count, half, gathered_low, rows_low)
    pick_rows(count, half, whole_ref, rows_own)

    @pl.loop(0, whole_ref.shape[1] // TILE)
    def _(i):
        at = pl.ds(pl.multiple_of(i * TILE, TILE), TILE)
        value = level * rows_own[:, at].astype(FULL) + product(rows_low[...], whole_ref[:, at])
        out_ref[:, at] = (value * scale).astype(LOW)


def orth_square_kernel(
    count, half, whole_ref, out_ref, square_ref, current_ref, square_low, mapped_low, first_low, second_low,
    rows_low, rows_own,
):
    size = whole_ref.shape[0]

    def start(at):
        square_ref[at, :] = product(whole_ref[at, :], whole_ref[...], (1, 1))

    row_loop(size, start)
    scale = 1.0 / (jnp.sqrt(trace_of(square_ref)) + 1e-07)

    def scaled(at):
        value = whole_ref[at, :].astype(FULL) * scale
        current_ref[at, :] = value
        first_low[at, :] = value.astype(LOW)
        value = square_ref[at, :] * (scale * scale)
        square_ref[at, :] = value
        square_low[at, :] = value.astype(LOW)

    row_loop(size, scaled)
    now, later = first_low, second_low
    for sweep in range(NS_STEPS):
        if sweep:
            def squared(at):
                value = product(now[at, :], now[...], (1, 1))
                square_ref[at, :] = value
                square_low[at, :] = value.astype(LOW)

            row_loop(size, squared)

        def mapping(at):
            value = coef_cubic * square_ref[at, :] + coef_quintic * product(square_low[at, :], square_low[...])
            mapped_low[at, :] = value.astype(LOW)

        row_loop(size, mapping)
        if sweep < NS_STEPS - 1:
            def step(at):
                value = coef_linear * current_ref[at, :] + product(mapped_low[at, :], now[...])
                current_ref[at, :] = value
                later[at, :] = value.astype(LOW)

            row_loop(size, step)
            now, later = later, now
    pick_rows(count, half, mapped_low, rows_low)
    pick_rows(count, half, current_ref, rows_own)

    @pl.loop(0, size // TILE)
    def _(i):
        at = pl.ds(pl.multiple_of(i * TILE, TILE), TILE)
        value = coef_linear * rows_own[:, at] + product(rows_low[...], now[:, at])
        out_ref[:, at] = value.astype(LOW)


def orth_call(kernel, scratch, count, whole):
    half, width = whole.shape[2:]
    size = count * 2 * half
    flat = whole.reshape(size, width)
    vmem = pl.BlockSpec(memory_space=pltpu.VMEM)
    result = pl.pallas_call(
        partial(kernel, count, half),
        in_specs=[vmem],
        out_specs=vmem,
        out_shape=jax.ShapeDtypeStruct((size // 2, width), LOW),
        scratch_shapes=scratch(size, width),
        compiler_params=pltpu.CompilerParams(vmem_limit_bytes=56 << 20),
    )(flat)
    return result.reshape(count, half, width)


def orth_wide(count, whole):
    def scratch(size, width):
        return (
            [pltpu.VMEM((size, size), FULL)] * 4
            + [pltpu.VMEM((size, size), LOW)] * 4
            + [pltpu.VMEM((size // 2, size), LOW), pltpu.VMEM((size // 2, width), LOW)]
        )

    return orth_call(orth_wide_kernel, scratch, count, whole)


def orth_square(count, whole):
    def scratch(size, width):
        return (
            [pltpu.VMEM((size, size), FULL)] * 2
            + [pltpu.VMEM((size, size), LOW)] * 4
            + [pltpu.VMEM((size // 2, size), LOW), pltpu.VMEM((size // 2, width), FULL)]
        )

    return orth_call(orth_square_kernel, scratch, count, whole)


def chosen_place(owners, mine, chip):
    chosen = (mine == owners[0][1]) & (chip == owners[0][0])
    for row, place in owners[1:]:
        chosen = chosen | ((mine == place) & (chip == row))
    return chosen


def orthogonal(whole, owners, method, mine, chip, count):
    half, width = whole.shape[2:]
    return lax.cond(
        chosen_place(owners, mine, chip),
        partial(method, count),
        lambda one: jnp.zeros((count, half, width), LOW),
        whole,
    )


def on_device(
    inputs,
    cotangent,
    lengths,
    mixer_weight,
    strength_weight,
    filter_weight,
    norm_gain,
    head_gain,
    output_weight,
    gate_up_weight,
    down_weight,
    mixer_moment,
    strength_moment,
    filter_moment,
    gain_moment,
    head_gain_moment,
    output_moment,
    gate_up_moment,
    down_moment,
):
    seq_count = lax.axis_size("seq")
    seq_index = lax.axis_index("seq")
    fsdp_count = lax.axis_size("fsdp")
    fsdp_index = lax.axis_index("fsdp")
    row_count, width = inputs.shape
    shard = width // fsdp_count
    heads_all = strength_weight.shape[1]

    wide_ff = tile_count(gate_up_weight.shape[2], seq_count) * HD
    core = seq_index % 2
    half = shard // 2
    groups = heads_all // GROUP
    span = GROUP * HD
    small_count = heads_all + 3 * CONV + 3
    top_near = core_swapped(cotangent)
    top_far = [chip_shifted(cotangent, k) for k in range(1, seq_count // 2)]
    square_own, ff_own, small_own = prepared(
        mixer_weight, output_weight, gate_up_weight, down_weight, strength_weight, filter_weight, norm_gain, head_gain,
        seq_count,
    )
    square_full, small_full = gathered_mixer(square_own, small_own, seq_count, fsdp_count)
    by_place = small_full.reshape(-1, fsdp_count, 128)
    small_wide = small_full if shard == 128 else by_place[:, :, :shard].reshape(-1, width)
    strength_full = small_wide[:heads_all]
    filters_wide = small_wide[heads_all : heads_all + 3 * CONV].reshape(3, CONV, width).astype(FULL)
    gains_wide = small_wide[heads_all + 3 * CONV : heads_all + 3 * CONV + 2].astype(FULL)
    head_part = head_gain.shape[0]
    head_gain_full = by_place[small_count - 1, :, :head_part].reshape(1, HD).astype(FULL)

    square_full, ff_own, top_near, top_far = lax.optimization_barrier((square_full, ff_own, top_near, top_far))
    top_parts = [cotangent, top_near] + [part for one in top_far for part in (one, core_swapped(one))]
    ff_full = lax.all_gather(ff_own, "fsdp", axis=0, tiled=True)
    mixer_full, output_full = square_full[:, : 3 * width], square_full[:, 3 * width :]
    ff_parts = [ff_full[:, j * wide_ff : (j + 1) * wide_ff] for j in range(3)]

    my_lengths = lax.dynamic_slice_in_dim(lengths, fsdp_index, 1, 0)[0]
    doc_ends = jnp.cumsum(my_lengths)

    def passed_docs(at):
        return (at[:, None] >= doc_ends[None, :]).astype(jnp.int32)

    own = seq_index * row_count + jnp.arange(row_count, dtype=jnp.int32)
    passed = passed_docs(own)
    segment = jnp.sum(passed, axis=1)
    doc_first = jnp.sum(passed * my_lengths[None, :], axis=1)
    block_start = own.reshape(-1, BLOCK)[:, 0]
    before = jnp.where(block_start == 0, -1, jnp.sum(passed_docs(block_start - 1), axis=1))
    blocked = segment.reshape(-1, BLOCK)
    carried = (blocked == before[:, None]).reshape(-1)
    trailing = (blocked == blocked[:, -1:]).reshape(-1)
    columns = [own - lag >= doc_first for lag in range(CONV)] + [carried, trailing, segment]
    meta = jnp.stack([one.astype(FULL) for one in columns] + [jnp.zeros((row_count,), FULL)], axis=1)
    meta_row = jnp.broadcast_to(segment.astype(FULL)[None, :], (8, row_count))

    residual_in = inputs.astype(FULL)
    scale_one = lax.rsqrt(jnp.mean(residual_in * residual_in, axis=-1, keepdims=True) + norm_eps)
    unit_one = residual_in * scale_one
    normed_low = (unit_one * gains_wide[0]).astype(LOW)
    projected = low_dot(normed_low, mixer_full, (1, 0)).astype(LOW)
    logits = low_dot(normed_low, strength_full, (1, 1))
    strength = jax.nn.sigmoid(logits).astype(LOW).astype(FULL)
    forth = [(i, i + 1) for i in range(seq_count - 1)]
    rim = lax.ppermute(projected[row_count - RIM :], "seq", forth)
    mixed, solve, weight, update, drift, local_out, effective, states, end, transfer = forward_blocks(
        projected, rim, filters_wide, strength, meta, meta_row
    )
    enter = exchanged(end, transfer, False, 4)
    delta_out, head_normed = head_outputs(local_out, effective, enter, head_gain_full)
    residual = residual_in + low_dot(head_normed, output_full, (1, 0))
    scale_two = lax.rsqrt(jnp.mean(residual * residual, axis=-1, keepdims=True) + norm_eps)
    unit_two = residual * scale_two
    normed_two = (unit_two * gains_wide[1]).astype(LOW)
    gate_full, up_full, down_full = ff_parts
    chips = seq_count // 2
    near_norm = jnp.concatenate([normed_two, core_swapped(normed_two)])
    far_straight = [chip_shifted(normed_two, k) for k in range(1, chips)]

    def spread_out(normed_part, top_part):
        gate = low_dot(normed_part, gate_full, (1, 0))
        up = low_dot(normed_part, up_full, (1, 0))
        gate_sigmoid = jax.nn.sigmoid(gate)
        gate_silu = gate * gate_sigmoid
        hidden = (gate_silu * up).astype(LOW)
        grad_hidden = low_dot(top_part, down_full, (1, 0))
        grad_gate = (grad_hidden * up * (gate_sigmoid * (1.0 + gate * (1.0 - gate_sigmoid)))).astype(LOW)
        grad_up = (grad_hidden * gate_silu).astype(LOW)
        return hidden, grad_gate, grad_up

    def grad_in(values):
        return low_dot(values[1], gate_full, (1, 1)) + low_dot(values[2], up_full, (1, 1))

    def weight_grad(values, normed_part, top_part, which):
        left, right = ((normed_part, values[1]), (normed_part, values[2]), (top_part, values[0]))[which]
        return low_dot(left, right, (0, 0))

    near_top, far_top = jnp.concatenate(top_parts[:2]), jnp.concatenate(top_parts[2:])
    near = spread_out(near_norm, near_top)
    near_grad = grad_in(near)
    far_straight, near, near_grad = lax.optimization_barrier((far_straight, near, near_grad))
    far_parts = [part for one in far_straight for part in (one, core_swapped(one))]
    near_back = core_swapped(near_grad[row_count:].astype(LOW))
    near_out = low_dot(near[0], down_full, (1, 1))
    near_weights = [weight_grad(near, near_norm, near_top, 0)]
    near_weights, near_out, far_parts = lax.optimization_barrier((near_weights, near_out, far_parts))
    far_norm = jnp.concatenate(far_parts)
    far = spread_out(far_norm, far_top)

    def picked(values, side):
        size = 2 * row_count
        return [
            tuple(one[i * size + side * row_count : i * size + (side + 1) * row_count] for one in values)
            for i in range(chips - 1)
        ]

    crossed = [core_swapped(grad_in(one).astype(LOW)) for one in picked(far, 1)]
    joint = [(grad_in(one) + other.astype(FULL)).astype(LOW) for one, other in zip(picked(far, 0), crossed)]
    far, near, joint = lax.optimization_barrier((far, near, joint))
    grad_parts = [chip_shifted(one, -(k + 1)) for k, one in enumerate(joint)]
    near_weights = list(near_weights) + [weight_grad(near, near_norm, near_top, j) for j in (1, 2)]
    far_weights = [weight_grad(far, far_norm, far_top, j) for j in range(3)]
    ff_grads = jnp.concatenate([(a + b).astype(LOW) for a, b in zip(near_weights, far_weights)], axis=1)
    ff_part = lax.psum_scatter(ff_grads, "fsdp", scatter_dimension=0, tiled=True)
    far_out = low_dot(far[0], down_full, (1, 1))
    out_crossed = [core_swapped(one[0].astype(LOW)) for one in picked((far_out,), 1)]
    out_joint = [(one[0] + other.astype(FULL)).astype(LOW) for one, other in zip(picked((far_out,), 0), out_crossed)]
    out_near = near_out[:row_count] + core_swapped(near_out[row_count:].astype(LOW)).astype(FULL)
    done_grads, out_joint, out_near, grad_parts = lax.optimization_barrier((ff_grads, out_joint, out_near, grad_parts))
    grad_normed_two = near_grad[:row_count] + sum(one.astype(FULL) for one in [near_back] + list(grad_parts))
    back_two, grad_gain_two = norm_back(unit_two, scale_two, gains_wide[1], grad_normed_two)
    grad_residual = back_two + cotangent.astype(FULL)
    grad_attention = grad_residual.astype(LOW)
    grad_head_normed = low_dot(grad_attention, output_full, (1, 1)).astype(LOW)

    upstream, adjoint_local, grad_head_gain = head_back(
        grad_head_normed, delta_out, effective, head_gain_full
    )
    leave = exchanged(adjoint_local, transfer, True, 5)
    leave, out_joint = lax.optimization_barrier((leave, out_joint))
    out_parts = [chip_shifted(one, -(k + 1)) for k, one in enumerate(out_joint)]
    grad_projected, grad_strength, grad_filter, edge, lead = backward_blocks(
        projected, rim, filters_wide, strength, meta, meta_row, mixed, solve, weight, update, drift,
        upstream, states, enter, leave,
    )
    lead, out_parts = lax.optimization_barrier((lead, out_parts))
    back = [(i + 1, i) for i in range(seq_count - 1)]
    incoming = lax.ppermute(lead.astype(LOW), "seq", back).astype(FULL)
    grad_projected = lax.dynamic_update_slice(
        grad_projected, (edge + incoming).astype(LOW), (row_count - 8, 0)
    )
    grad_strength = grad_strength.astype(LOW).astype(FULL)
    grad_logits = (grad_strength * strength * (1.0 - strength)).astype(LOW)
    def core_rows(values):
        by_core = values.reshape(row_count, fsdp_count, 2, half)
        return [
            lax.dynamic_slice_in_dim(by_core, at, 1, 2).reshape(row_count, width // 2) for at in (core, 1 - core)
        ]

    grad_mixer = [low_dot(one, grad_projected, (0, 0)) for one in core_rows(normed_low)]
    grad_output = [low_dot(one, grad_attention, (0, 0)) for one in core_rows(head_normed)]
    square_grads = jnp.concatenate(
        [
            (mine + core_swapped(other.astype(LOW)).astype(FULL)).astype(LOW)
            for mine, other in (grad_mixer, grad_output)
        ],
        axis=1,
    )
    square_grads, ff_part, grad_projected, grad_logits = lax.optimization_barrier(
        (square_grads, ff_part, grad_projected, grad_logits)
    )
    square_part = lax.psum_scatter(square_grads, "fsdp", scatter_dimension=0, tiled=True)
    grad_strength_weight = low_dot(grad_logits, normed_low, (0, 0))
    grad_normed = low_dot(grad_logits, strength_full, (1, 0)) + low_dot(grad_projected, mixer_full, (1, 1))
    ff_stack = seq_stacked(ff_part)
    back_one, grad_gain_one = norm_back(unit_one, scale_one, gains_wide[0], grad_normed)
    input_grad = grad_residual + back_one

    head_row = jnp.pad(
        grad_head_gain.reshape(fsdp_count, head_part), ((0, 0), (0, shard - head_part))
    ).reshape(1, width)
    small_grads = jnp.concatenate(
        [
            grad_strength_weight,
            grad_filter.reshape(3 * CONV, width),
            grad_gain_one[None],
            grad_gain_two[None],
            head_row,
            jnp.zeros((-small_count % 8, width), FULL),
        ],
        axis=0,
    )
    small_pieces = small_grads.reshape(-1, fsdp_count, shard).transpose(1, 0, 2)

    ff_stack, input_grad, small_pieces = lax.optimization_barrier((ff_stack, input_grad, small_pieces))
    new_gate_up_moment, new_down_moment, wide_sent = wide_moments(gate_up_moment, down_moment, ff_stack, seq_count)
    owners = tuple(matrix_owners(fsdp_count))
    chip = seq_index // 2
    mixer_prior = lax.dynamic_slice_in_dim(mixer_moment, core * half, half, 1)
    output_prior = lax.dynamic_slice_in_dim(output_moment, core * half, half, 0)
    square_prior = jnp.concatenate(
        [mixer_prior[j, :, g * span : (g + 1) * span] for g in range(groups) for j in range(3)] + [output_prior], axis=1
    )
    block_output = residual + (out_near + sum(one.astype(FULL) for one in out_parts))
    wide_sent, square_prior, block_output = lax.optimization_barrier((wide_sent, square_prior, block_output))
    square_sum, small_own, square_all, wide_all = middle(
        square_part, square_prior, small_pieces, wide_sent, owners, 2, seq_count, fsdp_count
    )
    square_rows = orthogonal(square_all, owners[3:], orth_square, fsdp_index, chip, fsdp_count)
    wide_rows = orthogonal(wide_all, owners[:3], orth_wide, fsdp_index, chip, fsdp_count)
    wide_parts, square_parts = handed_back(wide_rows, square_rows, owners, 3, seq_count, fsdp_count)
    weights = (
        mixer_weight, output_weight, gate_up_weight, down_weight, strength_weight, filter_weight, norm_gain, head_gain
    )
    moments = (mixer_moment, output_moment, strength_moment, filter_moment, gain_moment, head_gain_moment)
    done = finished(
        wide_parts.reshape(3, shard, -1),
        square_parts.reshape(4, shard, width),
        square_sum.reshape(shard, -1),
        small_own,
        weights,
        moments,
    )
    head_pair = [one[0] for one in done[8:10]]
    return (
        (block_output, input_grad)
        + tuple(done[:8])
        + tuple(head_pair)
        + tuple(done[10:12])
        + (new_gate_up_moment, done[12], new_down_moment, done[13])
    )


def solution(mesh):
    return jax.shard_map(
        on_device,
        mesh=mesh,
        in_specs=(
            P(("seq", "fsdp"), None),
            P(("seq", "fsdp"), None),
            P(),
            P(None, "fsdp", None),
            P("fsdp", None),
            P(None, None, "fsdp"),
            P(None, "fsdp"),
            P("fsdp"),
            P("fsdp", None),
            P(None, "fsdp", None),
            P(None, "fsdp"),
            P(None, "fsdp", None),
            P("fsdp", None),
            P(None, None, "fsdp"),
            P(None, "fsdp"),
            P("fsdp"),
            P("fsdp", None),
            P(None, "fsdp", None),
            P(None, "fsdp"),
        ),
        out_specs=(
            P(("seq", "fsdp"), None),
            P(("seq", "fsdp"), None),
            P(None, "fsdp", None),
            P(None, "fsdp", None),
            P("fsdp", None),
            P("fsdp", None),
            P(None, None, "fsdp"),
            P(None, None, "fsdp"),
            P(None, "fsdp"),
            P(None, "fsdp"),
            P("fsdp"),
            P("fsdp"),
            P("fsdp", None),
            P("fsdp", None),
            P(None, "fsdp", None),
            P(None, "fsdp", None),
            P(None, "fsdp"),
            P(None, "fsdp"),
        ),
        check_vma=False,
    )
```

```python
from functools import partial

import jax
import jax.numpy as jnp
from jax import lax
from jax.experimental import pallas as pl
from jax.experimental.pallas import tpu as pltpu
from jax.sharding import PartitionSpec as P

HD = 128
CONV = 4
BLOCK = 128
GROUP = 8
RIM = 16
NS_STEPS = 3

norm_eps = 1e-06
head_eps = 0.001
momentum_decay = 0.9
matrix_rate = 1.0
filter_rate = 0.01
gain_rate = 0.001
strength_rate = 0.001
coef_linear = 3.4445
coef_cubic = -4.775
coef_quintic = 2.0315

LOW = jnp.bfloat16
FULL = jnp.float32


def halves(values):
    top = values.astype(LOW)
    return (top, (values - top.astype(FULL)).astype(LOW))


def product(left, right, dims=(1, 0)):
    left = left if isinstance(left, tuple) else (left,)
    right = right if isinstance(right, tuple) else (right,)
    total = None
    for i, a in enumerate(left):
        for j, b in enumerate(right):
            if i + j < 2:
                term = lax.dot_general(
                    a, b, (((dims[0],), (dims[1],)), ((), ())), preferred_element_type=FULL
                )
                total = term if total is None else total + term
    return total


def low_product(left, right, dims=(1, 0)):
    return product(left.astype(LOW), right.astype(LOW), dims)


def lanes(values, head):
    return values[:, head * HD : (head + 1) * HD]


def unit_scale(values):
    return lax.rsqrt(jnp.sum(values * values, axis=-1, keepdims=True) + norm_eps)


def block_ids():
    rows = lax.broadcasted_iota(jnp.int32, (BLOCK, BLOCK), 0)
    cols = lax.broadcasted_iota(jnp.int32, (BLOCK, BLOCK), 1)
    return rows, cols


def short_conv(current, previous, taps, meta):
    joined = jnp.concatenate([previous, current], axis=0)
    total = None
    shifted = []
    for lag in range(CONV):
        moved = joined if lag == 0 else pltpu.roll(joined, lag, 0)
        moved = moved[RIM:] * meta[:, lag : lag + 1]
        shifted.append(moved)
        term = moved * taps[lag : lag + 1, :]
        total = term if total is None else total + term
    return total, shifted


def inverse(system, differ):
    rows, cols = block_ids()
    eye = jnp.where(rows == cols, 1.0, 0.0).astype(FULL)
    found = [eye - jnp.where((differ >> 0) == 1, one, 0.0) for one in system]
    level = 1
    while (1 << level) < BLOCK:
        picked = [jnp.where((differ >> level) == 1, one, 0.0).astype(LOW) for one in system]
        low = [one.astype(LOW) for one in found]
        inner = [product(a, b).astype(LOW) for a, b in zip(picked, low)]
        outer = [product(b, a) for a, b in zip(inner, low)]
        found = [a - b for a, b in zip(found, outer)]
        level += 1
    split = [halves(one) for one in found]
    wide = [halves(one) for one in system]
    error = [eye - a - product(b, c) for a, b, c in zip(found, wide, split)]
    return [a + product(b[0], c.astype(LOW)) for a, b, c in zip(found, split, error)]


def forward_kernel(
    proj_ref, prev_ref, rim_ref, taps_ref, strength_ref, strength_row_ref, meta_ref, meta_row_ref,
    mixed_ref, solve_ref, weight_ref, update_ref, drift_ref, out_ref, query_ref, state_ref, end_ref, transfer_ref,
    carry_ref,
):
    step = pl.program_id(1)
    rows, cols = block_ids()
    meta = meta_ref[...]
    carry, tail, segment = meta[:, 4:5], meta[:, 5:6], meta[:, 6:7]
    same = segment == meta_row_ref[0:1, :]
    strict = (rows > cols) & same
    inclusive = (rows >= cols) & same
    differ = rows ^ cols
    carry_last = carry[BLOCK - 1 : BLOCK, :]

    @pl.when(step == 0)
    def _():
        start = jnp.concatenate(
            [jnp.zeros((HD, HD), FULL), jnp.where(rows == cols, 1.0, 0.0).astype(FULL)], axis=1
        )
        for head in range(GROUP):
            carry_ref[head] = start

    first = step == 0
    parts = []
    for j in range(3):
        at = slice(j * GROUP * HD, (j + 1) * GROUP * HD)
        previous = jnp.where(first, rim_ref[:, at].astype(FULL), prev_ref[:, at].astype(FULL))
        conv, _ = short_conv(proj_ref[:, at].astype(FULL), previous, taps_ref[j], meta)
        parts.append(conv * jax.nn.sigmoid(conv))
    queries, keys, values = [], [], []
    for head in range(GROUP):
        query, key = lanes(parts[0], head), lanes(parts[1], head)
        queries.append((query * (unit_scale(query) * HD ** (-0.5))).astype(LOW))
        keys.append((key * unit_scale(key)).astype(LOW))
        values.append(lanes(parts[2], head).astype(LOW))
        mixed_ref[0, :, head * HD : (head + 1) * HD] = queries[head]
        mixed_ref[1, :, head * HD : (head + 1) * HD] = keys[head]
        mixed_ref[2, :, head * HD : (head + 1) * HD] = values[head]
    strength = strength_ref[0]
    strength_row = strength_row_ref[0]
    heads = range(GROUP)
    gram = [product(keys[h], keys[h], (1, 1)) for h in heads]
    system = [jnp.where(strict, strength[:, h : h + 1] * gram[h], 0.0) for h in heads]
    scores = [jnp.where(inclusive, product(queries[h], keys[h], (1, 1)), 0.0) for h in heads]
    solve = inverse(system, differ)
    carry_low, tail_low = carry.astype(LOW), tail.astype(LOW)
    carried_query = [queries[h] * carry_low for h in heads]
    tail_key = [keys[h] * tail_low for h in heads]
    right = [jnp.concatenate([values[h], keys[h] * carry_low], axis=1) for h in heads]
    solved = [product(halves(solve[h] * strength_row[h : h + 1, :]), right[h]) for h in heads]
    state = [carry_ref[h] for h in heads]
    state_parts = [halves(state[h]) for h in heads]
    passed = [product(halves(solved[h][:, HD:]), state_parts[h]) for h in heads]
    zero = jnp.zeros((BLOCK, HD), FULL)
    both = [
        jnp.concatenate([solved[h][:, :HD], zero], axis=1) - passed[h] for h in heads
    ]
    both_parts = [halves(both[h]) for h in heads]
    result = [
        product(carried_query[h], state_parts[h]) + product(halves(scores[h]), both_parts[h])
        for h in heads
    ]
    after = [
        carry_last * state[h] + product(tail_key[h], both_parts[h], (0, 0)) for h in heads
    ]
    for h in heads:
        solve_ref[0, h] = solve[h].astype(LOW)
        at = slice(h * HD, (h + 1) * HD)
        weight_ref[:, at] = solved[h][:, HD:].astype(LOW)
        update_ref[:, at] = both[h][:, :HD]
        drift_ref[:, at] = both[h][:, HD:].astype(LOW)
        out_ref[:, at] = result[h][:, :HD]
        query_ref[:, at] = result[h][:, HD:]
        state_ref[0, h] = state[h]
        carry_ref[h] = after[h]
        end_ref[h] = after[h][:, :HD]
        transfer_ref[h] = after[h][:, HD:]


def forward_blocks(projected, rim, taps, strength, meta, meta_row):
    total = projected.shape[0]
    width = projected.shape[1] // 3
    head_count = width // HD
    groups, steps = head_count // GROUP, total // BLOCK
    span = GROUP * HD
    grouped = strength.reshape(total, groups, GROUP)
    strength_col = grouped.transpose(1, 0, 2)
    strength_row = grouped.transpose(1, 2, 0)
    rows_of = lambda g, n: (n, g)
    shapes = (
        jax.ShapeDtypeStruct((3, total, width), LOW),
        jax.ShapeDtypeStruct((steps, head_count, BLOCK, BLOCK), LOW),
        jax.ShapeDtypeStruct((total, width), LOW),
        jax.ShapeDtypeStruct((total, width), FULL),
        jax.ShapeDtypeStruct((total, width), LOW),
        jax.ShapeDtypeStruct((total, width), FULL),
        jax.ShapeDtypeStruct((total, width), FULL),
        jax.ShapeDtypeStruct((steps, head_count, HD, 2 * HD), FULL),
        jax.ShapeDtypeStruct((head_count, HD, HD), FULL),
        jax.ShapeDtypeStruct((head_count, HD, HD), FULL),
    )
    wide = pl.BlockSpec((BLOCK, span), rows_of)
    ratio = BLOCK // RIM
    return pl.pallas_call(
        forward_kernel,
        grid=(groups, steps),
        in_specs=[
            pl.BlockSpec((BLOCK, 3 * span), rows_of),
            pl.BlockSpec((RIM, 3 * span), lambda g, n: (jnp.maximum(n * ratio - 1, 0), g)),
            pl.BlockSpec((RIM, 3 * span), lambda g, n: (0, g)),
            pl.BlockSpec((3, CONV, span), lambda g, n: (0, 0, g)),
            pl.BlockSpec((1, BLOCK, GROUP), lambda g, n: (g, n, 0)),
            pl.BlockSpec((1, GROUP, BLOCK), lambda g, n: (g, 0, n)),
            pl.BlockSpec((BLOCK, 8), lambda g, n: (n, 0)),
            pl.BlockSpec((8, BLOCK), lambda g, n: (0, n)),
        ],
        out_specs=(
            pl.BlockSpec((3, BLOCK, span), lambda g, n: (0, n, g)),
            pl.BlockSpec((1, GROUP, BLOCK, BLOCK), lambda g, n: (n, g, 0, 0)),
            wide,
            wide,
            wide,
            wide,
            wide,
            pl.BlockSpec((1, GROUP, HD, 2 * HD), lambda g, n: (n, g, 0, 0)),
            pl.BlockSpec((GROUP, HD, HD), lambda g, n: (g, 0, 0)),
            pl.BlockSpec((GROUP, HD, HD), lambda g, n: (g, 0, 0)),
        ),
        out_shape=shapes,
        scratch_shapes=[pltpu.VMEM((GROUP, HD, 2 * HD), FULL)],
        compiler_params=pltpu.CompilerParams(vmem_limit_bytes=48 << 20),
        cost_estimate=pl.CostEstimate(flops=8 << 30, bytes_accessed=24 << 20, transcendentals=0),
    )(projected, projected, rim, taps, strength_col, strength_row, meta, meta_row)


def out_kernel(local_ref, query_ref, state_ref, gain_ref, delta_ref, normed_ref):
    gain = gain_ref[0:1, :]
    for head in range(local_ref.shape[1] // HD):
        at = slice(head * HD, (head + 1) * HD)
        value = local_ref[:, at] + product(halves(query_ref[:, at]), halves(state_ref[head]))
        delta_ref[:, at] = value
        scale = lax.rsqrt(jnp.mean(value * value, axis=-1, keepdims=True) + head_eps)
        normed_ref[:, at] = (value * scale * gain).astype(LOW)


def head_outputs(local_out, effective, state_in, gain):
    total, width = local_out.shape
    rows = pl.BlockSpec((BLOCK, width), lambda n: (n, 0))
    return pl.pallas_call(
        out_kernel,
        grid=(total // BLOCK,),
        in_specs=[
            rows,
            rows,
            pl.BlockSpec(state_in.shape, lambda n: (0, 0, 0)),
            pl.BlockSpec((1, HD), lambda n: (0, 0)),
        ],
        out_specs=(rows, rows),
        out_shape=(
            jax.ShapeDtypeStruct((total, width), FULL),
            jax.ShapeDtypeStruct((total, width), LOW),
        ),
        compiler_params=pltpu.CompilerParams(vmem_limit_bytes=32 << 20),
    )(local_out, effective, state_in, gain)


def head_back_kernel(grad_ref, delta_ref, query_ref, gain_ref, upstream_ref, adjoint_ref, gain_grad_ref):
    step = pl.program_id(0)
    gain = gain_ref[0:1, :]

    @pl.when(step == 0)
    def _():
        adjoint_ref[...] = jnp.zeros_like(adjoint_ref)
        gain_grad_ref[...] = jnp.zeros_like(gain_grad_ref)

    gained = jnp.zeros((1, HD), FULL)
    for head in range(grad_ref.shape[1] // HD):
        at = slice(head * HD, (head + 1) * HD)
        value = delta_ref[:, at]
        grad = grad_ref[:, at].astype(FULL)
        scale = lax.rsqrt(jnp.mean(value * value, axis=-1, keepdims=True) + head_eps)
        unit = value * scale
        gained = gained + jnp.sum(grad * unit, axis=0, keepdims=True)
        grad = grad * gain
        back = scale * (grad - unit * jnp.mean(grad * unit, axis=-1, keepdims=True))
        low = back.astype(LOW)
        upstream_ref[:, at] = low
        adjoint_ref[head] += product(query_ref[:, at].astype(LOW), low, (0, 0))
    gain_grad_ref[...] += gained


def head_back(grad_normed, delta_out, effective, gain):
    total, width = delta_out.shape
    head_count = width // HD
    rows = pl.BlockSpec((BLOCK, width), lambda n: (n, 0))
    return pl.pallas_call(
        head_back_kernel,
        grid=(total // BLOCK,),
        in_specs=[rows, rows, rows, pl.BlockSpec((1, HD), lambda n: (0, 0))],
        out_specs=(
            rows,
            pl.BlockSpec((head_count, HD, HD), lambda n: (0, 0, 0)),
            pl.BlockSpec((1, HD), lambda n: (0, 0)),
        ),
        out_shape=(
            jax.ShapeDtypeStruct((total, width), LOW),
            jax.ShapeDtypeStruct((head_count, HD, HD), FULL),
            jax.ShapeDtypeStruct((1, HD), FULL),
        ),
        compiler_params=pltpu.CompilerParams(vmem_limit_bytes=32 << 20),
    )(grad_normed, delta_out, effective, gain)


def backward_kernel(
    proj_ref, prev_ref, rim_ref, taps_ref, strength_ref, meta_ref, meta_row_ref,
    mixed_ref, solve_ref, weight_ref, update_ref, drift_ref, upstream_ref, state_ref, enter_ref, leave_ref,
    grad_ref, strength_grad_ref, taps_grad_ref, edge_ref, lead_ref,
    adjoint_ref, spill_ref,
):
    turn = pl.program_id(1)
    last_turn = pl.num_programs(1) - 1
    rows, cols = block_ids()
    meta = meta_ref[...]
    carry, tail, segment = meta[:, 4:5], meta[:, 5:6], meta[:, 6:7]
    same = segment == meta_row_ref[0:1, :]
    strict = (rows > cols) & same
    inclusive = (rows >= cols) & same
    carry_last = carry[BLOCK - 1 : BLOCK, :]
    carry_low, tail_low = carry.astype(LOW), tail.astype(LOW)
    heads = range(GROUP)

    @pl.when(turn == 0)
    def _():
        for h in heads:
            adjoint_ref[h] = leave_ref[h]
        spill_ref[...] = jnp.zeros_like(spill_ref)
        taps_grad_ref[...] = jnp.zeros_like(taps_grad_ref)

    strength = strength_ref[0]
    at = [slice(h * HD, (h + 1) * HD) for h in heads]
    query = [mixed_ref[0, :, at[h]] for h in heads]
    key = [mixed_ref[1, :, at[h]] for h in heads]
    value = [mixed_ref[2, :, at[h]] for h in heads]
    upstream = [upstream_ref[:, at[h]] for h in heads]
    enter = [enter_ref[h].astype(LOW) for h in heads]
    state = [
        (state_ref[0, h, :, :HD] + product(state_ref[0, h, :, HD:].astype(LOW), enter[h])).astype(LOW)
        for h in heads
    ]
    update = [
        (update_ref[:, at[h]] + product(drift_ref[:, at[h]], enter[h])).astype(LOW) for h in heads
    ]
    gram = [product(key[h], key[h], (1, 1)) for h in heads]
    scores = [
        jnp.where(inclusive, product(query[h], key[h], (1, 1)), 0.0).astype(LOW) for h in heads
    ]
    tail_key = [key[h] * tail_low for h in heads]
    adjoint = [adjoint_ref[h] for h in heads]
    adjoint_low = [adjoint[h].astype(LOW) for h in heads]
    grad_update = [
        (product(scores[h], upstream[h], (0, 0)) + product(tail_key[h], adjoint_low[h])).astype(LOW)
        for h in heads
    ]
    for h in heads:
        adjoint_ref[h] = (
            carry_last * adjoint[h]
            + product(query[h] * carry_low, upstream[h], (0, 0))
            - product(weight_ref[:, at[h]], grad_update[h], (0, 0))
        )
    grad_right = [product(solve_ref[0, h], grad_update[h], (0, 0)) for h in heads]
    right_low = [grad_right[h].astype(LOW) for h in heads]
    grad_scores = [
        jnp.where(inclusive, product(upstream[h], update[h], (1, 1)), 0.0).astype(LOW) for h in heads
    ]
    grad_query = [
        carry * product(upstream[h], state[h], (1, 1)) + product(grad_scores[h], key[h]) for h in heads
    ]
    right_state = [product(right_low[h], state[h], (1, 1)) for h in heads]
    grad_system = [
        jnp.where(strict, -product(right_low[h], update[h], (1, 1)), 0.0) for h in heads
    ]
    beta = [strength[:, h : h + 1] for h in heads]
    grad_gram = [(beta[h] * grad_system[h]).astype(LOW) for h in heads]
    grad_key = [
        product(grad_scores[h], query[h], (0, 0))
        + tail * product(update[h], adjoint_low[h], (1, 1))
        - (beta[h] * carry) * right_state[h]
        + product(grad_gram[h], key[h])
        + product(grad_gram[h], key[h], (0, 0))
        for h in heads
    ]
    grad_value = [beta[h] * grad_right[h] for h in heads]
    columns = [
        jnp.sum(
            grad_right[h] * value[h].astype(FULL)
            - carry * right_state[h] * key[h].astype(FULL)
            + grad_system[h] * gram[h],
            axis=-1,
            keepdims=True,
        )
        for h in heads
    ]
    strength_grad_ref[0] = jnp.concatenate(columns, axis=1)

    def rounded(values):
        return values.astype(LOW).astype(FULL)

    first = turn == last_turn
    grads = (grad_query, grad_key, grad_value)
    span = GROUP * HD
    for j in range(3):
        at = slice(j * span, (j + 1) * span)
        previous = jnp.where(first, rim_ref[:, at].astype(FULL), prev_ref[:, at].astype(FULL))
        taps = taps_ref[j]
        conv, shifted = short_conv(proj_ref[:, at].astype(FULL), previous, taps, meta)
        gate = jax.nn.sigmoid(conv)
        active = conv * gate
        pieces = []
        for h in heads:
            grad = rounded(grads[j][h])
            if j < 2:
                raw = lanes(active, h)
                scale = unit_scale(raw)
                unit = raw * scale
                if j == 0:
                    grad = grad * HD ** (-0.5)
                grad = scale * (grad - unit * jnp.sum(unit * grad, axis=-1, keepdims=True))
            pieces.append(grad)
        grad_conv = jnp.concatenate(pieces, axis=1) * (gate * (1.0 + conv * (1.0 - gate)))
        total = None
        for lag in range(CONV):
            taps_grad_ref[j, lag : lag + 1, :] += jnp.sum(grad_conv * shifted[lag], axis=0, keepdims=True)
            spread = grad_conv * (meta[:, lag : lag + 1] * taps[lag : lag + 1, :])
            spread = jnp.concatenate([jnp.zeros((8, span), FULL), spread], axis=0)
            if lag:
                spread = pltpu.roll(spread, BLOCK + 8 - lag, 0)
            total = spread if total is None else total + spread
        bottom = total[BLOCK:] + spill_ref[j]
        spill_ref[j] = total[:8]
        grad_ref[:, at] = jnp.concatenate([total[8:BLOCK], bottom], axis=0).astype(LOW)

        @pl.when(turn == 0)
        def _():
            edge_ref[:, at] = bottom

        lead_ref[:, at] = total[:8]


def backward_blocks(
    projected, rim, taps, strength, meta, meta_row, mixed, solve, weight, update, drift, upstream,
    states, enter, leave,
):
    total, width = projected.shape[0], projected.shape[1] // 3
    head_count = width // HD
    groups, steps = head_count // GROUP, total // BLOCK
    span = GROUP * HD
    strength_col = strength.reshape(total, groups, GROUP).transpose(1, 0, 2)
    ratio = BLOCK // RIM
    back = lambda n: steps - 1 - n
    wide = pl.BlockSpec((BLOCK, span), lambda g, n: (back(n), g))
    deep = pl.BlockSpec((3, BLOCK, span), lambda g, n: (0, back(n), g))
    per_group = pl.BlockSpec((GROUP, HD, HD), lambda g, n: (g, 0, 0))
    flat = pl.BlockSpec((BLOCK, 3 * span), lambda g, n: (back(n), g))
    narrow = pl.BlockSpec((8, 3 * span), lambda g, n: (0, g))
    grads, strength_grad, taps_grad, edge, lead = pl.pallas_call(
        backward_kernel,
        grid=(groups, steps),
        in_specs=[
            flat,
            pl.BlockSpec((RIM, 3 * span), lambda g, n: (jnp.maximum(back(n) * ratio - 1, 0), g)),
            pl.BlockSpec((RIM, 3 * span), lambda g, n: (0, g)),
            pl.BlockSpec((3, CONV, span), lambda g, n: (0, 0, g)),
            pl.BlockSpec((1, BLOCK, GROUP), lambda g, n: (g, back(n), 0)),
            pl.BlockSpec((BLOCK, 8), lambda g, n: (back(n), 0)),
            pl.BlockSpec((8, BLOCK), lambda g, n: (0, back(n))),
            deep,
            pl.BlockSpec((1, GROUP, BLOCK, BLOCK), lambda g, n: (back(n), g, 0, 0)),
            wide,
            wide,
            wide,
            wide,
            pl.BlockSpec((1, GROUP, HD, 2 * HD), lambda g, n: (back(n), g, 0, 0)),
            per_group,
            per_group,
        ],
        out_specs=(
            flat,
            pl.BlockSpec((1, BLOCK, GROUP), lambda g, n: (g, back(n), 0)),
            pl.BlockSpec((3, CONV, span), lambda g, n: (0, 0, g)),
            narrow,
            narrow,
        ),
        out_shape=(
            jax.ShapeDtypeStruct((total, 3 * width), LOW),
            jax.ShapeDtypeStruct((groups, total, GROUP), FULL),
            jax.ShapeDtypeStruct((3, CONV, width), FULL),
            jax.ShapeDtypeStruct((8, 3 * width), FULL),
            jax.ShapeDtypeStruct((8, 3 * width), FULL),
        ),
        scratch_shapes=[pltpu.VMEM((GROUP, HD, HD), FULL), pltpu.VMEM((3, 8, span), FULL)],
        compiler_params=pltpu.CompilerParams(vmem_limit_bytes=48 << 20),
        cost_estimate=pl.CostEstimate(flops=4 << 30, bytes_accessed=24 << 20, transcendentals=0),
    )(
        projected, projected, rim, taps, strength_col, meta, meta_row, mixed, solve, weight, update,
        drift, upstream, states, enter, leave,
    )
    return grads, strength_grad.transpose(1, 0, 2).reshape(total, head_count), taps_grad, edge, lead


def fsdp_split(count):
    along = 4 if count % 4 == 0 else 1
    return along, count // along


def gather_kernel(along, across, seq_count, shard_ref, small_ref, full_ref, small_full_ref, local_sem, small_send,
                  small_recv, z_send, z_recv, x_send, x_recv, core_send, core_recv):
    count = along * across
    seq, mine = lax.axis_index("seq"), lax.axis_index("fsdp")
    core, z, x = lax.rem(seq, 2), lax.div(mine, across), lax.rem(mine, across)
    partner = seq + 1 - 2 * core
    rows = shard_ref.shape[0]
    half = rows // 2
    mesh_id = pl.DeviceIdType.MESH

    barrier = pltpu.get_barrier_semaphore()
    for d in range(1, count):
        pl.semaphore_signal(barrier, inc=1, device_id=(seq, lax.rem(mine + d, count)), device_id_type=mesh_id)
    pl.semaphore_signal(barrier, inc=1, device_id=(partner, mine), device_id_type=mesh_id)
    pl.semaphore_wait(barrier, count)

    def place(k, j):
        owner = lax.rem(z - k + along, along) * across + lax.rem(x - j + across, across)
        start = pl.multiple_of(owner * rows + core * half, 16)
        return full_ref.at[pl.ds(start, half), :]

    own_half = shard_ref.at[pl.ds(pl.multiple_of(core * half, 16), half), :]
    keep = pltpu.make_async_copy(
        shard_ref, full_ref.at[pl.ds(pl.multiple_of(mine * rows, 16), rows), :], local_sem.at[0]
    )
    keep.start()
    small_place = small_full_ref.at[:, pl.ds(pl.multiple_of(mine * 128, 128), 128)]
    keep_small = pltpu.make_async_copy(small_ref, small_place, local_sem.at[1])
    keep_small.start()

    def sent(source, target, send, recv, device):
        copy = pltpu.make_async_remote_copy(
            src_ref=source, dst_ref=target, send_sem=send, recv_sem=recv, device_id=device, device_id_type=mesh_id
        )
        copy.start()
        return copy

    def along_z(k):
        source = own_half if k == 1 else place(k - 1, 0)
        device = (seq, lax.rem(z + 1, along) * across + x)
        return sent(source, place(k - 1, 0), z_send.at[k - 1], z_recv.at[k - 1], device)

    def along_x(k, j):
        source = own_half if k == 0 else place(k, 0)
        at = k * (across - 1) + j - 1
        device = (seq, z * across + lax.rem(x + j, across))
        return sent(source, place(k, 0), x_send.at[at], x_recv.at[at], device)

    def to_core(k, j):
        at = k * across + j
        return sent(place(k, j), place(k, j), core_send.at[at], core_recv.at[at], (partner, mine))

    copies = []
    z_copies = {1: along_z(1)} if along > 1 else {}
    x_copies = {}
    for j in range(1, across):
        x_copies[0, j] = along_x(0, j)
    for d in range(1, count):
        copies.append(
            sent(small_ref, small_place, small_send.at[d - 1], small_recv.at[d - 1],
                 (seq, lax.rem(mine + d, count)))
        )
    core_copies = []
    for k in range(1, along):
        z_copies[k].wait_recv()
        if k + 1 < along:
            z_copies[k + 1] = along_z(k + 1)
        for j in range(1, across):
            x_copies[k, j] = along_x(k, j)
        core_copies.append(to_core(k, 0))
        for j in range(1, across):
            x_copies[k - 1, j].wait_recv()
            core_copies.append(to_core(k - 1, j))
    for j in range(1, across):
        x_copies[along - 1, j].wait_recv()
        core_copies.append(to_core(along - 1, j))
    keep.wait()
    keep_small.wait()
    for copy in list(z_copies.values()) + list(x_copies.values()):
        copy.wait_send()
    for copy in copies + core_copies:
        copy.wait()


def gathered_mixer(shard, small, seq_count, fsdp_count):
    along, across = fsdp_split(fsdp_count)
    rows, width = shard.shape
    dma = pltpu.SemaphoreType.DMA
    hold = pl.BlockSpec(memory_space=pl.ANY)
    links = max(along * (across - 1), 1)
    return pl.pallas_call(
        partial(gather_kernel, along, across, seq_count),
        in_specs=[hold, hold],
        out_specs=(hold, hold),
        out_shape=(
            jax.ShapeDtypeStruct((rows * fsdp_count, width), shard.dtype),
            jax.ShapeDtypeStruct((small.shape[0], fsdp_count * 128), small.dtype),
        ),
        scratch_shapes=[
            dma((2,)),
            dma((fsdp_count - 1,)),
            dma((fsdp_count - 1,)),
            dma((along,)),
            dma((along,)),
            dma((links,)),
            dma((links,)),
            dma((along * across,)),
            dma((along * across,)),
        ],
        compiler_params=pltpu.CompilerParams(collective_id=0, has_side_effects=True),
    )(shard, small)


def core_swapped(value):
    count = lax.axis_size("seq")
    return lax.ppermute(value, "seq", [(i, i + 1 - 2 * (i % 2)) for i in range(count)])


def chip_shifted(value, by):
    count = lax.axis_size("seq")
    return lax.ppermute(value, "seq", [(i, (i + 2 * by) % count) for i in range(count)])


def seq_blocks(value):
    chips = lax.axis_size("seq") // 2
    far = [chip_shifted(value, k) for k in range(1, chips)]
    found = []
    for one in [value] + far:
        found += [one, core_swapped(one)]
    return found


def seq_stacked(value):
    count, index = lax.axis_size("seq"), lax.axis_index("seq")
    core = index % 2
    result = jnp.zeros((count,) + value.shape, value.dtype)
    for place, one in enumerate(seq_blocks(value)):
        chip = (index // 2 - place // 2) % (count // 2)
        at = chip * 2 + (core if place % 2 == 0 else 1 - core)
        result = lax.dynamic_update_slice_in_dim(result, one[None], at, 0)
    return result


def low_dot(left, right, dims):
    return lax.dot_general(left, right, (((dims[0],), (dims[1],)), ((), ())), preferred_element_type=FULL)


def exchange_kernel(backward, seq_count, local_ref, transfer_ref, result_ref, local_low, transfer_low, other_local,
                    other_transfer, chip_ref, sent_ref,
                    swap_send, swap_recv, chip_send, chip_recv, half_send, half_recv):
    seq, mine = lax.axis_index("seq"), lax.axis_index("fsdp")
    core, chip = lax.rem(seq, 2), lax.div(seq, 2)
    partner = seq + 1 - 2 * core
    chips = seq_count // 2
    heads = local_ref.shape[0]
    mesh_id = pl.DeviceIdType.MESH
    lead = core == (1 if backward else 0)
    dims = (0, 0) if backward else (1, 0)
    step = -1 if backward else 1

    for head in range(heads):
        chip_ref[head] = jnp.zeros((HD, HD), LOW)
        local_low[head] = local_ref[head].astype(LOW)
        transfer_low[head] = transfer_ref[head].astype(LOW)
    barrier = pltpu.get_barrier_semaphore()
    pl.semaphore_signal(barrier, inc=1, device_id=(partner, mine), device_id_type=mesh_id)
    for k in range(1, chips):
        other = lax.rem(seq + 2 * k, seq_count)
        pl.semaphore_signal(barrier, inc=1, device_id=(other, mine), device_id_type=mesh_id)
    pl.semaphore_wait(barrier, chips)

    swaps = [
        pltpu.make_async_remote_copy(
            src_ref=source, dst_ref=target, send_sem=swap_send.at[i], recv_sem=swap_recv.at[i],
            device_id=(partner, mine), device_id_type=mesh_id,
        )
        for i, (source, target) in enumerate(((local_low, other_local), (transfer_low, other_transfer)))
    ]
    for swap in swaps:
        swap.start()
    for swap in swaps:
        swap.wait()
    share = pl.ds(pl.multiple_of(core * (heads // 2), heads // 2), heads // 2)

    def applied(matrix, value):
        return product(matrix, value.astype(LOW), dims)

    def by_role(head):
        own_local, own_transfer = local_ref[head], transfer_low[head]
        far_local, far_transfer = other_local[head].astype(FULL), other_transfer[head]
        return (
            jnp.where(lead, own_local, far_local),
            jnp.where(lead, own_transfer, far_transfer),
            jnp.where(lead, far_local, own_local),
            jnp.where(lead, far_transfer, own_transfer),
        )

    for i in range(chips - 1):
        source = chips - 1 - i if backward else i

        @pl.when(chip == source)
        def _():
            for head in range(heads):
                lead_local, lead_transfer, trail_local, trail_transfer = by_role(head)
                inner = lead_local if i == 0 else lead_local + applied(lead_transfer, chip_ref[head])
                sent_ref[head] = (trail_local + applied(trail_transfer, inner)).astype(LOW)

        onward = pltpu.make_async_remote_copy(
            src_ref=sent_ref.at[share], dst_ref=chip_ref.at[share], send_sem=chip_send.at[i], recv_sem=chip_recv.at[i],
            device_id=(lax.rem(seq + 2 * step + seq_count, seq_count), mine), device_id_type=mesh_id,
        )
        half = pltpu.make_async_remote_copy(
            src_ref=chip_ref.at[share], dst_ref=chip_ref.at[share], send_sem=half_send.at[i], recv_sem=half_recv.at[i],
            device_id=(partner, mine), device_id_type=mesh_id,
        )

        @pl.when(chip == source)
        def _():
            onward.start()
            onward.wait_send()

        @pl.when(chip == source + step)
        def _():
            onward.wait_recv()
            half.start()
            half.wait()

    for head in range(heads):
        lead_local, lead_transfer, _, _ = by_role(head)
        state = chip_ref[head]
        result_ref[head] = jnp.where(lead, state.astype(FULL), lead_local + applied(lead_transfer, state))


def exchanged(local, transfer, backward, call_id):
    seq_count = lax.axis_size("seq")
    dma = pltpu.SemaphoreType.DMA
    vmem = pl.BlockSpec(memory_space=pltpu.VMEM)
    hops = max(seq_count // 2 - 1, 1)
    return pl.pallas_call(
        partial(exchange_kernel, backward, seq_count),
        in_specs=[vmem, vmem],
        out_specs=vmem,
        out_shape=jax.ShapeDtypeStruct(local.shape, FULL),
        scratch_shapes=[pltpu.VMEM(local.shape, LOW)] * 6 + [dma((2,))] * 2 + [dma((hops,))] * 4,
        compiler_params=pltpu.CompilerParams(collective_id=call_id, has_side_effects=True, vmem_limit_bytes=24 << 20),
    )(local, transfer)


def norm_back(unit, scale, gain, grad):
    gained = jnp.sum(grad * unit, axis=0)
    grad = grad * gain
    return scale * (grad - unit * jnp.mean(grad * unit, axis=-1, keepdims=True)), gained


def matrix_owners(fsdp_count):
    along, across = fsdp_split(fsdp_count)
    if along == 4 and across > 1:
        first, second = across, 2 * across + 1
        return [(0, first), (0, second), (1, first), (1, second), (1, first + 1), (0, first + 1), (1, second - 1)]
    return [(m % 2, m * fsdp_count // 7) for m in range(7)]


def remote(source, target, send, recv, device):
    return pltpu.make_async_remote_copy(
        src_ref=source, dst_ref=target, send_sem=send, recv_sem=recv, device_id=device,
        device_id_type=pl.DeviceIdType.MESH,
    )


class Place:
    def __init__(self, seq_count, count):
        self.seq_count, self.count, self.chips = seq_count, count, seq_count // 2
        self.seq, self.mine = lax.axis_index("seq"), lax.axis_index("fsdp")
        self.core, self.chip = lax.rem(self.seq, 2), lax.div(self.seq, 2)
        self.partner = (self.seq + 1 - 2 * self.core, self.mine)

    def fsdp(self, d):
        return lax.rem(self.mine + d, self.count)

    def next_seq(self, k):
        return (lax.rem(self.seq + k, self.seq_count), self.mine)

    def next_chip(self, k):
        return (lax.rem(self.seq + 2 * k, self.seq_count), self.mine)

    def greet(self, chips_too):
        barrier = pltpu.get_barrier_semaphore()
        others = [(self.seq, self.fsdp(d)) for d in range(1, self.count)]
        others += [self.next_seq(k) for k in range(1, self.seq_count)] if chips_too else [self.partner]
        for other in others:
            pl.semaphore_signal(barrier, inc=1, device_id=other, device_id_type=pl.DeviceIdType.MESH)
        pl.semaphore_wait(barrier, len(others))


def collect(here, owners, pieces, whole, send, recv, local_sem, core_send, core_recv):
    def piece(n, target, source):
        return remote(pieces.at[n], whole.at[source, here.core], send.at[n], recv.at[source], (here.seq, target))

    for n, (row, owner) in enumerate(owners):
        @pl.when((here.chip == row) & (here.mine != owner))
        def _():
            piece(n, owner, here.mine).start()

    def finish():
        for n, (row, owner) in enumerate(owners):
            @pl.when((here.chip == row) & (here.mine == owner))
            def _():
                keep = pltpu.make_async_copy(pieces.at[n], whole.at[here.mine, here.core], local_sem)
                keep.start()
                for d in range(1, here.count):
                    piece(n, here.fsdp(d), here.fsdp(d)).wait_recv()
                keep.wait()
                half = whole.at[:, here.core]
                swap = remote(half, half, core_send, core_recv, here.partner)
                swap.start()
                swap.wait()

        for n, (row, owner) in enumerate(owners):
            @pl.when((here.chip == row) & (here.mine != owner))
            def _():
                piece(n, owner, here.mine).wait_send()

    return finish


def hand_back(here, owners, rows, parts, local_sem, send, recv, chip_send, chip_recv, core_send, core_recv):
    def part(m):
        return parts.at[m, here.core]

    def piece(m, d):
        return remote(rows.at[here.fsdp(d)], part(m), send.at[d], recv.at[m], (here.seq, here.fsdp(d)))

    def onward(m, k):
        return remote(part(m), part(m), chip_send.at[m, k - 1], chip_recv.at[m], here.next_chip(k))

    def swap(m):
        return remote(part(m), part(m), core_send.at[m], core_recv.at[m], here.partner)

    for m, (row, owner) in enumerate(owners):
        @pl.when((here.chip == row) & (here.mine == owner))
        def _():
            for d in range(1, here.count):
                piece(m, d).start()
            keep = pltpu.make_async_copy(rows.at[here.mine], part(m), local_sem)
            keep.start()
            keep.wait()

    def finish():
        for m, (row, owner) in enumerate(owners):
            @pl.when((here.chip == row) & (here.mine != owner))
            def _():
                piece(m, 0).wait_recv()

            @pl.when(here.chip == row)
            def _():
                for k in range(1, here.chips):
                    onward(m, k).start()
                swap(m).start()

        for m, (row, owner) in enumerate(owners):
            @pl.when(here.chip != row)
            def _():
                onward(m, 1).wait_recv()
                swap(m).start()

        for m, (row, owner) in enumerate(owners):
            swap(m).wait()

            @pl.when(here.chip == row)
            def _():
                for k in range(1, here.chips):
                    onward(m, k).wait_send()

            @pl.when((here.chip == row) & (here.mine == owner))
            def _():
                for d in range(1, here.count):
                    piece(m, d).wait_send()

    return finish


def collect_sems(kinds, count):
    dma = pltpu.SemaphoreType.DMA
    return [dma((kinds,)), dma((count,)), dma, dma, dma]


def hand_back_sems(kinds, count, chips):
    dma = pltpu.SemaphoreType.DMA
    return [dma, dma((count,)), dma((kinds,)), dma((kinds, chips)), dma((kinds,)), dma((kinds,)), dma((kinds,))]


def middle_kernel(owners, seq_count, count, part_ref, prior_ref, small_ref, wide_ref, sum_ref, small_out, square_whole,
                  wide_whole, chip_ref, total_ref, piece_ref, place_ref, seq_ref, chip_send, chip_recv, half_sem,
                  place_send, place_recv, seq_send, seq_recv, *sems):
    here = Place(seq_count, count)
    width = piece_ref.shape[2]
    chip_ref[here.chip] = part_ref[...]
    place_ref[here.mine] = small_ref[here.mine]
    here.greet(True)
    small_copies = []
    for d in range(1, count):
        copy = remote(
            small_ref.at[here.fsdp(d)], place_ref.at[here.mine], place_send.at[d - 1], place_recv.at[here.mine],
            (here.seq, here.fsdp(d)),
        )
        copy.start()
        small_copies.append(copy)
    own = chip_ref.at[here.chip]
    onward = [
        remote(own, own, chip_send.at[k - 1], chip_recv.at[here.chip], here.next_chip(k)) for k in range(1, here.chips)
    ]
    for copy in onward:
        copy.start()
    finish_wide = collect(here, owners[:3], wide_ref, wide_whole, *sems[:5])
    for k in range(1, here.chips):
        source = lax.rem(here.chip + k, here.chips)
        other = chip_ref.at[source]
        remote(other, other, chip_send.at[k - 1], chip_recv.at[source], here.next_chip(k)).wait_recv()
    total = chip_ref[0].astype(FULL)
    for i in range(1, here.chips):
        total = total + chip_ref[i].astype(FULL)
    total_ref[...] = total
    fresh = (momentum_decay * prior_ref[...] + total).astype(LOW)
    span = GROUP * HD
    for g in range(width // span):
        for j in range(3):
            at = (3 * g + j) * span
            piece_ref[j, :, g * span : (g + 1) * span] = fresh[:, at : at + span]
    piece_ref[3] = fresh[:, 3 * width :]
    finish_square = collect(here, owners[3:], piece_ref, square_whole, *sems[5:])
    half_copy = remote(total_ref, sum_ref.at[here.core], half_sem.at[0], half_sem.at[1], here.partner)
    half_copy.start()
    keep = pltpu.make_async_copy(total_ref, sum_ref.at[here.core], half_sem.at[2])
    keep.start()
    for d in range(1, count):
        source = here.fsdp(d)
        other = place_ref.at[source]
        remote(other, other, place_send.at[d - 1], place_recv.at[source], (here.seq, source)).wait_recv()
    small = place_ref[0]
    for i in range(1, count):
        small = small + place_ref[i]
    seq_ref[here.seq] = small
    own = seq_ref.at[here.seq]
    for k in range(1, seq_count):
        copy = remote(own, own, seq_send.at[k - 1], seq_recv.at[here.seq], here.next_seq(k))
        copy.start()
        small_copies.append(copy)
    for k in range(1, seq_count):
        source = lax.rem(here.seq + k, seq_count)
        other = seq_ref.at[source]
        remote(other, other, seq_send.at[k - 1], seq_recv.at[source], here.next_seq(k)).wait_recv()
    small = seq_ref[0]
    for i in range(1, seq_count):
        small = small + seq_ref[i]
    small_out[...] = small
    finish_square()
    finish_wide()
    keep.wait()
    half_copy.wait()
    for copy in onward + small_copies:
        copy.wait_send()


def middle(part, prior, small, wide, owners, call_id, seq_count, count):
    half, columns = part.shape
    width = columns // 4
    chips = seq_count // 2
    dma = pltpu.SemaphoreType.DMA
    hold, vmem = pl.BlockSpec(memory_space=pl.ANY), pl.BlockSpec(memory_space=pltpu.VMEM)
    return pl.pallas_call(
        partial(middle_kernel, owners, seq_count, count),
        in_specs=[vmem, vmem, vmem, hold],
        out_specs=(hold, vmem, hold, hold),
        out_shape=(
            jax.ShapeDtypeStruct((2, half, columns), FULL),
            jax.ShapeDtypeStruct(small.shape[1:], FULL),
            jax.ShapeDtypeStruct((count, 2, half, width), LOW),
            jax.ShapeDtypeStruct((count, 2) + wide.shape[1:], LOW),
        ),
        scratch_shapes=[
            pltpu.VMEM((chips, half, columns), LOW),
            pltpu.VMEM((half, columns), FULL),
            pltpu.VMEM((4, half, width), LOW),
            pltpu.VMEM(small.shape, FULL),
            pltpu.VMEM((seq_count,) + small.shape[1:], FULL),
            dma((max(chips - 1, 1),)),
            dma((chips,)),
            dma((3,)),
            dma((count,)),
            dma((count,)),
            dma((seq_count,)),
            dma((seq_count,)),
        ]
        + collect_sems(3, count)
        + collect_sems(4, count),
        compiler_params=pltpu.CompilerParams(collective_id=call_id, has_side_effects=True, vmem_limit_bytes=24 << 20),
    )(part, prior, small, wide)


def hand_back_kernel(owners, seq_count, count, wide_ref, square_ref, wide_parts, square_parts, *sems):
    here = Place(seq_count, count)
    here.greet(True)
    finish_square = hand_back(here, owners[3:], square_ref, square_parts, *sems[7:])
    finish_wide = hand_back(here, owners[:3], wide_ref, wide_parts, *sems[:7])
    finish_square()
    finish_wide()


def handed_back(wide_rows, square_rows, owners, call_id, seq_count, count):
    hold = pl.BlockSpec(memory_space=pl.ANY)
    chips = seq_count // 2
    return pl.pallas_call(
        partial(hand_back_kernel, owners, seq_count, count),
        in_specs=[hold, hold],
        out_specs=(hold, hold),
        out_shape=(
            jax.ShapeDtypeStruct((3, 2) + wide_rows.shape[1:], LOW),
            jax.ShapeDtypeStruct((4, 2) + square_rows.shape[1:], LOW),
        ),
        scratch_shapes=hand_back_sems(3, count, chips) + hand_back_sems(4, count, chips),
        compiler_params=pltpu.CompilerParams(collective_id=call_id, has_side_effects=True),
    )(wide_rows, square_rows)


def tile_count(width, seq_count):
    return -(-(width // HD) // seq_count)


def prepare_kernel(seq_count, mixer_ref, output_ref, gate_up_ref, down_ref, strength_ref, filter_ref, gain_ref, head_ref,
                   square_ref, ff_ref, small_ref):
    shard, width = output_ref.shape
    span = GROUP * HD
    tiles = gate_up_ref.shape[2] // HD
    per = tile_count(gate_up_ref.shape[2], seq_count)
    seq = lax.axis_index("seq")
    for g in range(width // span):
        for j in range(3):
            at = (3 * g + j) * span
            square_ref[:, at : at + span] = mixer_ref[j, :, g * span : (g + 1) * span].astype(LOW)
    square_ref[:, 3 * width :] = output_ref[...].astype(LOW)
    for i in range(per):
        tile = i * seq_count + seq
        at = pl.ds(pl.multiple_of(jnp.minimum(tile, tiles - 1) * HD, HD), HD)
        kept = jnp.where(tile < tiles, 1.0, 0.0).astype(FULL)
        for j in range(2):
            to = (j * per + i) * HD
            ff_ref[:, to : to + HD] = (gate_up_ref[j, :, at] * kept).astype(LOW)
        to = (2 * per + i) * HD
        ff_ref[:, to : to + HD] = (down_ref[at, :] * kept).T.astype(LOW)
    small_ref[...] = jnp.zeros_like(small_ref)
    heads = strength_ref.shape[1]
    rows = [strength_ref[...].T] + [filter_ref[j] for j in range(3)] + [gain_ref[...]]
    at = 0
    for one in rows:
        small_ref[at : at + one.shape[0], :shard] = one.astype(LOW)
        at += one.shape[0]
    small_ref[at : at + 1, : head_ref.shape[1]] = head_ref[...].astype(LOW)


def prepared(mixer, output, gate_up, down, strength, filters, gain, head, seq_count):
    shard, width = output.shape
    columns = 3 * tile_count(gate_up.shape[2], seq_count) * HD
    vmem = pl.BlockSpec(memory_space=pltpu.VMEM)
    return pl.pallas_call(
        partial(prepare_kernel, seq_count),
        in_specs=[vmem] * 8,
        out_specs=(vmem,) * 3,
        out_shape=(
            jax.ShapeDtypeStruct((shard, 4 * width), LOW),
            jax.ShapeDtypeStruct((shard, columns), LOW),
            jax.ShapeDtypeStruct((32, 128), LOW),
        ),
        compiler_params=pltpu.CompilerParams(vmem_limit_bytes=40 << 20),
    )(mixer, output, gate_up, down, strength, filters, gain, head[None])


def wide_moment_kernel(seq_count, gate_up_ref, down_ref, stack_ref, gate_up_out, down_out, sent_ref, hold_ref):
    half = sent_ref.shape[1]
    tiles = gate_up_ref.shape[2] // HD
    per = stack_ref.shape[2] // (3 * HD)
    core = lax.rem(lax.axis_index("seq"), 2)
    mine = pl.ds(pl.multiple_of(core * half, half), half)
    for t in range(tiles):
        source, i = t % seq_count, t // seq_count
        at = slice(t * HD, (t + 1) * HD)
        for j in range(2):
            grad = stack_ref[source, :, (j * per + i) * HD : (j * per + i + 1) * HD].astype(FULL)
            gate_up_out[j, :, at] = momentum_decay * gate_up_ref[j, :, at] + grad
            sent_ref[j, :, at] = gate_up_out[j, mine, at].astype(LOW)
        grad = stack_ref[source, :, (2 * per + i) * HD : (2 * per + i + 1) * HD].astype(FULL)
        fresh = momentum_decay * down_ref[at, :] + grad.T
        down_out[at, :] = fresh
        hold_ref[...] = fresh.T
        sent_ref[2, :, at] = hold_ref[mine, :].astype(LOW)


def wide_moments(gate_up, down, stack, seq_count):
    shard, width = gate_up.shape[1:]
    vmem = pl.BlockSpec(memory_space=pltpu.VMEM)
    return pl.pallas_call(
        partial(wide_moment_kernel, seq_count),
        in_specs=[vmem] * 3,
        out_specs=(vmem,) * 3,
        out_shape=(
            jax.ShapeDtypeStruct(gate_up.shape, FULL),
            jax.ShapeDtypeStruct(down.shape, FULL),
            jax.ShapeDtypeStruct((3, shard // 2, width), LOW),
        ),
        scratch_shapes=[pltpu.VMEM((shard, HD), FULL)],
        compiler_params=pltpu.CompilerParams(vmem_limit_bytes=40 << 20),
    )(gate_up, down, stack)


def finish_kernel(
    wide_ref, square_ref, sum_ref, small_ref, mixer_w, output_w, gate_up_w, down_w, strength_w, filter_w, gain_w, head_w,
    mixer_m, output_m, strength_m, filter_m, gain_m, head_m,
    new_mixer_m, new_mixer_w, new_strength_m, new_strength_w, new_filter_m, new_filter_w, new_gain_m, new_gain_w,
    new_head_m, new_head_w, new_output_m, new_output_w, new_gate_up_w, new_down_w,
):
    shard, width = output_w.shape
    span = GROUP * HD
    for g in range(width // span):
        for j in range(3):
            at, to = (3 * g + j) * span, slice(g * span, (g + 1) * span)
            new_mixer_m[j, :, to] = momentum_decay * mixer_m[j, :, to] + sum_ref[:, at : at + span]
    for j in range(3):
        new_mixer_w[j] = mixer_w[j] - matrix_rate * square_ref[j].astype(FULL)
    new_output_m[...] = momentum_decay * output_m[...] + sum_ref[:, 3 * width :]
    new_output_w[...] = output_w[...] - matrix_rate * square_ref[3].astype(FULL)
    for j in range(2):
        new_gate_up_w[j] = gate_up_w[j] - matrix_rate * wide_ref[j].astype(FULL)
    for t in range(down_w.shape[0] // HD):
        at = slice(t * HD, (t + 1) * HD)
        new_down_w[at, :] = down_w[at, :] - matrix_rate * wide_ref[2, :, at].astype(FULL).T
    heads = strength_w.shape[1]
    fresh = momentum_decay * strength_m[...] + small_ref[:heads, :].T
    new_strength_m[...] = fresh
    new_strength_w[...] = strength_w[...] - strength_rate * fresh
    for j in range(3):
        fresh = momentum_decay * filter_m[j] + small_ref[heads + CONV * j : heads + CONV * (j + 1), :]
        new_filter_m[j] = fresh
        new_filter_w[j] = filter_w[j] - filter_rate * fresh
    at = heads + 3 * CONV
    fresh = momentum_decay * gain_m[...] + small_ref[at : at + 2, :]
    new_gain_m[...] = fresh
    new_gain_w[...] = gain_w[...] - gain_rate * fresh
    fresh = momentum_decay * head_m[...] + small_ref[at + 2 : at + 3, : head_m.shape[1]]
    new_head_m[...] = fresh
    new_head_w[...] = head_w[...] - gain_rate * fresh


def finished(wide, square, total, small, weights, moments):
    mixer_w, output_w, gate_up_w, down_w, strength_w, filter_w, gain_w, head_w = weights
    mixer_m, output_m, strength_m, filter_m, gain_m, head_m = moments
    pairs = [mixer_w, strength_w, filter_w, gain_w, head_w[None], output_w]
    shapes = [jax.ShapeDtypeStruct(one.shape, FULL) for pair in zip(pairs, pairs) for one in pair]
    shapes += [jax.ShapeDtypeStruct(one.shape, FULL) for one in (gate_up_w, down_w)]
    vmem = pl.BlockSpec(memory_space=pltpu.VMEM)
    return pl.pallas_call(
        finish_kernel,
        in_specs=[vmem] * 18,
        out_specs=(vmem,) * len(shapes),
        out_shape=tuple(shapes),
        compiler_params=pltpu.CompilerParams(vmem_limit_bytes=56 << 20),
    )(
        wide, square, total, small, mixer_w, output_w, gate_up_w, down_w, strength_w, filter_w, gain_w, head_w[None],
        mixer_m, output_m, strength_m, filter_m, gain_m, head_m[None],
    )


TILE = 256


def row_loop(rows, body):
    @pl.loop(0, rows // TILE)
    def _(i):
        body(pl.ds(pl.multiple_of(i * TILE, TILE), TILE))


def trace_of(square_ref):
    total = jnp.zeros((1, 1), FULL)
    for i in range(square_ref.shape[0] // TILE):
        tile = square_ref[i * TILE : (i + 1) * TILE, i * TILE : (i + 1) * TILE]
        rows = lax.broadcasted_iota(jnp.int32, (TILE, TILE), 0)
        cols = lax.broadcasted_iota(jnp.int32, (TILE, TILE), 1)
        total = total + jnp.sum(jnp.where(rows == cols, tile, 0.0), keepdims=True)
    return total


def pick_rows(count, half, source_ref, target_ref):
    core = lax.rem(lax.axis_index("seq"), 2)
    for f in range(count):
        at = pl.multiple_of(f * 2 * half + core * half, 16)
        target_ref[f * half : (f + 1) * half, :] = source_ref[pl.ds(at, half), :]


def orth_wide_kernel(
    count, half, whole_ref, out_ref, square_ref, middle_ref, mapped_ref, gathered_ref,
    square_low, mapped_low, first_low, second_low, rows_low, rows_own,
):
    size = whole_ref.shape[0]

    def start(at):
        square_ref[at, :] = product(whole_ref[at, :], whole_ref[...], (1, 1))

    row_loop(size, start)
    scale = 1.0 / (jnp.sqrt(trace_of(square_ref)) + 1e-07)

    def scaled(at):
        value = square_ref[at, :] * (scale * scale)
        square_ref[at, :] = value
        square_low[at, :] = value.astype(LOW)

    row_loop(size, scaled)
    level = 1.0
    gathered_low, spare_low = first_low, second_low
    for sweep in range(NS_STEPS - 1):
        keep_ref = gathered_ref if sweep == 0 else mapped_ref

        def mapping(at):
            value = coef_cubic * square_ref[at, :] + coef_quintic * product(square_low[at, :], square_low[...])
            keep_ref[at, :] = value
            mapped_low[at, :] = value.astype(LOW)

        row_loop(size, mapping)
        if sweep == 0:
            def copy_low(at):
                gathered_low[at, :] = mapped_low[at, :]

            row_loop(size, copy_low)
        else:
            def gather(at):
                value = (
                    coef_linear * gathered_ref[at, :]
                    + level * mapped_ref[at, :]
                    + product(mapped_low[at, :], gathered_low[...])
                )
                gathered_ref[at, :] = value
                spare_low[at, :] = value.astype(LOW)

            row_loop(size, gather)
            gathered_low, spare_low = spare_low, gathered_low
        level = level * coef_linear

        def middle(at):
            value = coef_linear * square_ref[at, :] + product(mapped_low[at, :], square_low[...])
            middle_ref[at, :] = value
            spare_low[at, :] = value.astype(LOW)

        row_loop(size, middle)

        def squared(at):
            value = coef_linear * middle_ref[at, :] + product(spare_low[at, :], mapped_low[...])
            square_ref[at, :] = value
            square_low[at, :] = value.astype(LOW)

        row_loop(size, squared)

    pick_rows(count, half, square_low, rows_low)
    pick_rows(count, half, square_ref, mapped_ref)
    pick_rows(count, half, gathered_ref, middle_ref)
    pick_rows(count, half, whole_ref, rows_own)

    def last(at):
        mapped = coef_cubic * mapped_ref[at, :] + coef_quintic * product(rows_low[at, :], square_low[...])
        value = coef_linear * middle_ref[at, :] + level * mapped + product(mapped.astype(LOW), gathered_low[...])
        rows_low[at, :] = value.astype(LOW)

    row_loop(size // 2, last)
    level = level * coef_linear

    @pl.loop(0, whole_ref.shape[1] // TILE)
    def _(i):
        at = pl.ds(pl.multiple_of(i * TILE, TILE), TILE)
        value = level * rows_own[:, at].astype(FULL) + product(rows_low[...], whole_ref[:, at])
        out_ref[:, at] = (value * scale).astype(LOW)


def orth_square_kernel(
    count, half, whole_ref, out_ref, square_ref, current_ref, square_low, mapped_low, first_low, second_low,
    rows_low, rows_own,
):
    size = whole_ref.shape[0]

    def start(at):
        square_ref[at, :] = product(whole_ref[at, :], whole_ref[...], (1, 1))

    row_loop(size, start)
    scale = 1.0 / (jnp.sqrt(trace_of(square_ref)) + 1e-07)

    def scaled(at):
        value = whole_ref[at, :].astype(FULL) * scale
        current_ref[at, :] = value
        first_low[at, :] = value.astype(LOW)
        value = square_ref[at, :] * (scale * scale)
        square_ref[at, :] = value
        square_low[at, :] = value.astype(LOW)

    row_loop(size, scaled)
    now, later = first_low, second_low
    for sweep in range(NS_STEPS):
        if sweep:
            def squared(at):
                value = product(now[at, :], now[...], (1, 1))
                square_ref[at, :] = value
                square_low[at, :] = value.astype(LOW)

            row_loop(size, squared)

        def mapping(at):
            value = coef_cubic * square_ref[at, :] + coef_quintic * product(square_low[at, :], square_low[...])
            mapped_low[at, :] = value.astype(LOW)

        row_loop(size, mapping)
        if sweep < NS_STEPS - 1:
            def step(at):
                value = coef_linear * current_ref[at, :] + product(mapped_low[at, :], now[...])
                current_ref[at, :] = value
                later[at, :] = value.astype(LOW)

            row_loop(size, step)
            now, later = later, now
    pick_rows(count, half, mapped_low, rows_low)
    pick_rows(count, half, current_ref, rows_own)

    @pl.loop(0, size // TILE)
    def _(i):
        at = pl.ds(pl.multiple_of(i * TILE, TILE), TILE)
        value = coef_linear * rows_own[:, at] + product(rows_low[...], now[:, at])
        out_ref[:, at] = value.astype(LOW)


def orth_call(kernel, scratch, count, whole):
    half, width = whole.shape[2:]
    size = count * 2 * half
    flat = whole.reshape(size, width)
    vmem = pl.BlockSpec(memory_space=pltpu.VMEM)
    result = pl.pallas_call(
        partial(kernel, count, half),
        in_specs=[vmem],
        out_specs=vmem,
        out_shape=jax.ShapeDtypeStruct((size // 2, width), LOW),
        scratch_shapes=scratch(size, width),
        compiler_params=pltpu.CompilerParams(vmem_limit_bytes=56 << 20),
    )(flat)
    return result.reshape(count, half, width)


def orth_wide(count, whole):
    def scratch(size, width):
        return (
            [pltpu.VMEM((size, size), FULL)] * 4
            + [pltpu.VMEM((size, size), LOW)] * 4
            + [pltpu.VMEM((size // 2, size), LOW), pltpu.VMEM((size // 2, width), LOW)]
        )

    return orth_call(orth_wide_kernel, scratch, count, whole)


def orth_square(count, whole):
    def scratch(size, width):
        return (
            [pltpu.VMEM((size, size), FULL)] * 2
            + [pltpu.VMEM((size, size), LOW)] * 4
            + [pltpu.VMEM((size // 2, size), LOW), pltpu.VMEM((size // 2, width), FULL)]
        )

    return orth_call(orth_square_kernel, scratch, count, whole)


def chosen_place(owners, mine, chip):
    chosen = (mine == owners[0][1]) & (chip == owners[0][0])
    for row, place in owners[1:]:
        chosen = chosen | ((mine == place) & (chip == row))
    return chosen


def orthogonal(whole, owners, method, mine, chip, count):
    half, width = whole.shape[2:]
    return lax.cond(
        chosen_place(owners, mine, chip),
        partial(method, count),
        lambda one: jnp.zeros((count, half, width), LOW),
        whole,
    )


def on_device(
    inputs,
    cotangent,
    lengths,
    mixer_weight,
    strength_weight,
    filter_weight,
    norm_gain,
    head_gain,
    output_weight,
    gate_up_weight,
    down_weight,
    mixer_moment,
    strength_moment,
    filter_moment,
    gain_moment,
    head_gain_moment,
    output_moment,
    gate_up_moment,
    down_moment,
):
    seq_count = lax.axis_size("seq")
    seq_index = lax.axis_index("seq")
    fsdp_count = lax.axis_size("fsdp")
    fsdp_index = lax.axis_index("fsdp")
    row_count, width = inputs.shape
    shard = width // fsdp_count
    heads_all = strength_weight.shape[1]

    wide_ff = tile_count(gate_up_weight.shape[2], seq_count) * HD
    core = seq_index % 2
    half = shard // 2
    groups = heads_all // GROUP
    span = GROUP * HD
    small_count = heads_all + 3 * CONV + 3
    top_near = core_swapped(cotangent)
    top_far = [chip_shifted(cotangent, k) for k in range(1, seq_count // 2)]
    square_own, ff_own, small_own = prepared(
        mixer_weight, output_weight, gate_up_weight, down_weight, strength_weight, filter_weight, norm_gain, head_gain,
        seq_count,
    )
    square_full, small_full = gathered_mixer(square_own, small_own, seq_count, fsdp_count)
    by_place = small_full.reshape(-1, fsdp_count, 128)
    small_wide = small_full if shard == 128 else by_place[:, :, :shard].reshape(-1, width)
    strength_full = small_wide[:heads_all]
    filters_wide = small_wide[heads_all : heads_all + 3 * CONV].reshape(3, CONV, width).astype(FULL)
    gains_wide = small_wide[heads_all + 3 * CONV : heads_all + 3 * CONV + 2].astype(FULL)
    head_part = head_gain.shape[0]
    head_gain_full = by_place[small_count - 1, :, :head_part].reshape(1, HD).astype(FULL)

    square_full, ff_own, top_near, top_far = lax.optimization_barrier((square_full, ff_own, top_near, top_far))
    top_parts = [cotangent, top_near] + [part for one in top_far for part in (one, core_swapped(one))]
    ff_full = lax.all_gather(ff_own, "fsdp", axis=0, tiled=True)
    mixer_full, output_full = square_full[:, : 3 * width], square_full[:, 3 * width :]
    ff_parts = [ff_full[:, j * wide_ff : (j + 1) * wide_ff] for j in range(3)]

    my_lengths = lax.dynamic_slice_in_dim(lengths, fsdp_index, 1, 0)[0]
    doc_ends = jnp.cumsum(my_lengths)

    def passed_docs(at):
        return (at[:, None] >= doc_ends[None, :]).astype(jnp.int32)

    own = seq_index * row_count + jnp.arange(row_count, dtype=jnp.int32)
    passed = passed_docs(own)
    segment = jnp.sum(passed, axis=1)
    doc_first = jnp.sum(passed * my_lengths[None, :], axis=1)
    block_start = own.reshape(-1, BLOCK)[:, 0]
    before = jnp.where(block_start == 0, -1, jnp.sum(passed_docs(block_start - 1), axis=1))
    blocked = segment.reshape(-1, BLOCK)
    carried = (blocked == before[:, None]).reshape(-1)
    trailing = (blocked == blocked[:, -1:]).reshape(-1)
    columns = [own - lag >= doc_first for lag in range(CONV)] + [carried, trailing, segment]
    meta = jnp.stack([one.astype(FULL) for one in columns] + [jnp.zeros((row_count,), FULL)], axis=1)
    meta_row = jnp.broadcast_to(segment.astype(FULL)[None, :], (8, row_count))

    residual_in = inputs.astype(FULL)
    scale_one = lax.rsqrt(jnp.mean(residual_in * residual_in, axis=-1, keepdims=True) + norm_eps)
    unit_one = residual_in * scale_one
    normed_low = (unit_one * gains_wide[0]).astype(LOW)
    projected = low_dot(normed_low, mixer_full, (1, 0)).astype(LOW)
    logits = low_dot(normed_low, strength_full, (1, 1))
    strength = jax.nn.sigmoid(logits).astype(LOW).astype(FULL)
    forth = [(i, i + 1) for i in range(seq_count - 1)]
    rim = lax.ppermute(projected[row_count - RIM :], "seq", forth)
    mixed, solve, weight, update, drift, local_out, effective, states, end, transfer = forward_blocks(
        projected, rim, filters_wide, strength, meta, meta_row
    )
    enter = exchanged(end, transfer, False, 4)
    delta_out, head_normed = head_outputs(local_out, effective, enter, head_gain_full)
    residual = residual_in + low_dot(head_normed, output_full, (1, 0))
    scale_two = lax.rsqrt(jnp.mean(residual * residual, axis=-1, keepdims=True) + norm_eps)
    unit_two = residual * scale_two
    normed_two = (unit_two * gains_wide[1]).astype(LOW)
    gate_full, up_full, down_full = ff_parts
    chips = seq_count // 2
    near_norm = jnp.concatenate([normed_two, core_swapped(normed_two)])
    far_straight = [chip_shifted(normed_two, k) for k in range(1, chips)]

    def spread_out(normed_part, top_part):
        gate = low_dot(normed_part, gate_full, (1, 0))
        up = low_dot(normed_part, up_full, (1, 0))
        gate_sigmoid = jax.nn.sigmoid(gate)
        gate_silu = gate * gate_sigmoid
        hidden = (gate_silu * up).astype(LOW)
        grad_hidden = low_dot(top_part, down_full, (1, 0))
        grad_gate = (grad_hidden * up * (gate_sigmoid * (1.0 + gate * (1.0 - gate_sigmoid)))).astype(LOW)
        grad_up = (grad_hidden * gate_silu).astype(LOW)
        return hidden, grad_gate, grad_up

    def grad_in(values):
        return low_dot(values[1], gate_full, (1, 1)) + low_dot(values[2], up_full, (1, 1))

    def weight_grad(values, normed_part, top_part, which):
        left, right = ((normed_part, values[1]), (normed_part, values[2]), (top_part, values[0]))[which]
        return low_dot(left, right, (0, 0))

    near_top, far_top = jnp.concatenate(top_parts[:2]), jnp.concatenate(top_parts[2:])
    near = spread_out(near_norm, near_top)
    far_straight, near = lax.optimization_barrier((far_straight, near))
    far_parts = [part for one in far_straight for part in (one, core_swapped(one))]
    near_grad = grad_in(near)
    near_back = core_swapped(near_grad[row_count:].astype(LOW))
    near_grad, far_parts = lax.optimization_barrier((near_grad, far_parts))
    far_norm = jnp.concatenate(far_parts)
    far = spread_out(far_norm, far_top)

    def picked(values, side):
        size = 2 * row_count
        return [
            tuple(one[i * size + side * row_count : i * size + (side + 1) * row_count] for one in values)
            for i in range(chips - 1)
        ]

    crossed = [core_swapped(grad_in(one).astype(LOW)) for one in picked(far, 1)]
    joint = [(grad_in(one) + other.astype(FULL)).astype(LOW) for one, other in zip(picked(far, 0), crossed)]
    far, near, joint = lax.optimization_barrier((far, near, joint))
    grad_parts = [chip_shifted(one, -(k + 1)) for k, one in enumerate(joint)]
    near_weights = [weight_grad(near, near_norm, near_top, j) for j in range(3)]
    far_weights = [weight_grad(far, far_norm, far_top, j) for j in range(3)]
    ff_grads = jnp.concatenate([(a + b).astype(LOW) for a, b in zip(near_weights, far_weights)], axis=1)
    ff_part = lax.psum_scatter(ff_grads, "fsdp", scatter_dimension=0, tiled=True)
    done_grads, grad_parts = lax.optimization_barrier((ff_grads, grad_parts))
    grad_normed_two = near_grad[:row_count] + sum(one.astype(FULL) for one in [near_back] + list(grad_parts))
    back_two, grad_gain_two = norm_back(unit_two, scale_two, gains_wide[1], grad_normed_two)
    grad_residual = back_two + cotangent.astype(FULL)
    grad_attention = grad_residual.astype(LOW)
    grad_head_normed = low_dot(grad_attention, output_full, (1, 1)).astype(LOW)

    upstream, adjoint_local, grad_head_gain = head_back(
        grad_head_normed, delta_out, effective, head_gain_full
    )
    leave = exchanged(adjoint_local, transfer, True, 5)
    grad_projected, grad_strength, grad_filter, edge, lead = backward_blocks(
        projected, rim, filters_wide, strength, meta, meta_row, mixed, solve, weight, update, drift,
        upstream, states, enter, leave,
    )
    back = [(i + 1, i) for i in range(seq_count - 1)]
    incoming = lax.ppermute(lead.astype(LOW), "seq", back).astype(FULL)
    grad_projected = lax.dynamic_update_slice(
        grad_projected, (edge + incoming).astype(LOW), (row_count - 8, 0)
    )
    grad_strength = grad_strength.astype(LOW).astype(FULL)
    grad_logits = (grad_strength * strength * (1.0 - strength)).astype(LOW)
    def core_rows(values):
        by_core = values.reshape(row_count, fsdp_count, 2, half)
        return [
            lax.dynamic_slice_in_dim(by_core, at, 1, 2).reshape(row_count, width // 2) for at in (core, 1 - core)
        ]

    grad_mixer = [low_dot(one, grad_projected, (0, 0)) for one in core_rows(normed_low)]
    grad_output = [low_dot(one, grad_attention, (0, 0)) for one in core_rows(head_normed)]
    square_grads = jnp.concatenate(
        [
            (mine + core_swapped(other.astype(LOW)).astype(FULL)).astype(LOW)
            for mine, other in (grad_mixer, grad_output)
        ],
        axis=1,
    )
    near_hidden, far_hidden = near[0], far[0]
    square_grads, ff_part, grad_projected, grad_logits, near_hidden, far_hidden = lax.optimization_barrier(
        (square_grads, ff_part, grad_projected, grad_logits, near_hidden, far_hidden)
    )
    far_out, near_out = low_dot(far_hidden, down_full, (1, 1)), low_dot(near_hidden, down_full, (1, 1))
    out_crossed = [core_swapped(one[0].astype(LOW)) for one in picked((far_out,), 1)]
    out_joint = [(one[0] + other.astype(FULL)).astype(LOW) for one, other in zip(picked((far_out,), 0), out_crossed)]
    out_parts = [chip_shifted(one, -(k + 1)) for k, one in enumerate(out_joint)]
    out_near = near_out[:row_count] + core_swapped(near_out[row_count:].astype(LOW)).astype(FULL)
    square_part = lax.psum_scatter(square_grads, "fsdp", scatter_dimension=0, tiled=True)
    grad_strength_weight = low_dot(grad_logits, normed_low, (0, 0))
    grad_normed = low_dot(grad_logits, strength_full, (1, 0)) + low_dot(grad_projected, mixer_full, (1, 1))
    ff_stack = seq_stacked(ff_part)
    back_one, grad_gain_one = norm_back(unit_one, scale_one, gains_wide[0], grad_normed)
    input_grad = grad_residual + back_one

    head_row = jnp.pad(
        grad_head_gain.reshape(fsdp_count, head_part), ((0, 0), (0, shard - head_part))
    ).reshape(1, width)
    small_grads = jnp.concatenate(
        [
            grad_strength_weight,
            grad_filter.reshape(3 * CONV, width),
            grad_gain_one[None],
            grad_gain_two[None],
            head_row,
            jnp.zeros((-small_count % 8, width), FULL),
        ],
        axis=0,
    )
    small_pieces = small_grads.reshape(-1, fsdp_count, shard).transpose(1, 0, 2)

    ff_stack, input_grad, small_pieces = lax.optimization_barrier((ff_stack, input_grad, small_pieces))
    new_gate_up_moment, new_down_moment, wide_sent = wide_moments(gate_up_moment, down_moment, ff_stack, seq_count)
    owners = tuple(matrix_owners(fsdp_count))
    chip = seq_index // 2
    mixer_prior = lax.dynamic_slice_in_dim(mixer_moment, core * half, half, 1)
    output_prior = lax.dynamic_slice_in_dim(output_moment, core * half, half, 0)
    square_prior = jnp.concatenate(
        [mixer_prior[j, :, g * span : (g + 1) * span] for g in range(groups) for j in range(3)] + [output_prior], axis=1
    )
    block_output = residual + (out_near + sum(one.astype(FULL) for one in out_parts))
    wide_sent, square_prior, block_output = lax.optimization_barrier((wide_sent, square_prior, block_output))
    square_sum, small_own, square_all, wide_all = middle(
        square_part, square_prior, small_pieces, wide_sent, owners, 2, seq_count, fsdp_count
    )
    square_rows = orthogonal(square_all, owners[3:], orth_square, fsdp_index, chip, fsdp_count)
    wide_rows = orthogonal(wide_all, owners[:3], orth_wide, fsdp_index, chip, fsdp_count)
    wide_parts, square_parts = handed_back(wide_rows, square_rows, owners, 3, seq_count, fsdp_count)
    weights = (
        mixer_weight, output_weight, gate_up_weight, down_weight, strength_weight, filter_weight, norm_gain, head_gain
    )
    moments = (mixer_moment, output_moment, strength_moment, filter_moment, gain_moment, head_gain_moment)
    done = finished(
        wide_parts.reshape(3, shard, -1),
        square_parts.reshape(4, shard, width),
        square_sum.reshape(shard, -1),
        small_own,
        weights,
        moments,
    )
    head_pair = [one[0] for one in done[8:10]]
    return (
        (block_output, input_grad)
        + tuple(done[:8])
        + tuple(head_pair)
        + tuple(done[10:12])
        + (new_gate_up_moment, done[12], new_down_moment, done[13])
    )


def solution(mesh):
    return jax.shard_map(
        on_device,
        mesh=mesh,
        in_specs=(
            P(("seq", "fsdp"), None),
            P(("seq", "fsdp"), None),
            P(),
            P(None, "fsdp", None),
            P("fsdp", None),
            P(None, None, "fsdp"),
            P(None, "fsdp"),
            P("fsdp"),
            P("fsdp", None),
            P(None, "fsdp", None),
            P(None, "fsdp"),
            P(None, "fsdp", None),
            P("fsdp", None),
            P(None, None, "fsdp"),
            P(None, "fsdp"),
            P("fsdp"),
            P("fsdp", None),
            P(None, "fsdp", None),
            P(None, "fsdp"),
        ),
        out_specs=(
            P(("seq", "fsdp"), None),
            P(("seq", "fsdp"), None),
            P(None, "fsdp", None),
            P(None, "fsdp", None),
            P("fsdp", None),
            P("fsdp", None),
            P(None, None, "fsdp"),
            P(None, None, "fsdp"),
            P(None, "fsdp"),
            P(None, "fsdp"),
            P("fsdp"),
            P("fsdp"),
            P("fsdp", None),
            P("fsdp", None),
            P(None, "fsdp", None),
            P(None, "fsdp", None),
            P(None, "fsdp"),
            P(None, "fsdp"),
        ),
        check_vma=False,
    )
```

```python
from functools import partial

import jax
import jax.numpy as jnp
from jax import lax
from jax.experimental import pallas as pl
from jax.experimental.pallas import tpu as pltpu
from jax.sharding import PartitionSpec as P

HD = 128
CONV = 4
BLOCK = 128
GROUP = 8
RIM = 16
NS_STEPS = 3

norm_eps = 1e-06
head_eps = 0.001
momentum_decay = 0.9
matrix_rate = 1.0
filter_rate = 0.01
gain_rate = 0.001
strength_rate = 0.001
coef_linear = 3.4445
coef_cubic = -4.775
coef_quintic = 2.0315

LOW = jnp.bfloat16
FULL = jnp.float32


def halves(values):
    top = values.astype(LOW)
    return (top, (values - top.astype(FULL)).astype(LOW))


def product(left, right, dims=(1, 0)):
    left = left if isinstance(left, tuple) else (left,)
    right = right if isinstance(right, tuple) else (right,)
    total = None
    for i, a in enumerate(left):
        for j, b in enumerate(right):
            if i + j < 2:
                term = lax.dot_general(
                    a, b, (((dims[0],), (dims[1],)), ((), ())), preferred_element_type=FULL
                )
                total = term if total is None else total + term
    return total


def low_product(left, right, dims=(1, 0)):
    return product(left.astype(LOW), right.astype(LOW), dims)


def lanes(values, head):
    return values[:, head * HD : (head + 1) * HD]


def unit_scale(values):
    return lax.rsqrt(jnp.sum(values * values, axis=-1, keepdims=True) + norm_eps)


def block_ids():
    rows = lax.broadcasted_iota(jnp.int32, (BLOCK, BLOCK), 0)
    cols = lax.broadcasted_iota(jnp.int32, (BLOCK, BLOCK), 1)
    return rows, cols


def short_conv(current, previous, taps, meta):
    joined = jnp.concatenate([previous, current], axis=0)
    total = None
    shifted = []
    for lag in range(CONV):
        moved = joined if lag == 0 else pltpu.roll(joined, lag, 0)
        moved = moved[RIM:] * meta[:, lag : lag + 1]
        shifted.append(moved)
        term = moved * taps[lag : lag + 1, :]
        total = term if total is None else total + term
    return total, shifted


def inverse(system, differ):
    rows, cols = block_ids()
    eye = jnp.where(rows == cols, 1.0, 0.0).astype(FULL)
    found = [eye - jnp.where((differ >> 0) == 1, one, 0.0) for one in system]
    level = 1
    while (1 << level) < BLOCK:
        picked = [jnp.where((differ >> level) == 1, one, 0.0).astype(LOW) for one in system]
        low = [one.astype(LOW) for one in found]
        inner = [product(a, b).astype(LOW) for a, b in zip(picked, low)]
        outer = [product(b, a) for a, b in zip(inner, low)]
        found = [a - b for a, b in zip(found, outer)]
        level += 1
    split = [halves(one) for one in found]
    wide = [halves(one) for one in system]
    error = [eye - a - product(b, c) for a, b, c in zip(found, wide, split)]
    return [a + product(b[0], c.astype(LOW)) for a, b, c in zip(found, split, error)]


def forward_kernel(
    proj_ref, prev_ref, rim_ref, taps_ref, strength_ref, strength_row_ref, meta_ref, meta_row_ref,
    mixed_ref, solve_ref, weight_ref, update_ref, drift_ref, out_ref, query_ref, state_ref, end_ref, transfer_ref,
    carry_ref,
):
    step = pl.program_id(1)
    rows, cols = block_ids()
    meta = meta_ref[...]
    carry, tail, segment = meta[:, 4:5], meta[:, 5:6], meta[:, 6:7]
    same = segment == meta_row_ref[0:1, :]
    strict = (rows > cols) & same
    inclusive = (rows >= cols) & same
    differ = rows ^ cols
    carry_last = carry[BLOCK - 1 : BLOCK, :]

    @pl.when(step == 0)
    def _():
        start = jnp.concatenate(
            [jnp.zeros((HD, HD), FULL), jnp.where(rows == cols, 1.0, 0.0).astype(FULL)], axis=1
        )
        for head in range(GROUP):
            carry_ref[head] = start

    first = step == 0
    parts = []
    for j in range(3):
        at = slice(j * GROUP * HD, (j + 1) * GROUP * HD)
        previous = jnp.where(first, rim_ref[:, at].astype(FULL), prev_ref[:, at].astype(FULL))
        conv, _ = short_conv(proj_ref[:, at].astype(FULL), previous, taps_ref[j], meta)
        parts.append(conv * jax.nn.sigmoid(conv))
    queries, keys, values = [], [], []
    for head in range(GROUP):
        query, key = lanes(parts[0], head), lanes(parts[1], head)
        queries.append((query * (unit_scale(query) * HD ** (-0.5))).astype(LOW))
        keys.append((key * unit_scale(key)).astype(LOW))
        values.append(lanes(parts[2], head).astype(LOW))
        mixed_ref[0, :, head * HD : (head + 1) * HD] = queries[head]
        mixed_ref[1, :, head * HD : (head + 1) * HD] = keys[head]
        mixed_ref[2, :, head * HD : (head + 1) * HD] = values[head]
    strength = strength_ref[0]
    strength_row = strength_row_ref[0]
    heads = range(GROUP)
    gram = [product(keys[h], keys[h], (1, 1)) for h in heads]
    system = [jnp.where(strict, strength[:, h : h + 1] * gram[h], 0.0) for h in heads]
    scores = [jnp.where(inclusive, product(queries[h], keys[h], (1, 1)), 0.0) for h in heads]
    solve = inverse(system, differ)
    carry_low, tail_low = carry.astype(LOW), tail.astype(LOW)
    carried_query = [queries[h] * carry_low for h in heads]
    tail_key = [keys[h] * tail_low for h in heads]
    right = [jnp.concatenate([values[h], keys[h] * carry_low], axis=1) for h in heads]
    solved = [product(halves(solve[h] * strength_row[h : h + 1, :]), right[h]) for h in heads]
    state = [carry_ref[h] for h in heads]
    state_parts = [halves(state[h]) for h in heads]
    passed = [product(halves(solved[h][:, HD:]), state_parts[h]) for h in heads]
    zero = jnp.zeros((BLOCK, HD), FULL)
    both = [
        jnp.concatenate([solved[h][:, :HD], zero], axis=1) - passed[h] for h in heads
    ]
    both_parts = [halves(both[h]) for h in heads]
    result = [
        product(carried_query[h], state_parts[h]) + product(halves(scores[h]), both_parts[h])
        for h in heads
    ]
    after = [
        carry_last * state[h] + product(tail_key[h], both_parts[h], (0, 0)) for h in heads
    ]
    for h in heads:
        solve_ref[0, h] = solve[h].astype(LOW)
        at = slice(h * HD, (h + 1) * HD)
        weight_ref[:, at] = solved[h][:, HD:].astype(LOW)
        update_ref[:, at] = both[h][:, :HD]
        drift_ref[:, at] = both[h][:, HD:].astype(LOW)
        out_ref[:, at] = result[h][:, :HD]
        query_ref[:, at] = result[h][:, HD:]
        state_ref[0, h] = state[h]
        carry_ref[h] = after[h]
        end_ref[h] = after[h][:, :HD]
        transfer_ref[h] = after[h][:, HD:]


def forward_blocks(projected, rim, taps, strength, meta, meta_row):
    total = projected.shape[0]
    width = projected.shape[1] // 3
    head_count = width // HD
    groups, steps = head_count // GROUP, total // BLOCK
    span = GROUP * HD
    grouped = strength.reshape(total, groups, GROUP)
    strength_col = grouped.transpose(1, 0, 2)
    strength_row = grouped.transpose(1, 2, 0)
    rows_of = lambda g, n: (n, g)
    shapes = (
        jax.ShapeDtypeStruct((3, total, width), LOW),
        jax.ShapeDtypeStruct((steps, head_count, BLOCK, BLOCK), LOW),
        jax.ShapeDtypeStruct((total, width), LOW),
        jax.ShapeDtypeStruct((total, width), FULL),
        jax.ShapeDtypeStruct((total, width), LOW),
        jax.ShapeDtypeStruct((total, width), FULL),
        jax.ShapeDtypeStruct((total, width), FULL),
        jax.ShapeDtypeStruct((steps, head_count, HD, 2 * HD), FULL),
        jax.ShapeDtypeStruct((head_count, HD, HD), FULL),
        jax.ShapeDtypeStruct((head_count, HD, HD), FULL),
    )
    wide = pl.BlockSpec((BLOCK, span), rows_of)
    ratio = BLOCK // RIM
    return pl.pallas_call(
        forward_kernel,
        grid=(groups, steps),
        in_specs=[
            pl.BlockSpec((BLOCK, 3 * span), rows_of),
            pl.BlockSpec((RIM, 3 * span), lambda g, n: (jnp.maximum(n * ratio - 1, 0), g)),
            pl.BlockSpec((RIM, 3 * span), lambda g, n: (0, g)),
            pl.BlockSpec((3, CONV, span), lambda g, n: (0, 0, g)),
            pl.BlockSpec((1, BLOCK, GROUP), lambda g, n: (g, n, 0)),
            pl.BlockSpec((1, GROUP, BLOCK), lambda g, n: (g, 0, n)),
            pl.BlockSpec((BLOCK, 8), lambda g, n: (n, 0)),
            pl.BlockSpec((8, BLOCK), lambda g, n: (0, n)),
        ],
        out_specs=(
            pl.BlockSpec((3, BLOCK, span), lambda g, n: (0, n, g)),
            pl.BlockSpec((1, GROUP, BLOCK, BLOCK), lambda g, n: (n, g, 0, 0)),
            wide,
            wide,
            wide,
            wide,
            wide,
            pl.BlockSpec((1, GROUP, HD, 2 * HD), lambda g, n: (n, g, 0, 0)),
            pl.BlockSpec((GROUP, HD, HD), lambda g, n: (g, 0, 0)),
            pl.BlockSpec((GROUP, HD, HD), lambda g, n: (g, 0, 0)),
        ),
        out_shape=shapes,
        scratch_shapes=[pltpu.VMEM((GROUP, HD, 2 * HD), FULL)],
        compiler_params=pltpu.CompilerParams(vmem_limit_bytes=48 << 20),
        cost_estimate=pl.CostEstimate(flops=8 << 30, bytes_accessed=24 << 20, transcendentals=0),
    )(projected, projected, rim, taps, strength_col, strength_row, meta, meta_row)


def out_kernel(local_ref, query_ref, state_ref, gain_ref, delta_ref, normed_ref):
    gain = gain_ref[0:1, :]
    for head in range(local_ref.shape[1] // HD):
        at = slice(head * HD, (head + 1) * HD)
        value = local_ref[:, at] + product(halves(query_ref[:, at]), halves(state_ref[head]))
        delta_ref[:, at] = value
        scale = lax.rsqrt(jnp.mean(value * value, axis=-1, keepdims=True) + head_eps)
        normed_ref[:, at] = (value * scale * gain).astype(LOW)


def head_outputs(local_out, effective, state_in, gain):
    total, width = local_out.shape
    rows = pl.BlockSpec((BLOCK, width), lambda n: (n, 0))
    return pl.pallas_call(
        out_kernel,
        grid=(total // BLOCK,),
        in_specs=[
            rows,
            rows,
            pl.BlockSpec(state_in.shape, lambda n: (0, 0, 0)),
            pl.BlockSpec((1, HD), lambda n: (0, 0)),
        ],
        out_specs=(rows, rows),
        out_shape=(
            jax.ShapeDtypeStruct((total, width), FULL),
            jax.ShapeDtypeStruct((total, width), LOW),
        ),
        compiler_params=pltpu.CompilerParams(vmem_limit_bytes=32 << 20),
    )(local_out, effective, state_in, gain)


def head_back_kernel(grad_ref, delta_ref, query_ref, gain_ref, upstream_ref, adjoint_ref, gain_grad_ref):
    step = pl.program_id(0)
    gain = gain_ref[0:1, :]

    @pl.when(step == 0)
    def _():
        adjoint_ref[...] = jnp.zeros_like(adjoint_ref)
        gain_grad_ref[...] = jnp.zeros_like(gain_grad_ref)

    gained = jnp.zeros((1, HD), FULL)
    for head in range(grad_ref.shape[1] // HD):
        at = slice(head * HD, (head + 1) * HD)
        value = delta_ref[:, at]
        grad = grad_ref[:, at].astype(FULL)
        scale = lax.rsqrt(jnp.mean(value * value, axis=-1, keepdims=True) + head_eps)
        unit = value * scale
        gained = gained + jnp.sum(grad * unit, axis=0, keepdims=True)
        grad = grad * gain
        back = scale * (grad - unit * jnp.mean(grad * unit, axis=-1, keepdims=True))
        low = back.astype(LOW)
        upstream_ref[:, at] = low
        adjoint_ref[head] += product(query_ref[:, at].astype(LOW), low, (0, 0))
    gain_grad_ref[...] += gained


def head_back(grad_normed, delta_out, effective, gain):
    total, width = delta_out.shape
    head_count = width // HD
    rows = pl.BlockSpec((BLOCK, width), lambda n: (n, 0))
    return pl.pallas_call(
        head_back_kernel,
        grid=(total // BLOCK,),
        in_specs=[rows, rows, rows, pl.BlockSpec((1, HD), lambda n: (0, 0))],
        out_specs=(
            rows,
            pl.BlockSpec((head_count, HD, HD), lambda n: (0, 0, 0)),
            pl.BlockSpec((1, HD), lambda n: (0, 0)),
        ),
        out_shape=(
            jax.ShapeDtypeStruct((total, width), LOW),
            jax.ShapeDtypeStruct((head_count, HD, HD), FULL),
            jax.ShapeDtypeStruct((1, HD), FULL),
        ),
        compiler_params=pltpu.CompilerParams(vmem_limit_bytes=32 << 20),
    )(grad_normed, delta_out, effective, gain)


def backward_kernel(
    proj_ref, prev_ref, rim_ref, taps_ref, strength_ref, meta_ref, meta_row_ref,
    mixed_ref, solve_ref, weight_ref, update_ref, drift_ref, upstream_ref, state_ref, enter_ref, leave_ref,
    grad_ref, strength_grad_ref, taps_grad_ref, edge_ref, lead_ref,
    adjoint_ref, spill_ref,
):
    turn = pl.program_id(1)
    last_turn = pl.num_programs(1) - 1
    rows, cols = block_ids()
    meta = meta_ref[...]
    carry, tail, segment = meta[:, 4:5], meta[:, 5:6], meta[:, 6:7]
    same = segment == meta_row_ref[0:1, :]
    strict = (rows > cols) & same
    inclusive = (rows >= cols) & same
    carry_last = carry[BLOCK - 1 : BLOCK, :]
    carry_low, tail_low = carry.astype(LOW), tail.astype(LOW)
    heads = range(GROUP)

    @pl.when(turn == 0)
    def _():
        for h in heads:
            adjoint_ref[h] = leave_ref[h]
        spill_ref[...] = jnp.zeros_like(spill_ref)
        taps_grad_ref[...] = jnp.zeros_like(taps_grad_ref)

    strength = strength_ref[0]
    at = [slice(h * HD, (h + 1) * HD) for h in heads]
    query = [mixed_ref[0, :, at[h]] for h in heads]
    key = [mixed_ref[1, :, at[h]] for h in heads]
    value = [mixed_ref[2, :, at[h]] for h in heads]
    upstream = [upstream_ref[:, at[h]] for h in heads]
    enter = [enter_ref[h].astype(LOW) for h in heads]
    state = [
        (state_ref[0, h, :, :HD] + product(state_ref[0, h, :, HD:].astype(LOW), enter[h])).astype(LOW)
        for h in heads
    ]
    update = [
        (update_ref[:, at[h]] + product(drift_ref[:, at[h]], enter[h])).astype(LOW) for h in heads
    ]
    gram = [product(key[h], key[h], (1, 1)) for h in heads]
    scores = [
        jnp.where(inclusive, product(query[h], key[h], (1, 1)), 0.0).astype(LOW) for h in heads
    ]
    tail_key = [key[h] * tail_low for h in heads]
    adjoint = [adjoint_ref[h] for h in heads]
    adjoint_low = [adjoint[h].astype(LOW) for h in heads]
    grad_update = [
        (product(scores[h], upstream[h], (0, 0)) + product(tail_key[h], adjoint_low[h])).astype(LOW)
        for h in heads
    ]
    for h in heads:
        adjoint_ref[h] = (
            carry_last * adjoint[h]
            + product(query[h] * carry_low, upstream[h], (0, 0))
            - product(weight_ref[:, at[h]], grad_update[h], (0, 0))
        )
    grad_right = [product(solve_ref[0, h], grad_update[h], (0, 0)) for h in heads]
    right_low = [grad_right[h].astype(LOW) for h in heads]
    grad_scores = [
        jnp.where(inclusive, product(upstream[h], update[h], (1, 1)), 0.0).astype(LOW) for h in heads
    ]
    grad_query = [
        carry * product(upstream[h], state[h], (1, 1)) + product(grad_scores[h], key[h]) for h in heads
    ]
    right_state = [product(right_low[h], state[h], (1, 1)) for h in heads]
    grad_system = [
        jnp.where(strict, -product(right_low[h], update[h], (1, 1)), 0.0) for h in heads
    ]
    beta = [strength[:, h : h + 1] for h in heads]
    grad_gram = [(beta[h] * grad_system[h]).astype(LOW) for h in heads]
    grad_key = [
        product(grad_scores[h], query[h], (0, 0))
        + tail * product(update[h], adjoint_low[h], (1, 1))
        - (beta[h] * carry) * right_state[h]
        + product(grad_gram[h], key[h])
        + product(grad_gram[h], key[h], (0, 0))
        for h in heads
    ]
    grad_value = [beta[h] * grad_right[h] for h in heads]
    columns = [
        jnp.sum(
            grad_right[h] * value[h].astype(FULL)
            - carry * right_state[h] * key[h].astype(FULL)
            + grad_system[h] * gram[h],
            axis=-1,
            keepdims=True,
        )
        for h in heads
    ]
    strength_grad_ref[0] = jnp.concatenate(columns, axis=1)

    def rounded(values):
        return values.astype(LOW).astype(FULL)

    first = turn == last_turn
    grads = (grad_query, grad_key, grad_value)
    span = GROUP * HD
    for j in range(3):
        at = slice(j * span, (j + 1) * span)
        previous = jnp.where(first, rim_ref[:, at].astype(FULL), prev_ref[:, at].astype(FULL))
        taps = taps_ref[j]
        conv, shifted = short_conv(proj_ref[:, at].astype(FULL), previous, taps, meta)
        gate = jax.nn.sigmoid(conv)
        active = conv * gate
        pieces = []
        for h in heads:
            grad = rounded(grads[j][h])
            if j < 2:
                raw = lanes(active, h)
                scale = unit_scale(raw)
                unit = raw * scale
                if j == 0:
                    grad = grad * HD ** (-0.5)
                grad = scale * (grad - unit * jnp.sum(unit * grad, axis=-1, keepdims=True))
            pieces.append(grad)
        grad_conv = jnp.concatenate(pieces, axis=1) * (gate * (1.0 + conv * (1.0 - gate)))
        total = None
        for lag in range(CONV):
            taps_grad_ref[j, lag : lag + 1, :] += jnp.sum(grad_conv * shifted[lag], axis=0, keepdims=True)
            spread = grad_conv * (meta[:, lag : lag + 1] * taps[lag : lag + 1, :])
            spread = jnp.concatenate([jnp.zeros((8, span), FULL), spread], axis=0)
            if lag:
                spread = pltpu.roll(spread, BLOCK + 8 - lag, 0)
            total = spread if total is None else total + spread
        bottom = total[BLOCK:] + spill_ref[j]
        spill_ref[j] = total[:8]
        grad_ref[:, at] = jnp.concatenate([total[8:BLOCK], bottom], axis=0).astype(LOW)

        @pl.when(turn == 0)
        def _():
            edge_ref[:, at] = bottom

        lead_ref[:, at] = total[:8]


def backward_blocks(
    projected, rim, taps, strength, meta, meta_row, mixed, solve, weight, update, drift, upstream,
    states, enter, leave,
):
    total, width = projected.shape[0], projected.shape[1] // 3
    head_count = width // HD
    groups, steps = head_count // GROUP, total // BLOCK
    span = GROUP * HD
    strength_col = strength.reshape(total, groups, GROUP).transpose(1, 0, 2)
    ratio = BLOCK // RIM
    back = lambda n: steps - 1 - n
    wide = pl.BlockSpec((BLOCK, span), lambda g, n: (back(n), g))
    deep = pl.BlockSpec((3, BLOCK, span), lambda g, n: (0, back(n), g))
    per_group = pl.BlockSpec((GROUP, HD, HD), lambda g, n: (g, 0, 0))
    flat = pl.BlockSpec((BLOCK, 3 * span), lambda g, n: (back(n), g))
    narrow = pl.BlockSpec((8, 3 * span), lambda g, n: (0, g))
    grads, strength_grad, taps_grad, edge, lead = pl.pallas_call(
        backward_kernel,
        grid=(groups, steps),
        in_specs=[
            flat,
            pl.BlockSpec((RIM, 3 * span), lambda g, n: (jnp.maximum(back(n) * ratio - 1, 0), g)),
            pl.BlockSpec((RIM, 3 * span), lambda g, n: (0, g)),
            pl.BlockSpec((3, CONV, span), lambda g, n: (0, 0, g)),
            pl.BlockSpec((1, BLOCK, GROUP), lambda g, n: (g, back(n), 0)),
            pl.BlockSpec((BLOCK, 8), lambda g, n: (back(n), 0)),
            pl.BlockSpec((8, BLOCK), lambda g, n: (0, back(n))),
            deep,
            pl.BlockSpec((1, GROUP, BLOCK, BLOCK), lambda g, n: (back(n), g, 0, 0)),
            wide,
            wide,
            wide,
            wide,
            pl.BlockSpec((1, GROUP, HD, 2 * HD), lambda g, n: (back(n), g, 0, 0)),
            per_group,
            per_group,
        ],
        out_specs=(
            flat,
            pl.BlockSpec((1, BLOCK, GROUP), lambda g, n: (g, back(n), 0)),
            pl.BlockSpec((3, CONV, span), lambda g, n: (0, 0, g)),
            narrow,
            narrow,
        ),
        out_shape=(
            jax.ShapeDtypeStruct((total, 3 * width), LOW),
            jax.ShapeDtypeStruct((groups, total, GROUP), FULL),
            jax.ShapeDtypeStruct((3, CONV, width), FULL),
            jax.ShapeDtypeStruct((8, 3 * width), FULL),
            jax.ShapeDtypeStruct((8, 3 * width), FULL),
        ),
        scratch_shapes=[pltpu.VMEM((GROUP, HD, HD), FULL), pltpu.VMEM((3, 8, span), FULL)],
        compiler_params=pltpu.CompilerParams(vmem_limit_bytes=48 << 20),
        cost_estimate=pl.CostEstimate(flops=4 << 30, bytes_accessed=24 << 20, transcendentals=0),
    )(
        projected, projected, rim, taps, strength_col, meta, meta_row, mixed, solve, weight, update,
        drift, upstream, states, enter, leave,
    )
    return grads, strength_grad.transpose(1, 0, 2).reshape(total, head_count), taps_grad, edge, lead


def fsdp_split(count):
    along = 4 if count % 4 == 0 else 1
    return along, count // along


def gather_kernel(along, across, seq_count, shard_ref, small_ref, full_ref, small_full_ref, local_sem, small_send,
                  small_recv, z_send, z_recv, x_send, x_recv, core_send, core_recv):
    count = along * across
    seq, mine = lax.axis_index("seq"), lax.axis_index("fsdp")
    core, z, x = lax.rem(seq, 2), lax.div(mine, across), lax.rem(mine, across)
    partner = seq + 1 - 2 * core
    rows = shard_ref.shape[0]
    half = rows // 2
    mesh_id = pl.DeviceIdType.MESH

    barrier = pltpu.get_barrier_semaphore()
    for d in range(1, count):
        pl.semaphore_signal(barrier, inc=1, device_id=(seq, lax.rem(mine + d, count)), device_id_type=mesh_id)
    pl.semaphore_signal(barrier, inc=1, device_id=(partner, mine), device_id_type=mesh_id)
    pl.semaphore_wait(barrier, count)

    def place(k, j):
        owner = lax.rem(z - k + along, along) * across + lax.rem(x - j + across, across)
        start = pl.multiple_of(owner * rows + core * half, 16)
        return full_ref.at[pl.ds(start, half), :]

    own_half = shard_ref.at[pl.ds(pl.multiple_of(core * half, 16), half), :]
    keep = pltpu.make_async_copy(
        shard_ref, full_ref.at[pl.ds(pl.multiple_of(mine * rows, 16), rows), :], local_sem.at[0]
    )
    keep.start()
    small_place = small_full_ref.at[:, pl.ds(pl.multiple_of(mine * 128, 128), 128)]
    keep_small = pltpu.make_async_copy(small_ref, small_place, local_sem.at[1])
    keep_small.start()

    def sent(source, target, send, recv, device):
        copy = pltpu.make_async_remote_copy(
            src_ref=source, dst_ref=target, send_sem=send, recv_sem=recv, device_id=device, device_id_type=mesh_id
        )
        copy.start()
        return copy

    def along_z(k):
        source = own_half if k == 1 else place(k - 1, 0)
        device = (seq, lax.rem(z + 1, along) * across + x)
        return sent(source, place(k - 1, 0), z_send.at[k - 1], z_recv.at[k - 1], device)

    def along_x(k, j):
        source = own_half if k == 0 else place(k, 0)
        at = k * (across - 1) + j - 1
        device = (seq, z * across + lax.rem(x + j, across))
        return sent(source, place(k, 0), x_send.at[at], x_recv.at[at], device)

    def to_core(k, j):
        at = k * across + j
        return sent(place(k, j), place(k, j), core_send.at[at], core_recv.at[at], (partner, mine))

    copies = []
    z_copies = {1: along_z(1)} if along > 1 else {}
    x_copies = {}
    for j in range(1, across):
        x_copies[0, j] = along_x(0, j)
    for d in range(1, count):
        copies.append(
            sent(small_ref, small_place, small_send.at[d - 1], small_recv.at[d - 1],
                 (seq, lax.rem(mine + d, count)))
        )
    core_copies = []
    for k in range(1, along):
        z_copies[k].wait_recv()
        if k + 1 < along:
            z_copies[k + 1] = along_z(k + 1)
        for j in range(1, across):
            x_copies[k, j] = along_x(k, j)
        core_copies.append(to_core(k, 0))
        for j in range(1, across):
            x_copies[k - 1, j].wait_recv()
            core_copies.append(to_core(k - 1, j))
    for j in range(1, across):
        x_copies[along - 1, j].wait_recv()
        core_copies.append(to_core(along - 1, j))
    keep.wait()
    keep_small.wait()
    for copy in list(z_copies.values()) + list(x_copies.values()):
        copy.wait_send()
    for copy in copies + core_copies:
        copy.wait()


def gathered_mixer(shard, small, seq_count, fsdp_count):
    along, across = fsdp_split(fsdp_count)
    rows, width = shard.shape
    dma = pltpu.SemaphoreType.DMA
    hold = pl.BlockSpec(memory_space=pl.ANY)
    links = max(along * (across - 1), 1)
    return pl.pallas_call(
        partial(gather_kernel, along, across, seq_count),
        in_specs=[hold, hold],
        out_specs=(hold, hold),
        out_shape=(
            jax.ShapeDtypeStruct((rows * fsdp_count, width), shard.dtype),
            jax.ShapeDtypeStruct((small.shape[0], fsdp_count * 128), small.dtype),
        ),
        scratch_shapes=[
            dma((2,)),
            dma((fsdp_count - 1,)),
            dma((fsdp_count - 1,)),
            dma((along,)),
            dma((along,)),
            dma((links,)),
            dma((links,)),
            dma((along * across,)),
            dma((along * across,)),
        ],
        compiler_params=pltpu.CompilerParams(collective_id=0, has_side_effects=True),
    )(shard, small)


def core_swapped(value):
    count = lax.axis_size("seq")
    return lax.ppermute(value, "seq", [(i, i + 1 - 2 * (i % 2)) for i in range(count)])


def chip_shifted(value, by):
    count = lax.axis_size("seq")
    return lax.ppermute(value, "seq", [(i, (i + 2 * by) % count) for i in range(count)])


def seq_blocks(value):
    chips = lax.axis_size("seq") // 2
    far = [chip_shifted(value, k) for k in range(1, chips)]
    found = []
    for one in [value] + far:
        found += [one, core_swapped(one)]
    return found


def seq_stacked(value):
    count, index = lax.axis_size("seq"), lax.axis_index("seq")
    core = index % 2
    result = jnp.zeros((count,) + value.shape, value.dtype)
    for place, one in enumerate(seq_blocks(value)):
        chip = (index // 2 - place // 2) % (count // 2)
        at = chip * 2 + (core if place % 2 == 0 else 1 - core)
        result = lax.dynamic_update_slice_in_dim(result, one[None], at, 0)
    return result


def low_dot(left, right, dims):
    return lax.dot_general(left, right, (((dims[0],), (dims[1],)), ((), ())), preferred_element_type=FULL)


def exchange_kernel(backward, seq_count, local_ref, transfer_ref, result_ref, local_low, transfer_low, other_local,
                    other_transfer, chip_ref, sent_ref,
                    swap_send, swap_recv, chip_send, chip_recv, half_send, half_recv):
    seq, mine = lax.axis_index("seq"), lax.axis_index("fsdp")
    core, chip = lax.rem(seq, 2), lax.div(seq, 2)
    partner = seq + 1 - 2 * core
    chips = seq_count // 2
    heads = local_ref.shape[0]
    mesh_id = pl.DeviceIdType.MESH
    lead = core == (1 if backward else 0)
    dims = (0, 0) if backward else (1, 0)
    step = -1 if backward else 1

    for head in range(heads):
        chip_ref[head] = jnp.zeros((HD, HD), LOW)
        local_low[head] = local_ref[head].astype(LOW)
        transfer_low[head] = transfer_ref[head].astype(LOW)
    barrier = pltpu.get_barrier_semaphore()
    pl.semaphore_signal(barrier, inc=1, device_id=(partner, mine), device_id_type=mesh_id)
    for k in range(1, chips):
        other = lax.rem(seq + 2 * k, seq_count)
        pl.semaphore_signal(barrier, inc=1, device_id=(other, mine), device_id_type=mesh_id)
    pl.semaphore_wait(barrier, chips)

    swaps = [
        pltpu.make_async_remote_copy(
            src_ref=source, dst_ref=target, send_sem=swap_send.at[i], recv_sem=swap_recv.at[i],
            device_id=(partner, mine), device_id_type=mesh_id,
        )
        for i, (source, target) in enumerate(((local_low, other_local), (transfer_low, other_transfer)))
    ]
    for swap in swaps:
        swap.start()
    for swap in swaps:
        swap.wait()
    share = pl.ds(pl.multiple_of(core * (heads // 2), heads // 2), heads // 2)

    def applied(matrix, value):
        return product(matrix, value.astype(LOW), dims)

    def by_role(head):
        own_local, own_transfer = local_ref[head], transfer_low[head]
        far_local, far_transfer = other_local[head].astype(FULL), other_transfer[head]
        return (
            jnp.where(lead, own_local, far_local),
            jnp.where(lead, own_transfer, far_transfer),
            jnp.where(lead, far_local, own_local),
            jnp.where(lead, far_transfer, own_transfer),
        )

    for i in range(chips - 1):
        source = chips - 1 - i if backward else i

        @pl.when(chip == source)
        def _():
            for head in range(heads):
                lead_local, lead_transfer, trail_local, trail_transfer = by_role(head)
                inner = lead_local if i == 0 else lead_local + applied(lead_transfer, chip_ref[head])
                sent_ref[head] = (trail_local + applied(trail_transfer, inner)).astype(LOW)

        onward = pltpu.make_async_remote_copy(
            src_ref=sent_ref.at[share], dst_ref=chip_ref.at[share], send_sem=chip_send.at[i], recv_sem=chip_recv.at[i],
            device_id=(lax.rem(seq + 2 * step + seq_count, seq_count), mine), device_id_type=mesh_id,
        )
        half = pltpu.make_async_remote_copy(
            src_ref=chip_ref.at[share], dst_ref=chip_ref.at[share], send_sem=half_send.at[i], recv_sem=half_recv.at[i],
            device_id=(partner, mine), device_id_type=mesh_id,
        )

        @pl.when(chip == source)
        def _():
            onward.start()
            onward.wait_send()

        @pl.when(chip == source + step)
        def _():
            onward.wait_recv()
            half.start()
            half.wait()

    for head in range(heads):
        lead_local, lead_transfer, _, _ = by_role(head)
        state = chip_ref[head]
        result_ref[head] = jnp.where(lead, state.astype(FULL), lead_local + applied(lead_transfer, state))


def exchanged(local, transfer, backward, call_id):
    seq_count = lax.axis_size("seq")
    dma = pltpu.SemaphoreType.DMA
    vmem = pl.BlockSpec(memory_space=pltpu.VMEM)
    hops = max(seq_count // 2 - 1, 1)
    return pl.pallas_call(
        partial(exchange_kernel, backward, seq_count),
        in_specs=[vmem, vmem],
        out_specs=vmem,
        out_shape=jax.ShapeDtypeStruct(local.shape, FULL),
        scratch_shapes=[pltpu.VMEM(local.shape, LOW)] * 6 + [dma((2,))] * 2 + [dma((hops,))] * 4,
        compiler_params=pltpu.CompilerParams(collective_id=call_id, has_side_effects=True, vmem_limit_bytes=24 << 20),
    )(local, transfer)


def norm_back(unit, scale, gain, grad):
    gained = jnp.sum(grad * unit, axis=0)
    grad = grad * gain
    return scale * (grad - unit * jnp.mean(grad * unit, axis=-1, keepdims=True)), gained


def matrix_owners(fsdp_count):
    along, across = fsdp_split(fsdp_count)
    if along == 4 and across > 1:
        first, second = across, 2 * across + 1
        return [(0, first), (0, second), (1, first), (1, second), (1, first + 1), (0, first + 1), (1, second - 1)]
    return [(m % 2, m * fsdp_count // 7) for m in range(7)]


def remote(source, target, send, recv, device):
    return pltpu.make_async_remote_copy(
        src_ref=source, dst_ref=target, send_sem=send, recv_sem=recv, device_id=device,
        device_id_type=pl.DeviceIdType.MESH,
    )


class Place:
    def __init__(self, seq_count, count):
        self.seq_count, self.count, self.chips = seq_count, count, seq_count // 2
        self.seq, self.mine = lax.axis_index("seq"), lax.axis_index("fsdp")
        self.core, self.chip = lax.rem(self.seq, 2), lax.div(self.seq, 2)
        self.partner = (self.seq + 1 - 2 * self.core, self.mine)

    def fsdp(self, d):
        return lax.rem(self.mine + d, self.count)

    def next_seq(self, k):
        return (lax.rem(self.seq + k, self.seq_count), self.mine)

    def next_chip(self, k):
        return (lax.rem(self.seq + 2 * k, self.seq_count), self.mine)

    def greet(self, chips_too):
        barrier = pltpu.get_barrier_semaphore()
        others = [(self.seq, self.fsdp(d)) for d in range(1, self.count)]
        others += [self.next_seq(k) for k in range(1, self.seq_count)] if chips_too else [self.partner]
        for other in others:
            pl.semaphore_signal(barrier, inc=1, device_id=other, device_id_type=pl.DeviceIdType.MESH)
        pl.semaphore_wait(barrier, len(others))


def collect(here, owners, pieces, whole, send, recv, local_sem, core_send, core_recv):
    def piece(n, target, source):
        return remote(pieces.at[n], whole.at[source, here.core], send.at[n], recv.at[source], (here.seq, target))

    for n, (row, owner) in enumerate(owners):
        @pl.when((here.chip == row) & (here.mine != owner))
        def _():
            piece(n, owner, here.mine).start()

    def finish():
        for n, (row, owner) in enumerate(owners):
            @pl.when((here.chip == row) & (here.mine == owner))
            def _():
                keep = pltpu.make_async_copy(pieces.at[n], whole.at[here.mine, here.core], local_sem)
                keep.start()
                for d in range(1, here.count):
                    piece(n, here.fsdp(d), here.fsdp(d)).wait_recv()
                keep.wait()
                half = whole.at[:, here.core]
                swap = remote(half, half, core_send, core_recv, here.partner)
                swap.start()
                swap.wait()

        for n, (row, owner) in enumerate(owners):
            @pl.when((here.chip == row) & (here.mine != owner))
            def _():
                piece(n, owner, here.mine).wait_send()

    return finish


def hand_back(here, owners, rows, parts, local_sem, send, recv, chip_send, chip_recv, core_send, core_recv):
    def part(m):
        return parts.at[m, here.core]

    def piece(m, d):
        return remote(rows.at[here.fsdp(d)], part(m), send.at[d], recv.at[m], (here.seq, here.fsdp(d)))

    def onward(m, k):
        return remote(part(m), part(m), chip_send.at[m, k - 1], chip_recv.at[m], here.next_chip(k))

    def swap(m):
        return remote(part(m), part(m), core_send.at[m], core_recv.at[m], here.partner)

    for m, (row, owner) in enumerate(owners):
        @pl.when((here.chip == row) & (here.mine == owner))
        def _():
            for d in range(1, here.count):
                piece(m, d).start()
            keep = pltpu.make_async_copy(rows.at[here.mine], part(m), local_sem)
            keep.start()
            keep.wait()

    def finish():
        for m, (row, owner) in enumerate(owners):
            @pl.when((here.chip == row) & (here.mine != owner))
            def _():
                piece(m, 0).wait_recv()

            @pl.when(here.chip == row)
            def _():
                for k in range(1, here.chips):
                    onward(m, k).start()
                swap(m).start()

        for m, (row, owner) in enumerate(owners):
            @pl.when(here.chip != row)
            def _():
                onward(m, 1).wait_recv()
                swap(m).start()

        for m, (row, owner) in enumerate(owners):
            swap(m).wait()

            @pl.when(here.chip == row)
            def _():
                for k in range(1, here.chips):
                    onward(m, k).wait_send()

            @pl.when((here.chip == row) & (here.mine == owner))
            def _():
                for d in range(1, here.count):
                    piece(m, d).wait_send()

    return finish


def collect_sems(kinds, count):
    dma = pltpu.SemaphoreType.DMA
    return [dma((kinds,)), dma((count,)), dma, dma, dma]


def hand_back_sems(kinds, count, chips):
    dma = pltpu.SemaphoreType.DMA
    return [dma, dma((count,)), dma((kinds,)), dma((kinds, chips)), dma((kinds,)), dma((kinds,)), dma((kinds,))]


def weight_grad_kernel(seq_count, joint_ref, near_norm, near_top, far_norm, far_top, near_hidden, near_gate, near_up,
                       far_hidden, far_gate, far_up, grads_ref, back_ref, send_sem, recv_sem):
    here = Place(seq_count, 1)
    turn = pl.program_id(0)

    def onward(k):
        device = here.next_chip(here.chips - k)
        return remote(joint_ref.at[k - 1], back_ref.at[k - 1], send_sem.at[k - 1], recv_sem.at[k - 1], device)

    @pl.when(turn == 0)
    def _():
        barrier = pltpu.get_barrier_semaphore()
        for k in range(1, here.chips):
            pl.semaphore_signal(barrier, inc=1, device_id=here.next_chip(k), device_id_type=pl.DeviceIdType.MESH)
        pl.semaphore_wait(barrier, here.chips - 1)
        for k in range(1, here.chips):
            onward(k).start()

    size = near_gate.shape[1]
    rows = (
        (near_norm, near_gate, far_norm, far_gate),
        (near_norm, near_up, far_norm, far_up),
        (near_top, near_hidden, far_top, far_hidden),
    )
    for j, (near_left, near_right, far_left, far_right) in enumerate(rows):
        value = product(near_left[...], near_right[...], (0, 0)) + product(far_left[...], far_right[...], (0, 0))
        grads_ref[:, j * size : (j + 1) * size] = value.astype(LOW)

    @pl.when(turn == pl.num_programs(0) - 1)
    def _():
        for k in range(1, here.chips):
            onward(k).wait()


def weight_grads(joint, near_norm, near_top, far_norm, far_top, near, far, seq_count, call_id):
    width, size = near_norm.shape[1], near[0].shape[1]
    dma = pltpu.SemaphoreType.DMA
    hold = pl.BlockSpec(memory_space=pl.ANY)

    def columns(one):
        return pl.BlockSpec((one.shape[0], TILE), lambda i: (0, i))

    def whole(one):
        return pl.BlockSpec(one.shape, lambda i: (0, 0))

    lefts, rights = (near_norm, near_top, far_norm, far_top), tuple(near) + tuple(far)
    tokens = near_norm.shape[0] + far_norm.shape[0]
    return pl.pallas_call(
        partial(weight_grad_kernel, seq_count),
        grid=(width // TILE,),
        in_specs=[hold] + [columns(one) for one in lefts] + [whole(one) for one in rights],
        out_specs=(pl.BlockSpec((TILE, 3 * size), lambda i: (i, 0)), hold),
        out_shape=(
            jax.ShapeDtypeStruct((width, 3 * size), LOW),
            jax.ShapeDtypeStruct(joint.shape, joint.dtype),
        ),
        scratch_shapes=[dma((max(seq_count // 2 - 1, 1),)), dma((max(seq_count // 2 - 1, 1),))],
        compiler_params=pltpu.CompilerParams(collective_id=call_id, has_side_effects=True, vmem_limit_bytes=48 << 20),
        cost_estimate=pl.CostEstimate(flops=6 * tokens * width * size, bytes_accessed=24 << 20, transcendentals=0),
    )(joint, *lefts, *rights)


def middle_kernel(owners, seq_count, count, part_ref, prior_ref, small_ref, wide_ref, sum_ref, small_out, square_whole,
                  wide_whole, chip_ref, total_ref, piece_ref, place_ref, seq_ref, chip_send, chip_recv, half_sem,
                  place_send, place_recv, seq_send, seq_recv, *sems):
    here = Place(seq_count, count)
    width = piece_ref.shape[2]
    chip_ref[here.chip] = part_ref[...]
    place_ref[here.mine] = small_ref[here.mine]
    here.greet(True)
    small_copies = []
    for d in range(1, count):
        copy = remote(
            small_ref.at[here.fsdp(d)], place_ref.at[here.mine], place_send.at[d - 1], place_recv.at[here.mine],
            (here.seq, here.fsdp(d)),
        )
        copy.start()
        small_copies.append(copy)
    own = chip_ref.at[here.chip]
    onward = [
        remote(own, own, chip_send.at[k - 1], chip_recv.at[here.chip], here.next_chip(k)) for k in range(1, here.chips)
    ]
    for copy in onward:
        copy.start()
    finish_wide = collect(here, owners[:3], wide_ref, wide_whole, *sems[:5])
    for k in range(1, here.chips):
        source = lax.rem(here.chip + k, here.chips)
        other = chip_ref.at[source]
        remote(other, other, chip_send.at[k - 1], chip_recv.at[source], here.next_chip(k)).wait_recv()
    total = chip_ref[0].astype(FULL)
    for i in range(1, here.chips):
        total = total + chip_ref[i].astype(FULL)
    total_ref[...] = total
    fresh = (momentum_decay * prior_ref[...] + total).astype(LOW)
    span = GROUP * HD
    for g in range(width // span):
        for j in range(3):
            at = (3 * g + j) * span
            piece_ref[j, :, g * span : (g + 1) * span] = fresh[:, at : at + span]
    piece_ref[3] = fresh[:, 3 * width :]
    finish_square = collect(here, owners[3:], piece_ref, square_whole, *sems[5:])
    half_copy = remote(total_ref, sum_ref.at[here.core], half_sem.at[0], half_sem.at[1], here.partner)
    half_copy.start()
    keep = pltpu.make_async_copy(total_ref, sum_ref.at[here.core], half_sem.at[2])
    keep.start()
    for d in range(1, count):
        source = here.fsdp(d)
        other = place_ref.at[source]
        remote(other, other, place_send.at[d - 1], place_recv.at[source], (here.seq, source)).wait_recv()
    small = place_ref[0]
    for i in range(1, count):
        small = small + place_ref[i]
    seq_ref[here.seq] = small
    own = seq_ref.at[here.seq]
    for k in range(1, seq_count):
        copy = remote(own, own, seq_send.at[k - 1], seq_recv.at[here.seq], here.next_seq(k))
        copy.start()
        small_copies.append(copy)
    for k in range(1, seq_count):
        source = lax.rem(here.seq + k, seq_count)
        other = seq_ref.at[source]
        remote(other, other, seq_send.at[k - 1], seq_recv.at[source], here.next_seq(k)).wait_recv()
    small = seq_ref[0]
    for i in range(1, seq_count):
        small = small + seq_ref[i]
    small_out[...] = small
    finish_square()
    finish_wide()
    keep.wait()
    half_copy.wait()
    for copy in onward + small_copies:
        copy.wait_send()


def middle(part, prior, small, wide, owners, call_id, seq_count, count):
    half, columns = part.shape
    width = columns // 4
    chips = seq_count // 2
    dma = pltpu.SemaphoreType.DMA
    hold, vmem = pl.BlockSpec(memory_space=pl.ANY), pl.BlockSpec(memory_space=pltpu.VMEM)
    return pl.pallas_call(
        partial(middle_kernel, owners, seq_count, count),
        in_specs=[vmem, vmem, vmem, hold],
        out_specs=(hold, vmem, hold, hold),
        out_shape=(
            jax.ShapeDtypeStruct((2, half, columns), FULL),
            jax.ShapeDtypeStruct(small.shape[1:], FULL),
            jax.ShapeDtypeStruct((count, 2, half, width), LOW),
            jax.ShapeDtypeStruct((count, 2) + wide.shape[1:], LOW),
        ),
        scratch_shapes=[
            pltpu.VMEM((chips, half, columns), LOW),
            pltpu.VMEM((half, columns), FULL),
            pltpu.VMEM((4, half, width), LOW),
            pltpu.VMEM(small.shape, FULL),
            pltpu.VMEM((seq_count,) + small.shape[1:], FULL),
            dma((max(chips - 1, 1),)),
            dma((chips,)),
            dma((3,)),
            dma((count,)),
            dma((count,)),
            dma((seq_count,)),
            dma((seq_count,)),
        ]
        + collect_sems(3, count)
        + collect_sems(4, count),
        compiler_params=pltpu.CompilerParams(collective_id=call_id, has_side_effects=True, vmem_limit_bytes=24 << 20),
    )(part, prior, small, wide)


def hand_back_kernel(owners, seq_count, count, wide_ref, square_ref, wide_parts, square_parts, *sems):
    here = Place(seq_count, count)
    here.greet(True)
    finish_square = hand_back(here, owners[3:], square_ref, square_parts, *sems[7:])
    finish_wide = hand_back(here, owners[:3], wide_ref, wide_parts, *sems[:7])
    finish_square()
    finish_wide()


def handed_back(wide_rows, square_rows, owners, call_id, seq_count, count):
    hold = pl.BlockSpec(memory_space=pl.ANY)
    chips = seq_count // 2
    return pl.pallas_call(
        partial(hand_back_kernel, owners, seq_count, count),
        in_specs=[hold, hold],
        out_specs=(hold, hold),
        out_shape=(
            jax.ShapeDtypeStruct((3, 2) + wide_rows.shape[1:], LOW),
            jax.ShapeDtypeStruct((4, 2) + square_rows.shape[1:], LOW),
        ),
        scratch_shapes=hand_back_sems(3, count, chips) + hand_back_sems(4, count, chips),
        compiler_params=pltpu.CompilerParams(collective_id=call_id, has_side_effects=True),
    )(wide_rows, square_rows)


def tile_count(width, seq_count):
    return -(-(width // HD) // seq_count)


def prepare_kernel(seq_count, mixer_ref, output_ref, gate_up_ref, down_ref, strength_ref, filter_ref, gain_ref, head_ref,
                   square_ref, ff_ref, small_ref):
    shard, width = output_ref.shape
    span = GROUP * HD
    tiles = gate_up_ref.shape[2] // HD
    per = tile_count(gate_up_ref.shape[2], seq_count)
    seq = lax.axis_index("seq")
    for g in range(width // span):
        for j in range(3):
            at = (3 * g + j) * span
            square_ref[:, at : at + span] = mixer_ref[j, :, g * span : (g + 1) * span].astype(LOW)
    square_ref[:, 3 * width :] = output_ref[...].astype(LOW)
    for i in range(per):
        tile = i * seq_count + seq
        at = pl.ds(pl.multiple_of(jnp.minimum(tile, tiles - 1) * HD, HD), HD)
        kept = jnp.where(tile < tiles, 1.0, 0.0).astype(FULL)
        for j in range(2):
            to = (j * per + i) * HD
            ff_ref[:, to : to + HD] = (gate_up_ref[j, :, at] * kept).astype(LOW)
        to = (2 * per + i) * HD
        ff_ref[:, to : to + HD] = (down_ref[at, :] * kept).T.astype(LOW)
    small_ref[...] = jnp.zeros_like(small_ref)
    heads = strength_ref.shape[1]
    rows = [strength_ref[...].T] + [filter_ref[j] for j in range(3)] + [gain_ref[...]]
    at = 0
    for one in rows:
        small_ref[at : at + one.shape[0], :shard] = one.astype(LOW)
        at += one.shape[0]
    small_ref[at : at + 1, : head_ref.shape[1]] = head_ref[...].astype(LOW)


def prepared(mixer, output, gate_up, down, strength, filters, gain, head, seq_count):
    shard, width = output.shape
    columns = 3 * tile_count(gate_up.shape[2], seq_count) * HD
    vmem = pl.BlockSpec(memory_space=pltpu.VMEM)
    return pl.pallas_call(
        partial(prepare_kernel, seq_count),
        in_specs=[vmem] * 8,
        out_specs=(vmem,) * 3,
        out_shape=(
            jax.ShapeDtypeStruct((shard, 4 * width), LOW),
            jax.ShapeDtypeStruct((shard, columns), LOW),
            jax.ShapeDtypeStruct((32, 128), LOW),
        ),
        compiler_params=pltpu.CompilerParams(vmem_limit_bytes=40 << 20),
    )(mixer, output, gate_up, down, strength, filters, gain, head[None])


def wide_moment_kernel(seq_count, gate_up_ref, down_ref, stack_ref, gate_up_out, down_out, sent_ref, hold_ref):
    half = sent_ref.shape[1]
    tiles = gate_up_ref.shape[2] // HD
    per = stack_ref.shape[2] // (3 * HD)
    core = lax.rem(lax.axis_index("seq"), 2)
    mine = pl.ds(pl.multiple_of(core * half, half), half)
    for t in range(tiles):
        source, i = t % seq_count, t // seq_count
        at = slice(t * HD, (t + 1) * HD)
        for j in range(2):
            grad = stack_ref[source, :, (j * per + i) * HD : (j * per + i + 1) * HD].astype(FULL)
            gate_up_out[j, :, at] = momentum_decay * gate_up_ref[j, :, at] + grad
            sent_ref[j, :, at] = gate_up_out[j, mine, at].astype(LOW)
        grad = stack_ref[source, :, (2 * per + i) * HD : (2 * per + i + 1) * HD].astype(FULL)
        fresh = momentum_decay * down_ref[at, :] + grad.T
        down_out[at, :] = fresh
        hold_ref[...] = fresh.T
        sent_ref[2, :, at] = hold_ref[mine, :].astype(LOW)


def wide_moments(gate_up, down, stack, seq_count):
    shard, width = gate_up.shape[1:]
    vmem = pl.BlockSpec(memory_space=pltpu.VMEM)
    return pl.pallas_call(
        partial(wide_moment_kernel, seq_count),
        in_specs=[vmem] * 3,
        out_specs=(vmem,) * 3,
        out_shape=(
            jax.ShapeDtypeStruct(gate_up.shape, FULL),
            jax.ShapeDtypeStruct(down.shape, FULL),
            jax.ShapeDtypeStruct((3, shard // 2, width), LOW),
        ),
        scratch_shapes=[pltpu.VMEM((shard, HD), FULL)],
        compiler_params=pltpu.CompilerParams(vmem_limit_bytes=40 << 20),
    )(gate_up, down, stack)


def finish_kernel(
    wide_ref, square_ref, sum_ref, small_ref, mixer_w, output_w, gate_up_w, down_w, strength_w, filter_w, gain_w, head_w,
    mixer_m, output_m, strength_m, filter_m, gain_m, head_m,
    new_mixer_m, new_mixer_w, new_strength_m, new_strength_w, new_filter_m, new_filter_w, new_gain_m, new_gain_w,
    new_head_m, new_head_w, new_output_m, new_output_w, new_gate_up_w, new_down_w,
):
    shard, width = output_w.shape
    span = GROUP * HD
    for g in range(width // span):
        for j in range(3):
            at, to = (3 * g + j) * span, slice(g * span, (g + 1) * span)
            new_mixer_m[j, :, to] = momentum_decay * mixer_m[j, :, to] + sum_ref[:, at : at + span]
    for j in range(3):
        new_mixer_w[j] = mixer_w[j] - matrix_rate * square_ref[j].astype(FULL)
    new_output_m[...] = momentum_decay * output_m[...] + sum_ref[:, 3 * width :]
    new_output_w[...] = output_w[...] - matrix_rate * square_ref[3].astype(FULL)
    for j in range(2):
        new_gate_up_w[j] = gate_up_w[j] - matrix_rate * wide_ref[j].astype(FULL)
    for t in range(down_w.shape[0] // HD):
        at = slice(t * HD, (t + 1) * HD)
        new_down_w[at, :] = down_w[at, :] - matrix_rate * wide_ref[2, :, at].astype(FULL).T
    heads = strength_w.shape[1]
    fresh = momentum_decay * strength_m[...] + small_ref[:heads, :].T
    new_strength_m[...] = fresh
    new_strength_w[...] = strength_w[...] - strength_rate * fresh
    for j in range(3):
        fresh = momentum_decay * filter_m[j] + small_ref[heads + CONV * j : heads + CONV * (j + 1), :]
        new_filter_m[j] = fresh
        new_filter_w[j] = filter_w[j] - filter_rate * fresh
    at = heads + 3 * CONV
    fresh = momentum_decay * gain_m[...] + small_ref[at : at + 2, :]
    new_gain_m[...] = fresh
    new_gain_w[...] = gain_w[...] - gain_rate * fresh
    fresh = momentum_decay * head_m[...] + small_ref[at + 2 : at + 3, : head_m.shape[1]]
    new_head_m[...] = fresh
    new_head_w[...] = head_w[...] - gain_rate * fresh


def finished(wide, square, total, small, weights, moments):
    mixer_w, output_w, gate_up_w, down_w, strength_w, filter_w, gain_w, head_w = weights
    mixer_m, output_m, strength_m, filter_m, gain_m, head_m = moments
    pairs = [mixer_w, strength_w, filter_w, gain_w, head_w[None], output_w]
    shapes = [jax.ShapeDtypeStruct(one.shape, FULL) for pair in zip(pairs, pairs) for one in pair]
    shapes += [jax.ShapeDtypeStruct(one.shape, FULL) for one in (gate_up_w, down_w)]
    vmem = pl.BlockSpec(memory_space=pltpu.VMEM)
    return pl.pallas_call(
        finish_kernel,
        in_specs=[vmem] * 18,
        out_specs=(vmem,) * len(shapes),
        out_shape=tuple(shapes),
        compiler_params=pltpu.CompilerParams(vmem_limit_bytes=56 << 20),
    )(
        wide, square, total, small, mixer_w, output_w, gate_up_w, down_w, strength_w, filter_w, gain_w, head_w[None],
        mixer_m, output_m, strength_m, filter_m, gain_m, head_m[None],
    )


TILE = 256


def row_loop(rows, body):
    @pl.loop(0, rows // TILE)
    def _(i):
        body(pl.ds(pl.multiple_of(i * TILE, TILE), TILE))


def trace_of(square_ref):
    total = jnp.zeros((1, 1), FULL)
    for i in range(square_ref.shape[0] // TILE):
        tile = square_ref[i * TILE : (i + 1) * TILE, i * TILE : (i + 1) * TILE]
        rows = lax.broadcasted_iota(jnp.int32, (TILE, TILE), 0)
        cols = lax.broadcasted_iota(jnp.int32, (TILE, TILE), 1)
        total = total + jnp.sum(jnp.where(rows == cols, tile, 0.0), keepdims=True)
    return total


def pick_rows(count, half, source_ref, target_ref):
    core = lax.rem(lax.axis_index("seq"), 2)
    for f in range(count):
        at = pl.multiple_of(f * 2 * half + core * half, 16)
        target_ref[f * half : (f + 1) * half, :] = source_ref[pl.ds(at, half), :]


def orth_wide_kernel(
    count, half, whole_ref, out_ref, square_ref, middle_ref, mapped_ref, gathered_ref,
    square_low, mapped_low, first_low, second_low, rows_low, rows_own,
):
    size = whole_ref.shape[0]

    def start(at):
        square_ref[at, :] = product(whole_ref[at, :], whole_ref[...], (1, 1))

    row_loop(size, start)
    scale = 1.0 / (jnp.sqrt(trace_of(square_ref)) + 1e-07)

    def scaled(at):
        value = square_ref[at, :] * (scale * scale)
        square_ref[at, :] = value
        square_low[at, :] = value.astype(LOW)

    row_loop(size, scaled)
    level = 1.0
    gathered_low, spare_low = first_low, second_low
    for sweep in range(NS_STEPS - 1):
        keep_ref = gathered_ref if sweep == 0 else mapped_ref

        def mapping(at):
            value = coef_cubic * square_ref[at, :] + coef_quintic * product(square_low[at, :], square_low[...])
            keep_ref[at, :] = value
            mapped_low[at, :] = value.astype(LOW)

        row_loop(size, mapping)
        if sweep == 0:
            def copy_low(at):
                gathered_low[at, :] = mapped_low[at, :]

            row_loop(size, copy_low)
        else:
            def gather(at):
                value = (
                    coef_linear * gathered_ref[at, :]
                    + level * mapped_ref[at, :]
                    + product(mapped_low[at, :], gathered_low[...])
                )
                gathered_ref[at, :] = value
                spare_low[at, :] = value.astype(LOW)

            row_loop(size, gather)
            gathered_low, spare_low = spare_low, gathered_low
        level = level * coef_linear

        def middle(at):
            value = coef_linear * square_ref[at, :] + product(mapped_low[at, :], square_low[...])
            middle_ref[at, :] = value
            spare_low[at, :] = value.astype(LOW)

        row_loop(size, middle)

        def squared(at):
            value = coef_linear * middle_ref[at, :] + product(spare_low[at, :], mapped_low[...])
            square_ref[at, :] = value
            square_low[at, :] = value.astype(LOW)

        row_loop(size, squared)

    pick_rows(count, half, square_low, rows_low)
    pick_rows(count, half, square_ref, mapped_ref)
    pick_rows(count, half, gathered_ref, middle_ref)
    pick_rows(count, half, whole_ref, rows_own)

    def last(at):
        mapped = coef_cubic * mapped_ref[at, :] + coef_quintic * product(rows_low[at, :], square_low[...])
        value = coef_linear * middle_ref[at, :] + level * mapped + product(mapped.astype(LOW), gathered_low[...])
        rows_low[at, :] = value.astype(LOW)

    row_loop(size // 2, last)
    level = level * coef_linear

    @pl.loop(0, whole_ref.shape[1] // TILE)
    def _(i):
        at = pl.ds(pl.multiple_of(i * TILE, TILE), TILE)
        value = level * rows_own[:, at].astype(FULL) + product(rows_low[...], whole_ref[:, at])
        out_ref[:, at] = (value * scale).astype(LOW)


def orth_square_kernel(
    count, half, whole_ref, out_ref, square_ref, current_ref, square_low, mapped_low, first_low, second_low,
    rows_low, rows_own,
):
    size = whole_ref.shape[0]

    def start(at):
        square_ref[at, :] = product(whole_ref[at, :], whole_ref[...], (1, 1))

    row_loop(size, start)
    scale = 1.0 / (jnp.sqrt(trace_of(square_ref)) + 1e-07)

    def scaled(at):
        value = whole_ref[at, :].astype(FULL) * scale
        current_ref[at, :] = value
        first_low[at, :] = value.astype(LOW)
        value = square_ref[at, :] * (scale * scale)
        square_ref[at, :] = value
        square_low[at, :] = value.astype(LOW)

    row_loop(size, scaled)
    now, later = first_low, second_low
    for sweep in range(NS_STEPS):
        if sweep:
            def squared(at):
                value = product(now[at, :], now[...], (1, 1))
                square_ref[at, :] = value
                square_low[at, :] = value.astype(LOW)

            row_loop(size, squared)

        def mapping(at):
            value = coef_cubic * square_ref[at, :] + coef_quintic * product(square_low[at, :], square_low[...])
            mapped_low[at, :] = value.astype(LOW)

        row_loop(size, mapping)
        if sweep < NS_STEPS - 1:
            def step(at):
                value = coef_linear * current_ref[at, :] + product(mapped_low[at, :], now[...])
                current_ref[at, :] = value
                later[at, :] = value.astype(LOW)

            row_loop(size, step)
            now, later = later, now
    pick_rows(count, half, mapped_low, rows_low)
    pick_rows(count, half, current_ref, rows_own)

    @pl.loop(0, size // TILE)
    def _(i):
        at = pl.ds(pl.multiple_of(i * TILE, TILE), TILE)
        value = coef_linear * rows_own[:, at] + product(rows_low[...], now[:, at])
        out_ref[:, at] = value.astype(LOW)


def orth_call(kernel, scratch, count, whole):
    half, width = whole.shape[2:]
    size = count * 2 * half
    flat = whole.reshape(size, width)
    vmem = pl.BlockSpec(memory_space=pltpu.VMEM)
    result = pl.pallas_call(
        partial(kernel, count, half),
        in_specs=[vmem],
        out_specs=vmem,
        out_shape=jax.ShapeDtypeStruct((size // 2, width), LOW),
        scratch_shapes=scratch(size, width),
        compiler_params=pltpu.CompilerParams(vmem_limit_bytes=56 << 20),
    )(flat)
    return result.reshape(count, half, width)


def orth_wide(count, whole):
    def scratch(size, width):
        return (
            [pltpu.VMEM((size, size), FULL)] * 4
            + [pltpu.VMEM((size, size), LOW)] * 4
            + [pltpu.VMEM((size // 2, size), LOW), pltpu.VMEM((size // 2, width), LOW)]
        )

    return orth_call(orth_wide_kernel, scratch, count, whole)


def orth_square(count, whole):
    def scratch(size, width):
        return (
            [pltpu.VMEM((size, size), FULL)] * 2
            + [pltpu.VMEM((size, size), LOW)] * 4
            + [pltpu.VMEM((size // 2, size), LOW), pltpu.VMEM((size // 2, width), FULL)]
        )

    return orth_call(orth_square_kernel, scratch, count, whole)


def chosen_place(owners, mine, chip):
    chosen = (mine == owners[0][1]) & (chip == owners[0][0])
    for row, place in owners[1:]:
        chosen = chosen | ((mine == place) & (chip == row))
    return chosen


def orthogonal(whole, owners, method, mine, chip, count):
    half, width = whole.shape[2:]
    return lax.cond(
        chosen_place(owners, mine, chip),
        partial(method, count),
        lambda one: jnp.zeros((count, half, width), LOW),
        whole,
    )


def on_device(
    inputs,
    cotangent,
    lengths,
    mixer_weight,
    strength_weight,
    filter_weight,
    norm_gain,
    head_gain,
    output_weight,
    gate_up_weight,
    down_weight,
    mixer_moment,
    strength_moment,
    filter_moment,
    gain_moment,
    head_gain_moment,
    output_moment,
    gate_up_moment,
    down_moment,
):
    seq_count = lax.axis_size("seq")
    seq_index = lax.axis_index("seq")
    fsdp_count = lax.axis_size("fsdp")
    fsdp_index = lax.axis_index("fsdp")
    row_count, width = inputs.shape
    shard = width // fsdp_count
    heads_all = strength_weight.shape[1]

    wide_ff = tile_count(gate_up_weight.shape[2], seq_count) * HD
    core = seq_index % 2
    half = shard // 2
    groups = heads_all // GROUP
    span = GROUP * HD
    small_count = heads_all + 3 * CONV + 3
    top_near = core_swapped(cotangent)
    top_far = [chip_shifted(cotangent, k) for k in range(1, seq_count // 2)]
    square_own, ff_own, small_own = prepared(
        mixer_weight, output_weight, gate_up_weight, down_weight, strength_weight, filter_weight, norm_gain, head_gain,
        seq_count,
    )
    square_full, small_full = gathered_mixer(square_own, small_own, seq_count, fsdp_count)
    by_place = small_full.reshape(-1, fsdp_count, 128)
    small_wide = small_full if shard == 128 else by_place[:, :, :shard].reshape(-1, width)
    strength_full = small_wide[:heads_all]
    filters_wide = small_wide[heads_all : heads_all + 3 * CONV].reshape(3, CONV, width).astype(FULL)
    gains_wide = small_wide[heads_all + 3 * CONV : heads_all + 3 * CONV + 2].astype(FULL)
    head_part = head_gain.shape[0]
    head_gain_full = by_place[small_count - 1, :, :head_part].reshape(1, HD).astype(FULL)

    square_full, ff_own, top_near, top_far = lax.optimization_barrier((square_full, ff_own, top_near, top_far))
    top_parts = [cotangent, top_near] + [part for one in top_far for part in (one, core_swapped(one))]
    ff_full = lax.all_gather(ff_own, "fsdp", axis=0, tiled=True)
    mixer_full, output_full = square_full[:, : 3 * width], square_full[:, 3 * width :]
    ff_parts = [ff_full[:, j * wide_ff : (j + 1) * wide_ff] for j in range(3)]

    my_lengths = lax.dynamic_slice_in_dim(lengths, fsdp_index, 1, 0)[0]
    doc_ends = jnp.cumsum(my_lengths)

    def passed_docs(at):
        return (at[:, None] >= doc_ends[None, :]).astype(jnp.int32)

    own = seq_index * row_count + jnp.arange(row_count, dtype=jnp.int32)
    passed = passed_docs(own)
    segment = jnp.sum(passed, axis=1)
    doc_first = jnp.sum(passed * my_lengths[None, :], axis=1)
    block_start = own.reshape(-1, BLOCK)[:, 0]
    before = jnp.where(block_start == 0, -1, jnp.sum(passed_docs(block_start - 1), axis=1))
    blocked = segment.reshape(-1, BLOCK)
    carried = (blocked == before[:, None]).reshape(-1)
    trailing = (blocked == blocked[:, -1:]).reshape(-1)
    columns = [own - lag >= doc_first for lag in range(CONV)] + [carried, trailing, segment]
    meta = jnp.stack([one.astype(FULL) for one in columns] + [jnp.zeros((row_count,), FULL)], axis=1)
    meta_row = jnp.broadcast_to(segment.astype(FULL)[None, :], (8, row_count))

    residual_in = inputs.astype(FULL)
    scale_one = lax.rsqrt(jnp.mean(residual_in * residual_in, axis=-1, keepdims=True) + norm_eps)
    unit_one = residual_in * scale_one
    normed_low = (unit_one * gains_wide[0]).astype(LOW)
    projected = low_dot(normed_low, mixer_full, (1, 0)).astype(LOW)
    logits = low_dot(normed_low, strength_full, (1, 1))
    strength = jax.nn.sigmoid(logits).astype(LOW).astype(FULL)
    forth = [(i, i + 1) for i in range(seq_count - 1)]
    rim = lax.ppermute(projected[row_count - RIM :], "seq", forth)
    mixed, solve, weight, update, drift, local_out, effective, states, end, transfer = forward_blocks(
        projected, rim, filters_wide, strength, meta, meta_row
    )
    enter = exchanged(end, transfer, False, 4)
    delta_out, head_normed = head_outputs(local_out, effective, enter, head_gain_full)
    residual = residual_in + low_dot(head_normed, output_full, (1, 0))
    scale_two = lax.rsqrt(jnp.mean(residual * residual, axis=-1, keepdims=True) + norm_eps)
    unit_two = residual * scale_two
    normed_two = (unit_two * gains_wide[1]).astype(LOW)
    gate_full, up_full, down_full = ff_parts
    chips = seq_count // 2
    near_norm = jnp.concatenate([normed_two, core_swapped(normed_two)])
    far_straight = [chip_shifted(normed_two, k) for k in range(1, chips)]

    def spread_out(normed_part, top_part):
        gate = low_dot(normed_part, gate_full, (1, 0))
        up = low_dot(normed_part, up_full, (1, 0))
        gate_sigmoid = jax.nn.sigmoid(gate)
        gate_silu = gate * gate_sigmoid
        hidden = (gate_silu * up).astype(LOW)
        grad_hidden = low_dot(top_part, down_full, (1, 0))
        grad_gate = (grad_hidden * up * (gate_sigmoid * (1.0 + gate * (1.0 - gate_sigmoid)))).astype(LOW)
        grad_up = (grad_hidden * gate_silu).astype(LOW)
        return hidden, grad_gate, grad_up

    def grad_in(values):
        return low_dot(values[1], gate_full, (1, 1)) + low_dot(values[2], up_full, (1, 1))

    near_top, far_top = jnp.concatenate(top_parts[:2]), jnp.concatenate(top_parts[2:])
    near = spread_out(near_norm, near_top)
    far_straight, near = lax.optimization_barrier((far_straight, near))
    far_parts = [part for one in far_straight for part in (one, core_swapped(one))]
    near_grad = grad_in(near)
    near_back = core_swapped(near_grad[row_count:].astype(LOW))
    near_grad, far_parts = lax.optimization_barrier((near_grad, far_parts))
    far_norm = jnp.concatenate(far_parts)
    far = spread_out(far_norm, far_top)

    def picked(values, side):
        size = 2 * row_count
        return [
            tuple(one[i * size + side * row_count : i * size + (side + 1) * row_count] for one in values)
            for i in range(chips - 1)
        ]

    crossed = [core_swapped(grad_in(one).astype(LOW)) for one in picked(far, 1)]
    joint = [(grad_in(one) + other.astype(FULL)).astype(LOW) for one, other in zip(picked(far, 0), crossed)]
    ff_grads, back_parts = weight_grads(
        jnp.stack(joint), near_norm, near_top, far_norm, far_top, near, far, seq_count, 6
    )
    ff_part = lax.psum_scatter(ff_grads, "fsdp", scatter_dimension=0, tiled=True)
    back_parts = [near_back] + [back_parts[k] for k in range(chips - 1)]
    grad_normed_two = near_grad[:row_count] + sum(one.astype(FULL) for one in back_parts)
    back_two, grad_gain_two = norm_back(unit_two, scale_two, gains_wide[1], grad_normed_two)
    grad_residual = back_two + cotangent.astype(FULL)
    grad_attention = grad_residual.astype(LOW)
    grad_head_normed = low_dot(grad_attention, output_full, (1, 1)).astype(LOW)

    upstream, adjoint_local, grad_head_gain = head_back(
        grad_head_normed, delta_out, effective, head_gain_full
    )
    leave = exchanged(adjoint_local, transfer, True, 5)
    grad_projected, grad_strength, grad_filter, edge, lead = backward_blocks(
        projected, rim, filters_wide, strength, meta, meta_row, mixed, solve, weight, update, drift,
        upstream, states, enter, leave,
    )
    back = [(i + 1, i) for i in range(seq_count - 1)]
    incoming = lax.ppermute(lead.astype(LOW), "seq", back).astype(FULL)
    grad_projected = lax.dynamic_update_slice(
        grad_projected, (edge + incoming).astype(LOW), (row_count - 8, 0)
    )
    grad_strength = grad_strength.astype(LOW).astype(FULL)
    grad_logits = (grad_strength * strength * (1.0 - strength)).astype(LOW)
    def core_rows(values):
        by_core = values.reshape(row_count, fsdp_count, 2, half)
        return [
            lax.dynamic_slice_in_dim(by_core, at, 1, 2).reshape(row_count, width // 2) for at in (core, 1 - core)
        ]

    grad_mixer = [low_dot(one, grad_projected, (0, 0)) for one in core_rows(normed_low)]
    grad_output = [low_dot(one, grad_attention, (0, 0)) for one in core_rows(head_normed)]
    square_grads = jnp.concatenate(
        [
            (mine + core_swapped(other.astype(LOW)).astype(FULL)).astype(LOW)
            for mine, other in (grad_mixer, grad_output)
        ],
        axis=1,
    )
    near_hidden, far_hidden = near[0], far[0]
    square_grads, ff_part, grad_projected, grad_logits, near_hidden, far_hidden = lax.optimization_barrier(
        (square_grads, ff_part, grad_projected, grad_logits, near_hidden, far_hidden)
    )
    far_out, near_out = low_dot(far_hidden, down_full, (1, 1)), low_dot(near_hidden, down_full, (1, 1))
    out_crossed = [core_swapped(one[0].astype(LOW)) for one in picked((far_out,), 1)]
    out_joint = [(one[0] + other.astype(FULL)).astype(LOW) for one, other in zip(picked((far_out,), 0), out_crossed)]
    out_parts = [chip_shifted(one, -(k + 1)) for k, one in enumerate(out_joint)]
    out_near = near_out[:row_count] + core_swapped(near_out[row_count:].astype(LOW)).astype(FULL)
    square_part = lax.psum_scatter(square_grads, "fsdp", scatter_dimension=0, tiled=True)
    grad_strength_weight = low_dot(grad_logits, normed_low, (0, 0))
    grad_normed = low_dot(grad_logits, strength_full, (1, 0)) + low_dot(grad_projected, mixer_full, (1, 1))
    ff_stack = seq_stacked(ff_part)
    back_one, grad_gain_one = norm_back(unit_one, scale_one, gains_wide[0], grad_normed)
    input_grad = grad_residual + back_one

    head_row = jnp.pad(
        grad_head_gain.reshape(fsdp_count, head_part), ((0, 0), (0, shard - head_part))
    ).reshape(1, width)
    small_grads = jnp.concatenate(
        [
            grad_strength_weight,
            grad_filter.reshape(3 * CONV, width),
            grad_gain_one[None],
            grad_gain_two[None],
            head_row,
            jnp.zeros((-small_count % 8, width), FULL),
        ],
        axis=0,
    )
    small_pieces = small_grads.reshape(-1, fsdp_count, shard).transpose(1, 0, 2)

    ff_stack, input_grad, small_pieces = lax.optimization_barrier((ff_stack, input_grad, small_pieces))
    new_gate_up_moment, new_down_moment, wide_sent = wide_moments(gate_up_moment, down_moment, ff_stack, seq_count)
    owners = tuple(matrix_owners(fsdp_count))
    chip = seq_index // 2
    mixer_prior = lax.dynamic_slice_in_dim(mixer_moment, core * half, half, 1)
    output_prior = lax.dynamic_slice_in_dim(output_moment, core * half, half, 0)
    square_prior = jnp.concatenate(
        [mixer_prior[j, :, g * span : (g + 1) * span] for g in range(groups) for j in range(3)] + [output_prior], axis=1
    )
    block_output = residual + (out_near + sum(one.astype(FULL) for one in out_parts))
    wide_sent, square_prior, block_output = lax.optimization_barrier((wide_sent, square_prior, block_output))
    square_sum, small_own, square_all, wide_all = middle(
        square_part, square_prior, small_pieces, wide_sent, owners, 2, seq_count, fsdp_count
    )
    square_rows = orthogonal(square_all, owners[3:], orth_square, fsdp_index, chip, fsdp_count)
    wide_rows = orthogonal(wide_all, owners[:3], orth_wide, fsdp_index, chip, fsdp_count)
    wide_parts, square_parts = handed_back(wide_rows, square_rows, owners, 3, seq_count, fsdp_count)
    weights = (
        mixer_weight, output_weight, gate_up_weight, down_weight, strength_weight, filter_weight, norm_gain, head_gain
    )
    moments = (mixer_moment, output_moment, strength_moment, filter_moment, gain_moment, head_gain_moment)
    done = finished(
        wide_parts.reshape(3, shard, -1),
        square_parts.reshape(4, shard, width),
        square_sum.reshape(shard, -1),
        small_own,
        weights,
        moments,
    )
    head_pair = [one[0] for one in done[8:10]]
    return (
        (block_output, input_grad)
        + tuple(done[:8])
        + tuple(head_pair)
        + tuple(done[10:12])
        + (new_gate_up_moment, done[12], new_down_moment, done[13])
    )


def solution(mesh):
    return jax.shard_map(
        on_device,
        mesh=mesh,
        in_specs=(
            P(("seq", "fsdp"), None),
            P(("seq", "fsdp"), None),
            P(),
            P(None, "fsdp", None),
            P("fsdp", None),
            P(None, None, "fsdp"),
            P(None, "fsdp"),
            P("fsdp"),
            P("fsdp", None),
            P(None, "fsdp", None),
            P(None, "fsdp"),
            P(None, "fsdp", None),
            P("fsdp", None),
            P(None, None, "fsdp"),
            P(None, "fsdp"),
            P("fsdp"),
            P("fsdp", None),
            P(None, "fsdp", None),
            P(None, "fsdp"),
        ),
        out_specs=(
            P(("seq", "fsdp"), None),
            P(("seq", "fsdp"), None),
            P(None, "fsdp", None),
            P(None, "fsdp", None),
            P("fsdp", None),
            P("fsdp", None),
            P(None, None, "fsdp"),
            P(None, None, "fsdp"),
            P(None, "fsdp"),
            P(None, "fsdp"),
            P("fsdp"),
            P("fsdp"),
            P("fsdp", None),
            P("fsdp", None),
            P(None, "fsdp", None),
            P(None, "fsdp", None),
            P(None, "fsdp"),
            P(None, "fsdp"),
        ),
        check_vma=False,
    )
```

```python
from functools import partial

import jax
import jax.numpy as jnp
from jax import lax
from jax.experimental import pallas as pl
from jax.experimental.pallas import tpu as pltpu
from jax.sharding import PartitionSpec as P

HD = 128
CONV = 4
BLOCK = 128
GROUP = 8
RIM = 16
NS_STEPS = 3

norm_eps = 1e-06
head_eps = 0.001
momentum_decay = 0.9
matrix_rate = 1.0
filter_rate = 0.01
gain_rate = 0.001
strength_rate = 0.001
coef_linear = 3.4445
coef_cubic = -4.775
coef_quintic = 2.0315

LOW = jnp.bfloat16
FULL = jnp.float32


def halves(values):
    top = values.astype(LOW)
    return (top, (values - top.astype(FULL)).astype(LOW))


def product(left, right, dims=(1, 0)):
    left = left if isinstance(left, tuple) else (left,)
    right = right if isinstance(right, tuple) else (right,)
    total = None
    for i, a in enumerate(left):
        for j, b in enumerate(right):
            if i + j < 2:
                term = lax.dot_general(
                    a, b, (((dims[0],), (dims[1],)), ((), ())), preferred_element_type=FULL
                )
                total = term if total is None else total + term
    return total


def low_product(left, right, dims=(1, 0)):
    return product(left.astype(LOW), right.astype(LOW), dims)


def lanes(values, head):
    return values[:, head * HD : (head + 1) * HD]


def unit_scale(values):
    return lax.rsqrt(jnp.sum(values * values, axis=-1, keepdims=True) + norm_eps)


def block_ids():
    rows = lax.broadcasted_iota(jnp.int32, (BLOCK, BLOCK), 0)
    cols = lax.broadcasted_iota(jnp.int32, (BLOCK, BLOCK), 1)
    return rows, cols


def short_conv(current, previous, taps, meta):
    joined = jnp.concatenate([previous, current], axis=0)
    total = None
    shifted = []
    for lag in range(CONV):
        moved = joined if lag == 0 else pltpu.roll(joined, lag, 0)
        moved = moved[RIM:] * meta[:, lag : lag + 1]
        shifted.append(moved)
        term = moved * taps[lag : lag + 1, :]
        total = term if total is None else total + term
    return total, shifted


def inverse(system, differ):
    rows, cols = block_ids()
    eye = jnp.where(rows == cols, 1.0, 0.0).astype(FULL)
    found = [eye - jnp.where((differ >> 0) == 1, one, 0.0) for one in system]
    level = 1
    while (1 << level) < BLOCK:
        picked = [jnp.where((differ >> level) == 1, one, 0.0).astype(LOW) for one in system]
        low = [one.astype(LOW) for one in found]
        inner = [product(a, b).astype(LOW) for a, b in zip(picked, low)]
        outer = [product(b, a) for a, b in zip(inner, low)]
        found = [a - b for a, b in zip(found, outer)]
        level += 1
    split = [halves(one) for one in found]
    wide = [halves(one) for one in system]
    error = [eye - a - product(b, c) for a, b, c in zip(found, wide, split)]
    return [a + product(b[0], c.astype(LOW)) for a, b, c in zip(found, split, error)]


def forward_kernel(
    proj_ref, prev_ref, rim_ref, taps_ref, strength_ref, strength_row_ref, meta_ref, meta_row_ref,
    mixed_ref, solve_ref, weight_ref, update_ref, drift_ref, out_ref, query_ref, state_ref, end_ref, transfer_ref,
    carry_ref,
):
    step = pl.program_id(1)
    rows, cols = block_ids()
    meta = meta_ref[...]
    carry, tail, segment = meta[:, 4:5], meta[:, 5:6], meta[:, 6:7]
    same = segment == meta_row_ref[0:1, :]
    strict = (rows > cols) & same
    inclusive = (rows >= cols) & same
    differ = rows ^ cols
    carry_last = carry[BLOCK - 1 : BLOCK, :]

    @pl.when(step == 0)
    def _():
        start = jnp.concatenate(
            [jnp.zeros((HD, HD), FULL), jnp.where(rows == cols, 1.0, 0.0).astype(FULL)], axis=1
        )
        for head in range(GROUP):
            carry_ref[head] = start

    first = step == 0
    parts = []
    for j in range(3):
        at = slice(j * GROUP * HD, (j + 1) * GROUP * HD)
        previous = jnp.where(first, rim_ref[:, at].astype(FULL), prev_ref[:, at].astype(FULL))
        conv, _ = short_conv(proj_ref[:, at].astype(FULL), previous, taps_ref[j], meta)
        parts.append(conv * jax.nn.sigmoid(conv))
    queries, keys, values = [], [], []
    for head in range(GROUP):
        query, key = lanes(parts[0], head), lanes(parts[1], head)
        queries.append((query * (unit_scale(query) * HD ** (-0.5))).astype(LOW))
        keys.append((key * unit_scale(key)).astype(LOW))
        values.append(lanes(parts[2], head).astype(LOW))
        mixed_ref[0, :, head * HD : (head + 1) * HD] = queries[head]
        mixed_ref[1, :, head * HD : (head + 1) * HD] = keys[head]
        mixed_ref[2, :, head * HD : (head + 1) * HD] = values[head]
    strength = strength_ref[0]
    strength_row = strength_row_ref[0]
    heads = range(GROUP)
    gram = [product(keys[h], keys[h], (1, 1)) for h in heads]
    system = [jnp.where(strict, strength[:, h : h + 1] * gram[h], 0.0) for h in heads]
    scores = [jnp.where(inclusive, product(queries[h], keys[h], (1, 1)), 0.0) for h in heads]
    solve = inverse(system, differ)
    carry_low, tail_low = carry.astype(LOW), tail.astype(LOW)
    carried_query = [queries[h] * carry_low for h in heads]
    tail_key = [keys[h] * tail_low for h in heads]
    right = [jnp.concatenate([values[h], keys[h] * carry_low], axis=1) for h in heads]
    solved = [product(halves(solve[h] * strength_row[h : h + 1, :]), right[h]) for h in heads]
    state = [carry_ref[h] for h in heads]
    state_parts = [halves(state[h]) for h in heads]
    passed = [product(halves(solved[h][:, HD:]), state_parts[h]) for h in heads]
    zero = jnp.zeros((BLOCK, HD), FULL)
    both = [
        jnp.concatenate([solved[h][:, :HD], zero], axis=1) - passed[h] for h in heads
    ]
    both_parts = [halves(both[h]) for h in heads]
    result = [
        product(carried_query[h], state_parts[h]) + product(halves(scores[h]), both_parts[h])
        for h in heads
    ]
    after = [
        carry_last * state[h] + product(tail_key[h], both_parts[h], (0, 0)) for h in heads
    ]
    for h in heads:
        solve_ref[0, h] = solve[h].astype(LOW)
        at = slice(h * HD, (h + 1) * HD)
        weight_ref[:, at] = solved[h][:, HD:].astype(LOW)
        update_ref[:, at] = both[h][:, :HD]
        drift_ref[:, at] = both[h][:, HD:].astype(LOW)
        out_ref[:, at] = result[h][:, :HD]
        query_ref[:, at] = result[h][:, HD:]
        state_ref[0, h] = state[h]
        carry_ref[h] = after[h]
        end_ref[h] = after[h][:, :HD]
        transfer_ref[h] = after[h][:, HD:]


def forward_blocks(projected, rim, taps, strength, meta, meta_row):
    total = projected.shape[0]
    width = projected.shape[1] // 3
    head_count = width // HD
    groups, steps = head_count // GROUP, total // BLOCK
    span = GROUP * HD
    grouped = strength.reshape(total, groups, GROUP)
    strength_col = grouped.transpose(1, 0, 2)
    strength_row = grouped.transpose(1, 2, 0)
    rows_of = lambda g, n: (n, g)
    shapes = (
        jax.ShapeDtypeStruct((3, total, width), LOW),
        jax.ShapeDtypeStruct((steps, head_count, BLOCK, BLOCK), LOW),
        jax.ShapeDtypeStruct((total, width), LOW),
        jax.ShapeDtypeStruct((total, width), FULL),
        jax.ShapeDtypeStruct((total, width), LOW),
        jax.ShapeDtypeStruct((total, width), FULL),
        jax.ShapeDtypeStruct((total, width), FULL),
        jax.ShapeDtypeStruct((steps, head_count, HD, 2 * HD), FULL),
        jax.ShapeDtypeStruct((head_count, HD, HD), FULL),
        jax.ShapeDtypeStruct((head_count, HD, HD), FULL),
    )
    wide = pl.BlockSpec((BLOCK, span), rows_of)
    ratio = BLOCK // RIM
    return pl.pallas_call(
        forward_kernel,
        grid=(groups, steps),
        in_specs=[
            pl.BlockSpec((BLOCK, 3 * span), rows_of),
            pl.BlockSpec((RIM, 3 * span), lambda g, n: (jnp.maximum(n * ratio - 1, 0), g)),
            pl.BlockSpec((RIM, 3 * span), lambda g, n: (0, g)),
            pl.BlockSpec((3, CONV, span), lambda g, n: (0, 0, g)),
            pl.BlockSpec((1, BLOCK, GROUP), lambda g, n: (g, n, 0)),
            pl.BlockSpec((1, GROUP, BLOCK), lambda g, n: (g, 0, n)),
            pl.BlockSpec((BLOCK, 8), lambda g, n: (n, 0)),
            pl.BlockSpec((8, BLOCK), lambda g, n: (0, n)),
        ],
        out_specs=(
            pl.BlockSpec((3, BLOCK, span), lambda g, n: (0, n, g)),
            pl.BlockSpec((1, GROUP, BLOCK, BLOCK), lambda g, n: (n, g, 0, 0)),
            wide,
            wide,
            wide,
            wide,
            wide,
            pl.BlockSpec((1, GROUP, HD, 2 * HD), lambda g, n: (n, g, 0, 0)),
            pl.BlockSpec((GROUP, HD, HD), lambda g, n: (g, 0, 0)),
            pl.BlockSpec((GROUP, HD, HD), lambda g, n: (g, 0, 0)),
        ),
        out_shape=shapes,
        scratch_shapes=[pltpu.VMEM((GROUP, HD, 2 * HD), FULL)],
        compiler_params=pltpu.CompilerParams(vmem_limit_bytes=48 << 20),
        cost_estimate=pl.CostEstimate(flops=8 << 30, bytes_accessed=24 << 20, transcendentals=0),
    )(projected, projected, rim, taps, strength_col, strength_row, meta, meta_row)


def out_kernel(local_ref, query_ref, state_ref, gain_ref, delta_ref, normed_ref):
    gain = gain_ref[0:1, :]
    for head in range(local_ref.shape[1] // HD):
        at = slice(head * HD, (head + 1) * HD)
        value = local_ref[:, at] + product(halves(query_ref[:, at]), halves(state_ref[head]))
        delta_ref[:, at] = value
        scale = lax.rsqrt(jnp.mean(value * value, axis=-1, keepdims=True) + head_eps)
        normed_ref[:, at] = (value * scale * gain).astype(LOW)


def head_outputs(local_out, effective, state_in, gain):
    total, width = local_out.shape
    rows = pl.BlockSpec((BLOCK, width), lambda n: (n, 0))
    return pl.pallas_call(
        out_kernel,
        grid=(total // BLOCK,),
        in_specs=[
            rows,
            rows,
            pl.BlockSpec(state_in.shape, lambda n: (0, 0, 0)),
            pl.BlockSpec((1, HD), lambda n: (0, 0)),
        ],
        out_specs=(rows, rows),
        out_shape=(
            jax.ShapeDtypeStruct((total, width), FULL),
            jax.ShapeDtypeStruct((total, width), LOW),
        ),
        compiler_params=pltpu.CompilerParams(vmem_limit_bytes=32 << 20),
    )(local_out, effective, state_in, gain)


def head_back_kernel(grad_ref, delta_ref, query_ref, gain_ref, upstream_ref, adjoint_ref, gain_grad_ref):
    step = pl.program_id(0)
    gain = gain_ref[0:1, :]

    @pl.when(step == 0)
    def _():
        adjoint_ref[...] = jnp.zeros_like(adjoint_ref)
        gain_grad_ref[...] = jnp.zeros_like(gain_grad_ref)

    gained = jnp.zeros((1, HD), FULL)
    for head in range(grad_ref.shape[1] // HD):
        at = slice(head * HD, (head + 1) * HD)
        value = delta_ref[:, at]
        grad = grad_ref[:, at].astype(FULL)
        scale = lax.rsqrt(jnp.mean(value * value, axis=-1, keepdims=True) + head_eps)
        unit = value * scale
        gained = gained + jnp.sum(grad * unit, axis=0, keepdims=True)
        grad = grad * gain
        back = scale * (grad - unit * jnp.mean(grad * unit, axis=-1, keepdims=True))
        low = back.astype(LOW)
        upstream_ref[:, at] = low
        adjoint_ref[head] += product(query_ref[:, at].astype(LOW), low, (0, 0))
    gain_grad_ref[...] += gained


def head_back(grad_normed, delta_out, effective, gain):
    total, width = delta_out.shape
    head_count = width // HD
    rows = pl.BlockSpec((BLOCK, width), lambda n: (n, 0))
    return pl.pallas_call(
        head_back_kernel,
        grid=(total // BLOCK,),
        in_specs=[rows, rows, rows, pl.BlockSpec((1, HD), lambda n: (0, 0))],
        out_specs=(
            rows,
            pl.BlockSpec((head_count, HD, HD), lambda n: (0, 0, 0)),
            pl.BlockSpec((1, HD), lambda n: (0, 0)),
        ),
        out_shape=(
            jax.ShapeDtypeStruct((total, width), LOW),
            jax.ShapeDtypeStruct((head_count, HD, HD), FULL),
            jax.ShapeDtypeStruct((1, HD), FULL),
        ),
        compiler_params=pltpu.CompilerParams(vmem_limit_bytes=32 << 20),
    )(grad_normed, delta_out, effective, gain)


def backward_kernel(
    proj_ref, prev_ref, rim_ref, taps_ref, strength_ref, meta_ref, meta_row_ref,
    mixed_ref, solve_ref, weight_ref, update_ref, drift_ref, upstream_ref, state_ref, enter_ref, leave_ref,
    grad_ref, strength_grad_ref, taps_grad_ref, edge_ref, lead_ref,
    adjoint_ref, spill_ref,
):
    turn = pl.program_id(1)
    last_turn = pl.num_programs(1) - 1
    rows, cols = block_ids()
    meta = meta_ref[...]
    carry, tail, segment = meta[:, 4:5], meta[:, 5:6], meta[:, 6:7]
    same = segment == meta_row_ref[0:1, :]
    strict = (rows > cols) & same
    inclusive = (rows >= cols) & same
    carry_last = carry[BLOCK - 1 : BLOCK, :]
    carry_low, tail_low = carry.astype(LOW), tail.astype(LOW)
    heads = range(GROUP)

    @pl.when(turn == 0)
    def _():
        for h in heads:
            adjoint_ref[h] = leave_ref[h]
        spill_ref[...] = jnp.zeros_like(spill_ref)
        taps_grad_ref[...] = jnp.zeros_like(taps_grad_ref)

    strength = strength_ref[0]
    at = [slice(h * HD, (h + 1) * HD) for h in heads]
    query = [mixed_ref[0, :, at[h]] for h in heads]
    key = [mixed_ref[1, :, at[h]] for h in heads]
    value = [mixed_ref[2, :, at[h]] for h in heads]
    upstream = [upstream_ref[:, at[h]] for h in heads]
    enter = [enter_ref[h].astype(LOW) for h in heads]
    state = [
        (state_ref[0, h, :, :HD] + product(state_ref[0, h, :, HD:].astype(LOW), enter[h])).astype(LOW)
        for h in heads
    ]
    update = [
        (update_ref[:, at[h]] + product(drift_ref[:, at[h]], enter[h])).astype(LOW) for h in heads
    ]
    gram = [product(key[h], key[h], (1, 1)) for h in heads]
    scores = [
        jnp.where(inclusive, product(query[h], key[h], (1, 1)), 0.0).astype(LOW) for h in heads
    ]
    tail_key = [key[h] * tail_low for h in heads]
    adjoint = [adjoint_ref[h] for h in heads]
    adjoint_low = [adjoint[h].astype(LOW) for h in heads]
    grad_update = [
        (product(scores[h], upstream[h], (0, 0)) + product(tail_key[h], adjoint_low[h])).astype(LOW)
        for h in heads
    ]
    for h in heads:
        adjoint_ref[h] = (
            carry_last * adjoint[h]
            + product(query[h] * carry_low, upstream[h], (0, 0))
            - product(weight_ref[:, at[h]], grad_update[h], (0, 0))
        )
    grad_right = [product(solve_ref[0, h], grad_update[h], (0, 0)) for h in heads]
    right_low = [grad_right[h].astype(LOW) for h in heads]
    grad_scores = [
        jnp.where(inclusive, product(upstream[h], update[h], (1, 1)), 0.0).astype(LOW) for h in heads
    ]
    grad_query = [
        carry * product(upstream[h], state[h], (1, 1)) + product(grad_scores[h], key[h]) for h in heads
    ]
    right_state = [product(right_low[h], state[h], (1, 1)) for h in heads]
    grad_system = [
        jnp.where(strict, -product(right_low[h], update[h], (1, 1)), 0.0) for h in heads
    ]
    beta = [strength[:, h : h + 1] for h in heads]
    grad_gram = [(beta[h] * grad_system[h]).astype(LOW) for h in heads]
    grad_key = [
        product(grad_scores[h], query[h], (0, 0))
        + tail * product(update[h], adjoint_low[h], (1, 1))
        - (beta[h] * carry) * right_state[h]
        + product(grad_gram[h], key[h])
        + product(grad_gram[h], key[h], (0, 0))
        for h in heads
    ]
    grad_value = [beta[h] * grad_right[h] for h in heads]
    columns = [
        jnp.sum(
            grad_right[h] * value[h].astype(FULL)
            - carry * right_state[h] * key[h].astype(FULL)
            + grad_system[h] * gram[h],
            axis=-1,
            keepdims=True,
        )
        for h in heads
    ]
    strength_grad_ref[0] = jnp.concatenate(columns, axis=1)

    def rounded(values):
        return values.astype(LOW).astype(FULL)

    first = turn == last_turn
    grads = (grad_query, grad_key, grad_value)
    span = GROUP * HD
    for j in range(3):
        at = slice(j * span, (j + 1) * span)
        previous = jnp.where(first, rim_ref[:, at].astype(FULL), prev_ref[:, at].astype(FULL))
        taps = taps_ref[j]
        conv, shifted = short_conv(proj_ref[:, at].astype(FULL), previous, taps, meta)
        gate = jax.nn.sigmoid(conv)
        active = conv * gate
        pieces = []
        for h in heads:
            grad = rounded(grads[j][h])
            if j < 2:
                raw = lanes(active, h)
                scale = unit_scale(raw)
                unit = raw * scale
                if j == 0:
                    grad = grad * HD ** (-0.5)
                grad = scale * (grad - unit * jnp.sum(unit * grad, axis=-1, keepdims=True))
            pieces.append(grad)
        grad_conv = jnp.concatenate(pieces, axis=1) * (gate * (1.0 + conv * (1.0 - gate)))
        total = None
        for lag in range(CONV):
            taps_grad_ref[j, lag : lag + 1, :] += jnp.sum(grad_conv * shifted[lag], axis=0, keepdims=True)
            spread = grad_conv * (meta[:, lag : lag + 1] * taps[lag : lag + 1, :])
            spread = jnp.concatenate([jnp.zeros((8, span), FULL), spread], axis=0)
            if lag:
                spread = pltpu.roll(spread, BLOCK + 8 - lag, 0)
            total = spread if total is None else total + spread
        bottom = total[BLOCK:] + spill_ref[j]
        spill_ref[j] = total[:8]
        grad_ref[:, at] = jnp.concatenate([total[8:BLOCK], bottom], axis=0).astype(LOW)

        @pl.when(turn == 0)
        def _():
            edge_ref[:, at] = bottom

        lead_ref[:, at] = total[:8]


def backward_blocks(
    projected, rim, taps, strength, meta, meta_row, mixed, solve, weight, update, drift, upstream,
    states, enter, leave,
):
    total, width = projected.shape[0], projected.shape[1] // 3
    head_count = width // HD
    groups, steps = head_count // GROUP, total // BLOCK
    span = GROUP * HD
    strength_col = strength.reshape(total, groups, GROUP).transpose(1, 0, 2)
    ratio = BLOCK // RIM
    back = lambda n: steps - 1 - n
    wide = pl.BlockSpec((BLOCK, span), lambda g, n: (back(n), g))
    deep = pl.BlockSpec((3, BLOCK, span), lambda g, n: (0, back(n), g))
    per_group = pl.BlockSpec((GROUP, HD, HD), lambda g, n: (g, 0, 0))
    flat = pl.BlockSpec((BLOCK, 3 * span), lambda g, n: (back(n), g))
    narrow = pl.BlockSpec((8, 3 * span), lambda g, n: (0, g))
    grads, strength_grad, taps_grad, edge, lead = pl.pallas_call(
        backward_kernel,
        grid=(groups, steps),
        in_specs=[
            flat,
            pl.BlockSpec((RIM, 3 * span), lambda g, n: (jnp.maximum(back(n) * ratio - 1, 0), g)),
            pl.BlockSpec((RIM, 3 * span), lambda g, n: (0, g)),
            pl.BlockSpec((3, CONV, span), lambda g, n: (0, 0, g)),
            pl.BlockSpec((1, BLOCK, GROUP), lambda g, n: (g, back(n), 0)),
            pl.BlockSpec((BLOCK, 8), lambda g, n: (back(n), 0)),
            pl.BlockSpec((8, BLOCK), lambda g, n: (0, back(n))),
            deep,
            pl.BlockSpec((1, GROUP, BLOCK, BLOCK), lambda g, n: (back(n), g, 0, 0)),
            wide,
            wide,
            wide,
            wide,
            pl.BlockSpec((1, GROUP, HD, 2 * HD), lambda g, n: (back(n), g, 0, 0)),
            per_group,
            per_group,
        ],
        out_specs=(
            flat,
            pl.BlockSpec((1, BLOCK, GROUP), lambda g, n: (g, back(n), 0)),
            pl.BlockSpec((3, CONV, span), lambda g, n: (0, 0, g)),
            narrow,
            narrow,
        ),
        out_shape=(
            jax.ShapeDtypeStruct((total, 3 * width), LOW),
            jax.ShapeDtypeStruct((groups, total, GROUP), FULL),
            jax.ShapeDtypeStruct((3, CONV, width), FULL),
            jax.ShapeDtypeStruct((8, 3 * width), FULL),
            jax.ShapeDtypeStruct((8, 3 * width), FULL),
        ),
        scratch_shapes=[pltpu.VMEM((GROUP, HD, HD), FULL), pltpu.VMEM((3, 8, span), FULL)],
        compiler_params=pltpu.CompilerParams(vmem_limit_bytes=48 << 20),
        cost_estimate=pl.CostEstimate(flops=4 << 30, bytes_accessed=24 << 20, transcendentals=0),
    )(
        projected, projected, rim, taps, strength_col, meta, meta_row, mixed, solve, weight, update,
        drift, upstream, states, enter, leave,
    )
    return grads, strength_grad.transpose(1, 0, 2).reshape(total, head_count), taps_grad, edge, lead


def fsdp_split(count):
    along = 4 if count % 4 == 0 else 1
    return along, count // along


def gather_kernel(along, across, seq_count, shard_ref, small_ref, full_ref, small_full_ref, local_sem, small_send,
                  small_recv, z_send, z_recv, x_send, x_recv, core_send, core_recv):
    count = along * across
    seq, mine = lax.axis_index("seq"), lax.axis_index("fsdp")
    core, z, x = lax.rem(seq, 2), lax.div(mine, across), lax.rem(mine, across)
    partner = seq + 1 - 2 * core
    rows = shard_ref.shape[0]
    half = rows // 2
    mesh_id = pl.DeviceIdType.MESH

    barrier = pltpu.get_barrier_semaphore()
    for d in range(1, count):
        pl.semaphore_signal(barrier, inc=1, device_id=(seq, lax.rem(mine + d, count)), device_id_type=mesh_id)
    pl.semaphore_signal(barrier, inc=1, device_id=(partner, mine), device_id_type=mesh_id)
    pl.semaphore_wait(barrier, count)

    def place(k, j):
        owner = lax.rem(z - k + along, along) * across + lax.rem(x - j + across, across)
        start = pl.multiple_of(owner * rows + core * half, 16)
        return full_ref.at[pl.ds(start, half), :]

    own_half = shard_ref.at[pl.ds(pl.multiple_of(core * half, 16), half), :]
    keep = pltpu.make_async_copy(
        shard_ref, full_ref.at[pl.ds(pl.multiple_of(mine * rows, 16), rows), :], local_sem.at[0]
    )
    keep.start()
    small_place = small_full_ref.at[:, pl.ds(pl.multiple_of(mine * 128, 128), 128)]
    keep_small = pltpu.make_async_copy(small_ref, small_place, local_sem.at[1])
    keep_small.start()

    def sent(source, target, send, recv, device):
        copy = pltpu.make_async_remote_copy(
            src_ref=source, dst_ref=target, send_sem=send, recv_sem=recv, device_id=device, device_id_type=mesh_id
        )
        copy.start()
        return copy

    def along_z(k):
        source = own_half if k == 1 else place(k - 1, 0)
        device = (seq, lax.rem(z + 1, along) * across + x)
        return sent(source, place(k - 1, 0), z_send.at[k - 1], z_recv.at[k - 1], device)

    def along_x(k, j):
        source = own_half if k == 0 else place(k, 0)
        at = k * (across - 1) + j - 1
        device = (seq, z * across + lax.rem(x + j, across))
        return sent(source, place(k, 0), x_send.at[at], x_recv.at[at], device)

    def to_core(k, j):
        at = k * across + j
        return sent(place(k, j), place(k, j), core_send.at[at], core_recv.at[at], (partner, mine))

    copies = []
    z_copies = {1: along_z(1)} if along > 1 else {}
    x_copies = {}
    for j in range(1, across):
        x_copies[0, j] = along_x(0, j)
    for d in range(1, count):
        copies.append(
            sent(small_ref, small_place, small_send.at[d - 1], small_recv.at[d - 1],
                 (seq, lax.rem(mine + d, count)))
        )
    core_copies = []
    for k in range(1, along):
        z_copies[k].wait_recv()
        if k + 1 < along:
            z_copies[k + 1] = along_z(k + 1)
        for j in range(1, across):
            x_copies[k, j] = along_x(k, j)
        core_copies.append(to_core(k, 0))
        for j in range(1, across):
            x_copies[k - 1, j].wait_recv()
            core_copies.append(to_core(k - 1, j))
    for j in range(1, across):
        x_copies[along - 1, j].wait_recv()
        core_copies.append(to_core(along - 1, j))
    keep.wait()
    keep_small.wait()
    for copy in list(z_copies.values()) + list(x_copies.values()):
        copy.wait_send()
    for copy in copies + core_copies:
        copy.wait()


def gathered_mixer(shard, small, seq_count, fsdp_count):
    along, across = fsdp_split(fsdp_count)
    rows, width = shard.shape
    dma = pltpu.SemaphoreType.DMA
    hold = pl.BlockSpec(memory_space=pl.ANY)
    links = max(along * (across - 1), 1)
    return pl.pallas_call(
        partial(gather_kernel, along, across, seq_count),
        in_specs=[hold, hold],
        out_specs=(hold, hold),
        out_shape=(
            jax.ShapeDtypeStruct((rows * fsdp_count, width), shard.dtype),
            jax.ShapeDtypeStruct((small.shape[0], fsdp_count * 128), small.dtype),
        ),
        scratch_shapes=[
            dma((2,)),
            dma((fsdp_count - 1,)),
            dma((fsdp_count - 1,)),
            dma((along,)),
            dma((along,)),
            dma((links,)),
            dma((links,)),
            dma((along * across,)),
            dma((along * across,)),
        ],
        compiler_params=pltpu.CompilerParams(collective_id=0, has_side_effects=True),
    )(shard, small)


def core_swapped(value):
    count = lax.axis_size("seq")
    return lax.ppermute(value, "seq", [(i, i + 1 - 2 * (i % 2)) for i in range(count)])


def chip_shifted(value, by):
    count = lax.axis_size("seq")
    return lax.ppermute(value, "seq", [(i, (i + 2 * by) % count) for i in range(count)])


def seq_blocks(value):
    chips = lax.axis_size("seq") // 2
    far = [chip_shifted(value, k) for k in range(1, chips)]
    found = []
    for one in [value] + far:
        found += [one, core_swapped(one)]
    return found


def seq_stacked(value):
    count, index = lax.axis_size("seq"), lax.axis_index("seq")
    core = index % 2
    result = jnp.zeros((count,) + value.shape, value.dtype)
    for place, one in enumerate(seq_blocks(value)):
        chip = (index // 2 - place // 2) % (count // 2)
        at = chip * 2 + (core if place % 2 == 0 else 1 - core)
        result = lax.dynamic_update_slice_in_dim(result, one[None], at, 0)
    return result


def low_dot(left, right, dims):
    return lax.dot_general(left, right, (((dims[0],), (dims[1],)), ((), ())), preferred_element_type=FULL)


def exchange_kernel(backward, seq_count, local_ref, transfer_ref, result_ref, local_low, transfer_low, other_local,
                    other_transfer, chip_ref, sent_ref,
                    swap_send, swap_recv, chip_send, chip_recv, half_send, half_recv):
    seq, mine = lax.axis_index("seq"), lax.axis_index("fsdp")
    core, chip = lax.rem(seq, 2), lax.div(seq, 2)
    partner = seq + 1 - 2 * core
    chips = seq_count // 2
    heads = local_ref.shape[0]
    mesh_id = pl.DeviceIdType.MESH
    lead = core == (1 if backward else 0)
    dims = (0, 0) if backward else (1, 0)
    step = -1 if backward else 1

    for head in range(heads):
        chip_ref[head] = jnp.zeros((HD, HD), LOW)
        local_low[head] = local_ref[head].astype(LOW)
        transfer_low[head] = transfer_ref[head].astype(LOW)
    barrier = pltpu.get_barrier_semaphore()
    pl.semaphore_signal(barrier, inc=1, device_id=(partner, mine), device_id_type=mesh_id)
    for k in range(1, chips):
        other = lax.rem(seq + 2 * k, seq_count)
        pl.semaphore_signal(barrier, inc=1, device_id=(other, mine), device_id_type=mesh_id)
    pl.semaphore_wait(barrier, chips)

    swaps = [
        pltpu.make_async_remote_copy(
            src_ref=source, dst_ref=target, send_sem=swap_send.at[i], recv_sem=swap_recv.at[i],
            device_id=(partner, mine), device_id_type=mesh_id,
        )
        for i, (source, target) in enumerate(((local_low, other_local), (transfer_low, other_transfer)))
    ]
    for swap in swaps:
        swap.start()
    for swap in swaps:
        swap.wait()
    share = pl.ds(pl.multiple_of(core * (heads // 2), heads // 2), heads // 2)

    def applied(matrix, value):
        return product(matrix, value.astype(LOW), dims)

    def by_role(head):
        own_local, own_transfer = local_ref[head], transfer_low[head]
        far_local, far_transfer = other_local[head].astype(FULL), other_transfer[head]
        return (
            jnp.where(lead, own_local, far_local),
            jnp.where(lead, own_transfer, far_transfer),
            jnp.where(lead, far_local, own_local),
            jnp.where(lead, far_transfer, own_transfer),
        )

    for i in range(chips - 1):
        source = chips - 1 - i if backward else i

        @pl.when(chip == source)
        def _():
            for head in range(heads):
                lead_local, lead_transfer, trail_local, trail_transfer = by_role(head)
                inner = lead_local if i == 0 else lead_local + applied(lead_transfer, chip_ref[head])
                sent_ref[head] = (trail_local + applied(trail_transfer, inner)).astype(LOW)

        onward = pltpu.make_async_remote_copy(
            src_ref=sent_ref.at[share], dst_ref=chip_ref.at[share], send_sem=chip_send.at[i], recv_sem=chip_recv.at[i],
            device_id=(lax.rem(seq + 2 * step + seq_count, seq_count), mine), device_id_type=mesh_id,
        )
        half = pltpu.make_async_remote_copy(
            src_ref=chip_ref.at[share], dst_ref=chip_ref.at[share], send_sem=half_send.at[i], recv_sem=half_recv.at[i],
            device_id=(partner, mine), device_id_type=mesh_id,
        )

        @pl.when(chip == source)
        def _():
            onward.start()
            onward.wait_send()

        @pl.when(chip == source + step)
        def _():
            onward.wait_recv()
            half.start()
            half.wait()

    for head in range(heads):
        lead_local, lead_transfer, _, _ = by_role(head)
        state = chip_ref[head]
        result_ref[head] = jnp.where(lead, state.astype(FULL), lead_local + applied(lead_transfer, state))


def exchanged(local, transfer, backward, call_id):
    seq_count = lax.axis_size("seq")
    dma = pltpu.SemaphoreType.DMA
    vmem = pl.BlockSpec(memory_space=pltpu.VMEM)
    hops = max(seq_count // 2 - 1, 1)
    return pl.pallas_call(
        partial(exchange_kernel, backward, seq_count),
        in_specs=[vmem, vmem],
        out_specs=vmem,
        out_shape=jax.ShapeDtypeStruct(local.shape, FULL),
        scratch_shapes=[pltpu.VMEM(local.shape, LOW)] * 6 + [dma((2,))] * 2 + [dma((hops,))] * 4,
        compiler_params=pltpu.CompilerParams(collective_id=call_id, has_side_effects=True, vmem_limit_bytes=24 << 20),
    )(local, transfer)


def norm_back(unit, scale, gain, grad):
    gained = jnp.sum(grad * unit, axis=0)
    grad = grad * gain
    return scale * (grad - unit * jnp.mean(grad * unit, axis=-1, keepdims=True)), gained


def matrix_owners(fsdp_count):
    along, across = fsdp_split(fsdp_count)
    if along == 4 and across > 1:
        first, second = across, 2 * across + 1
        return [(0, first), (0, second), (1, first), (1, second), (1, first + 1), (0, first + 1), (1, second - 1)]
    return [(m % 2, m * fsdp_count // 7) for m in range(7)]


def remote(source, target, send, recv, device):
    return pltpu.make_async_remote_copy(
        src_ref=source, dst_ref=target, send_sem=send, recv_sem=recv, device_id=device,
        device_id_type=pl.DeviceIdType.MESH,
    )


class Place:
    def __init__(self, seq_count, count):
        self.seq_count, self.count, self.chips = seq_count, count, seq_count // 2
        self.seq, self.mine = lax.axis_index("seq"), lax.axis_index("fsdp")
        self.core, self.chip = lax.rem(self.seq, 2), lax.div(self.seq, 2)
        self.partner = (self.seq + 1 - 2 * self.core, self.mine)

    def fsdp(self, d):
        return lax.rem(self.mine + d, self.count)

    def next_seq(self, k):
        return (lax.rem(self.seq + k, self.seq_count), self.mine)

    def next_chip(self, k):
        return (lax.rem(self.seq + 2 * k, self.seq_count), self.mine)

    def greet(self, chips_too):
        barrier = pltpu.get_barrier_semaphore()
        others = [(self.seq, self.fsdp(d)) for d in range(1, self.count)]
        others += [self.next_seq(k) for k in range(1, self.seq_count)] if chips_too else [self.partner]
        for other in others:
            pl.semaphore_signal(barrier, inc=1, device_id=other, device_id_type=pl.DeviceIdType.MESH)
        pl.semaphore_wait(barrier, len(others))


def collect(here, owners, pieces, whole, send, recv, local_sem, core_send, core_recv):
    def piece(n, target, source):
        return remote(pieces.at[n], whole.at[source, here.core], send.at[n], recv.at[source], (here.seq, target))

    for n, (row, owner) in enumerate(owners):
        @pl.when((here.chip == row) & (here.mine != owner))
        def _():
            piece(n, owner, here.mine).start()

    def finish():
        for n, (row, owner) in enumerate(owners):
            @pl.when((here.chip == row) & (here.mine == owner))
            def _():
                keep = pltpu.make_async_copy(pieces.at[n], whole.at[here.mine, here.core], local_sem)
                keep.start()
                for d in range(1, here.count):
                    piece(n, here.fsdp(d), here.fsdp(d)).wait_recv()
                keep.wait()
                half = whole.at[:, here.core]
                swap = remote(half, half, core_send, core_recv, here.partner)
                swap.start()
                swap.wait()

        for n, (row, owner) in enumerate(owners):
            @pl.when((here.chip == row) & (here.mine != owner))
            def _():
                piece(n, owner, here.mine).wait_send()

    return finish


def hand_back(here, owners, rows, parts, local_sem, send, recv, chip_send, chip_recv, core_send, core_recv):
    def part(m):
        return parts.at[m, here.core]

    def piece(m, d):
        return remote(rows.at[here.fsdp(d)], part(m), send.at[d], recv.at[m], (here.seq, here.fsdp(d)))

    def onward(m, k):
        return remote(part(m), part(m), chip_send.at[m, k - 1], chip_recv.at[m], here.next_chip(k))

    def swap(m):
        return remote(part(m), part(m), core_send.at[m], core_recv.at[m], here.partner)

    for m, (row, owner) in enumerate(owners):
        @pl.when((here.chip == row) & (here.mine == owner))
        def _():
            for d in range(1, here.count):
                piece(m, d).start()
            keep = pltpu.make_async_copy(rows.at[here.mine], part(m), local_sem)
            keep.start()
            keep.wait()

    def finish():
        for m, (row, owner) in enumerate(owners):
            @pl.when((here.chip == row) & (here.mine != owner))
            def _():
                piece(m, 0).wait_recv()

            @pl.when(here.chip == row)
            def _():
                for k in range(1, here.chips):
                    onward(m, k).start()
                swap(m).start()

        for m, (row, owner) in enumerate(owners):
            @pl.when(here.chip != row)
            def _():
                onward(m, 1).wait_recv()
                swap(m).start()

        for m, (row, owner) in enumerate(owners):
            swap(m).wait()

            @pl.when(here.chip == row)
            def _():
                for k in range(1, here.chips):
                    onward(m, k).wait_send()

            @pl.when((here.chip == row) & (here.mine == owner))
            def _():
                for d in range(1, here.count):
                    piece(m, d).wait_send()

    return finish


def collect_sems(kinds, count):
    dma = pltpu.SemaphoreType.DMA
    return [dma((kinds,)), dma((count,)), dma, dma, dma]


def hand_back_sems(kinds, count, chips):
    dma = pltpu.SemaphoreType.DMA
    return [dma, dma((count,)), dma((kinds,)), dma((kinds, chips)), dma((kinds,)), dma((kinds,)), dma((kinds,))]


def weight_grad_kernel(seq_count, joint_ref, near_norm, near_top, far_norm, far_top, near_hidden, near_gate, near_up,
                       far_hidden, far_gate, far_up, grads_ref, back_ref, send_sem, recv_sem):
    here = Place(seq_count, 1)
    turn = pl.program_id(0)

    def onward(k):
        device = here.next_chip(here.chips - k)
        return remote(joint_ref.at[k - 1], back_ref.at[k - 1], send_sem.at[k - 1], recv_sem.at[k - 1], device)

    @pl.when(turn == 0)
    def _():
        barrier = pltpu.get_barrier_semaphore()
        for k in range(1, here.chips):
            pl.semaphore_signal(barrier, inc=1, device_id=here.next_chip(k), device_id_type=pl.DeviceIdType.MESH)
        pl.semaphore_wait(barrier, here.chips - 1)
        for k in range(1, here.chips):
            onward(k).start()

    size = near_gate.shape[1]
    near_turned, far_turned = near_norm[...].T, far_norm[...].T
    for j, (near_right, far_right) in enumerate(((near_gate, far_gate), (near_up, far_up))):
        value = product(near_turned, near_right[...]) + product(far_turned, far_right[...])
        grads_ref[:, j * size : (j + 1) * size] = value.astype(LOW)
    value = product(near_top[...].T, near_hidden[...]) + product(far_top[...].T, far_hidden[...])
    grads_ref[:, 2 * size :] = value.astype(LOW)

    @pl.when(turn == pl.num_programs(0) - 1)
    def _():
        for k in range(1, here.chips):
            onward(k).wait()


def weight_grads(joint, near_norm, near_top, far_norm, far_top, near, far, seq_count, call_id):
    width, size = near_norm.shape[1], near[0].shape[1]
    dma = pltpu.SemaphoreType.DMA
    hold = pl.BlockSpec(memory_space=pl.ANY)

    def columns(one):
        return pl.BlockSpec((one.shape[0], TILE), lambda i: (0, i))

    def whole(one):
        return pl.BlockSpec(one.shape, lambda i: (0, 0))

    lefts, rights = (near_norm, near_top, far_norm, far_top), tuple(near) + tuple(far)
    tokens = near_norm.shape[0] + far_norm.shape[0]
    return pl.pallas_call(
        partial(weight_grad_kernel, seq_count),
        grid=(width // TILE,),
        in_specs=[hold] + [columns(one) for one in lefts] + [whole(one) for one in rights],
        out_specs=(pl.BlockSpec((TILE, 3 * size), lambda i: (i, 0)), hold),
        out_shape=(
            jax.ShapeDtypeStruct((width, 3 * size), LOW),
            jax.ShapeDtypeStruct(joint.shape, joint.dtype),
        ),
        scratch_shapes=[dma((max(seq_count // 2 - 1, 1),)), dma((max(seq_count // 2 - 1, 1),))],
        compiler_params=pltpu.CompilerParams(collective_id=call_id, has_side_effects=True, vmem_limit_bytes=48 << 20),
        cost_estimate=pl.CostEstimate(flops=6 * tokens * width * size, bytes_accessed=24 << 20, transcendentals=0),
    )(joint, *lefts, *rights)


def middle_kernel(owners, seq_count, count, part_ref, prior_ref, small_ref, wide_ref, sum_ref, small_out, square_whole,
                  wide_whole, chip_ref, total_ref, piece_ref, place_ref, seq_ref, chip_send, chip_recv, half_sem,
                  place_send, place_recv, seq_send, seq_recv, *sems):
    here = Place(seq_count, count)
    width = piece_ref.shape[2]
    chip_ref[here.chip] = part_ref[...]
    place_ref[here.mine] = small_ref[here.mine]
    here.greet(True)
    small_copies = []
    for d in range(1, count):
        copy = remote(
            small_ref.at[here.fsdp(d)], place_ref.at[here.mine], place_send.at[d - 1], place_recv.at[here.mine],
            (here.seq, here.fsdp(d)),
        )
        copy.start()
        small_copies.append(copy)
    own = chip_ref.at[here.chip]
    onward = [
        remote(own, own, chip_send.at[k - 1], chip_recv.at[here.chip], here.next_chip(k)) for k in range(1, here.chips)
    ]
    for copy in onward:
        copy.start()
    finish_wide = collect(here, owners[:3], wide_ref, wide_whole, *sems[:5])
    for k in range(1, here.chips):
        source = lax.rem(here.chip + k, here.chips)
        other = chip_ref.at[source]
        remote(other, other, chip_send.at[k - 1], chip_recv.at[source], here.next_chip(k)).wait_recv()
    total = chip_ref[0].astype(FULL)
    for i in range(1, here.chips):
        total = total + chip_ref[i].astype(FULL)
    total_ref[...] = total
    fresh = (momentum_decay * prior_ref[...] + total).astype(LOW)
    span = GROUP * HD
    for g in range(width // span):
        for j in range(3):
            at = (3 * g + j) * span
            piece_ref[j, :, g * span : (g + 1) * span] = fresh[:, at : at + span]
    piece_ref[3] = fresh[:, 3 * width :]
    finish_square = collect(here, owners[3:], piece_ref, square_whole, *sems[5:])
    half_copy = remote(total_ref, sum_ref.at[here.core], half_sem.at[0], half_sem.at[1], here.partner)
    half_copy.start()
    keep = pltpu.make_async_copy(total_ref, sum_ref.at[here.core], half_sem.at[2])
    keep.start()
    for d in range(1, count):
        source = here.fsdp(d)
        other = place_ref.at[source]
        remote(other, other, place_send.at[d - 1], place_recv.at[source], (here.seq, source)).wait_recv()
    small = place_ref[0]
    for i in range(1, count):
        small = small + place_ref[i]
    seq_ref[here.seq] = small
    own = seq_ref.at[here.seq]
    for k in range(1, seq_count):
        copy = remote(own, own, seq_send.at[k - 1], seq_recv.at[here.seq], here.next_seq(k))
        copy.start()
        small_copies.append(copy)
    for k in range(1, seq_count):
        source = lax.rem(here.seq + k, seq_count)
        other = seq_ref.at[source]
        remote(other, other, seq_send.at[k - 1], seq_recv.at[source], here.next_seq(k)).wait_recv()
    small = seq_ref[0]
    for i in range(1, seq_count):
        small = small + seq_ref[i]
    small_out[...] = small
    finish_square()
    finish_wide()
    keep.wait()
    half_copy.wait()
    for copy in onward + small_copies:
        copy.wait_send()


def middle(part, prior, small, wide, owners, call_id, seq_count, count):
    half, columns = part.shape
    width = columns // 4
    chips = seq_count // 2
    dma = pltpu.SemaphoreType.DMA
    hold, vmem = pl.BlockSpec(memory_space=pl.ANY), pl.BlockSpec(memory_space=pltpu.VMEM)
    return pl.pallas_call(
        partial(middle_kernel, owners, seq_count, count),
        in_specs=[vmem, vmem, vmem, hold],
        out_specs=(hold, vmem, hold, hold),
        out_shape=(
            jax.ShapeDtypeStruct((2, half, columns), FULL),
            jax.ShapeDtypeStruct(small.shape[1:], FULL),
            jax.ShapeDtypeStruct((count, 2, half, width), LOW),
            jax.ShapeDtypeStruct((count, 2) + wide.shape[1:], LOW),
        ),
        scratch_shapes=[
            pltpu.VMEM((chips, half, columns), LOW),
            pltpu.VMEM((half, columns), FULL),
            pltpu.VMEM((4, half, width), LOW),
            pltpu.VMEM(small.shape, FULL),
            pltpu.VMEM((seq_count,) + small.shape[1:], FULL),
            dma((max(chips - 1, 1),)),
            dma((chips,)),
            dma((3,)),
            dma((count,)),
            dma((count,)),
            dma((seq_count,)),
            dma((seq_count,)),
        ]
        + collect_sems(3, count)
        + collect_sems(4, count),
        compiler_params=pltpu.CompilerParams(collective_id=call_id, has_side_effects=True, vmem_limit_bytes=24 << 20),
    )(part, prior, small, wide)


def hand_back_kernel(owners, seq_count, count, wide_ref, square_ref, wide_parts, square_parts, *sems):
    here = Place(seq_count, count)
    here.greet(True)
    finish_square = hand_back(here, owners[3:], square_ref, square_parts, *sems[7:])
    finish_wide = hand_back(here, owners[:3], wide_ref, wide_parts, *sems[:7])
    finish_square()
    finish_wide()


def handed_back(wide_rows, square_rows, owners, call_id, seq_count, count):
    hold = pl.BlockSpec(memory_space=pl.ANY)
    chips = seq_count // 2
    return pl.pallas_call(
        partial(hand_back_kernel, owners, seq_count, count),
        in_specs=[hold, hold],
        out_specs=(hold, hold),
        out_shape=(
            jax.ShapeDtypeStruct((3, 2) + wide_rows.shape[1:], LOW),
            jax.ShapeDtypeStruct((4, 2) + square_rows.shape[1:], LOW),
        ),
        scratch_shapes=hand_back_sems(3, count, chips) + hand_back_sems(4, count, chips),
        compiler_params=pltpu.CompilerParams(collective_id=call_id, has_side_effects=True),
    )(wide_rows, square_rows)


def tile_count(width, seq_count):
    return -(-(width // HD) // seq_count)


def prepare_kernel(seq_count, mixer_ref, output_ref, gate_up_ref, down_ref, strength_ref, filter_ref, gain_ref, head_ref,
                   square_ref, ff_ref, small_ref):
    shard, width = output_ref.shape
    span = GROUP * HD
    tiles = gate_up_ref.shape[2] // HD
    per = tile_count(gate_up_ref.shape[2], seq_count)
    seq = lax.axis_index("seq")
    for g in range(width // span):
        for j in range(3):
            at = (3 * g + j) * span
            square_ref[:, at : at + span] = mixer_ref[j, :, g * span : (g + 1) * span].astype(LOW)
    square_ref[:, 3 * width :] = output_ref[...].astype(LOW)
    for i in range(per):
        tile = i * seq_count + seq
        at = pl.ds(pl.multiple_of(jnp.minimum(tile, tiles - 1) * HD, HD), HD)
        kept = jnp.where(tile < tiles, 1.0, 0.0).astype(FULL)
        for j in range(2):
            to = (j * per + i) * HD
            ff_ref[:, to : to + HD] = (gate_up_ref[j, :, at] * kept).astype(LOW)
        to = (2 * per + i) * HD
        ff_ref[:, to : to + HD] = (down_ref[at, :] * kept).T.astype(LOW)
    small_ref[...] = jnp.zeros_like(small_ref)
    heads = strength_ref.shape[1]
    rows = [strength_ref[...].T] + [filter_ref[j] for j in range(3)] + [gain_ref[...]]
    at = 0
    for one in rows:
        small_ref[at : at + one.shape[0], :shard] = one.astype(LOW)
        at += one.shape[0]
    small_ref[at : at + 1, : head_ref.shape[1]] = head_ref[...].astype(LOW)


def prepared(mixer, output, gate_up, down, strength, filters, gain, head, seq_count):
    shard, width = output.shape
    columns = 3 * tile_count(gate_up.shape[2], seq_count) * HD
    vmem = pl.BlockSpec(memory_space=pltpu.VMEM)
    return pl.pallas_call(
        partial(prepare_kernel, seq_count),
        in_specs=[vmem] * 8,
        out_specs=(vmem,) * 3,
        out_shape=(
            jax.ShapeDtypeStruct((shard, 4 * width), LOW),
            jax.ShapeDtypeStruct((shard, columns), LOW),
            jax.ShapeDtypeStruct((32, 128), LOW),
        ),
        compiler_params=pltpu.CompilerParams(vmem_limit_bytes=40 << 20),
    )(mixer, output, gate_up, down, strength, filters, gain, head[None])


def wide_moment_kernel(seq_count, gate_up_ref, down_ref, stack_ref, gate_up_out, down_out, sent_ref, hold_ref):
    half = sent_ref.shape[1]
    tiles = gate_up_ref.shape[2] // HD
    per = stack_ref.shape[2] // (3 * HD)
    core = lax.rem(lax.axis_index("seq"), 2)
    mine = pl.ds(pl.multiple_of(core * half, half), half)
    for t in range(tiles):
        source, i = t % seq_count, t // seq_count
        at = slice(t * HD, (t + 1) * HD)
        for j in range(2):
            grad = stack_ref[source, :, (j * per + i) * HD : (j * per + i + 1) * HD].astype(FULL)
            gate_up_out[j, :, at] = momentum_decay * gate_up_ref[j, :, at] + grad
            sent_ref[j, :, at] = gate_up_out[j, mine, at].astype(LOW)
        grad = stack_ref[source, :, (2 * per + i) * HD : (2 * per + i + 1) * HD].astype(FULL)
        fresh = momentum_decay * down_ref[at, :] + grad.T
        down_out[at, :] = fresh
        hold_ref[...] = fresh.T
        sent_ref[2, :, at] = hold_ref[mine, :].astype(LOW)


def wide_moments(gate_up, down, stack, seq_count):
    shard, width = gate_up.shape[1:]
    vmem = pl.BlockSpec(memory_space=pltpu.VMEM)
    return pl.pallas_call(
        partial(wide_moment_kernel, seq_count),
        in_specs=[vmem] * 3,
        out_specs=(vmem,) * 3,
        out_shape=(
            jax.ShapeDtypeStruct(gate_up.shape, FULL),
            jax.ShapeDtypeStruct(down.shape, FULL),
            jax.ShapeDtypeStruct((3, shard // 2, width), LOW),
        ),
        scratch_shapes=[pltpu.VMEM((shard, HD), FULL)],
        compiler_params=pltpu.CompilerParams(vmem_limit_bytes=40 << 20),
    )(gate_up, down, stack)


def finish_kernel(
    wide_ref, square_ref, sum_ref, small_ref, mixer_w, output_w, gate_up_w, down_w, strength_w, filter_w, gain_w, head_w,
    mixer_m, output_m, strength_m, filter_m, gain_m, head_m,
    new_mixer_m, new_mixer_w, new_strength_m, new_strength_w, new_filter_m, new_filter_w, new_gain_m, new_gain_w,
    new_head_m, new_head_w, new_output_m, new_output_w, new_gate_up_w, new_down_w,
):
    shard, width = output_w.shape
    span = GROUP * HD
    for g in range(width // span):
        for j in range(3):
            at, to = (3 * g + j) * span, slice(g * span, (g + 1) * span)
            new_mixer_m[j, :, to] = momentum_decay * mixer_m[j, :, to] + sum_ref[:, at : at + span]
    for j in range(3):
        new_mixer_w[j] = mixer_w[j] - matrix_rate * square_ref[j].astype(FULL)
    new_output_m[...] = momentum_decay * output_m[...] + sum_ref[:, 3 * width :]
    new_output_w[...] = output_w[...] - matrix_rate * square_ref[3].astype(FULL)
    for j in range(2):
        new_gate_up_w[j] = gate_up_w[j] - matrix_rate * wide_ref[j].astype(FULL)
    for t in range(down_w.shape[0] // HD):
        at = slice(t * HD, (t + 1) * HD)
        new_down_w[at, :] = down_w[at, :] - matrix_rate * wide_ref[2, :, at].astype(FULL).T
    heads = strength_w.shape[1]
    fresh = momentum_decay * strength_m[...] + small_ref[:heads, :].T
    new_strength_m[...] = fresh
    new_strength_w[...] = strength_w[...] - strength_rate * fresh
    for j in range(3):
        fresh = momentum_decay * filter_m[j] + small_ref[heads + CONV * j : heads + CONV * (j + 1), :]
        new_filter_m[j] = fresh
        new_filter_w[j] = filter_w[j] - filter_rate * fresh
    at = heads + 3 * CONV
    fresh = momentum_decay * gain_m[...] + small_ref[at : at + 2, :]
    new_gain_m[...] = fresh
    new_gain_w[...] = gain_w[...] - gain_rate * fresh
    fresh = momentum_decay * head_m[...] + small_ref[at + 2 : at + 3, : head_m.shape[1]]
    new_head_m[...] = fresh
    new_head_w[...] = head_w[...] - gain_rate * fresh


def finished(wide, square, total, small, weights, moments):
    mixer_w, output_w, gate_up_w, down_w, strength_w, filter_w, gain_w, head_w = weights
    mixer_m, output_m, strength_m, filter_m, gain_m, head_m = moments
    pairs = [mixer_w, strength_w, filter_w, gain_w, head_w[None], output_w]
    shapes = [jax.ShapeDtypeStruct(one.shape, FULL) for pair in zip(pairs, pairs) for one in pair]
    shapes += [jax.ShapeDtypeStruct(one.shape, FULL) for one in (gate_up_w, down_w)]
    vmem = pl.BlockSpec(memory_space=pltpu.VMEM)
    return pl.pallas_call(
        finish_kernel,
        in_specs=[vmem] * 18,
        out_specs=(vmem,) * len(shapes),
        out_shape=tuple(shapes),
        compiler_params=pltpu.CompilerParams(vmem_limit_bytes=56 << 20),
    )(
        wide, square, total, small, mixer_w, output_w, gate_up_w, down_w, strength_w, filter_w, gain_w, head_w[None],
        mixer_m, output_m, strength_m, filter_m, gain_m, head_m[None],
    )


TILE = 256


def row_loop(rows, body):
    @pl.loop(0, rows // TILE)
    def _(i):
        body(pl.ds(pl.multiple_of(i * TILE, TILE), TILE))


def trace_of(square_ref):
    total = jnp.zeros((1, 1), FULL)
    for i in range(square_ref.shape[0] // TILE):
        tile = square_ref[i * TILE : (i + 1) * TILE, i * TILE : (i + 1) * TILE]
        rows = lax.broadcasted_iota(jnp.int32, (TILE, TILE), 0)
        cols = lax.broadcasted_iota(jnp.int32, (TILE, TILE), 1)
        total = total + jnp.sum(jnp.where(rows == cols, tile, 0.0), keepdims=True)
    return total


def pick_rows(count, half, source_ref, target_ref):
    core = lax.rem(lax.axis_index("seq"), 2)
    for f in range(count):
        at = pl.multiple_of(f * 2 * half + core * half, 16)
        target_ref[f * half : (f + 1) * half, :] = source_ref[pl.ds(at, half), :]


def orth_wide_kernel(
    count, half, whole_ref, out_ref, square_ref, middle_ref, mapped_ref, gathered_ref,
    square_low, mapped_low, first_low, second_low, rows_low, rows_own,
):
    size = whole_ref.shape[0]

    def start(at):
        square_ref[at, :] = product(whole_ref[at, :], whole_ref[...], (1, 1))

    row_loop(size, start)
    scale = 1.0 / (jnp.sqrt(trace_of(square_ref)) + 1e-07)

    def scaled(at):
        value = square_ref[at, :] * (scale * scale)
        square_ref[at, :] = value
        square_low[at, :] = value.astype(LOW)

    row_loop(size, scaled)
    level = 1.0
    gathered_low, spare_low = first_low, second_low
    for sweep in range(NS_STEPS - 1):
        keep_ref = gathered_ref if sweep == 0 else mapped_ref

        def mapping(at):
            value = coef_cubic * square_ref[at, :] + coef_quintic * product(square_low[at, :], square_low[...])
            keep_ref[at, :] = value
            mapped_low[at, :] = value.astype(LOW)

        row_loop(size, mapping)
        if sweep == 0:
            def copy_low(at):
                gathered_low[at, :] = mapped_low[at, :]

            row_loop(size, copy_low)
        else:
            def gather(at):
                value = (
                    coef_linear * gathered_ref[at, :]
                    + level * mapped_ref[at, :]
                    + product(mapped_low[at, :], gathered_low[...])
                )
                gathered_ref[at, :] = value
                spare_low[at, :] = value.astype(LOW)

            row_loop(size, gather)
            gathered_low, spare_low = spare_low, gathered_low
        level = level * coef_linear

        def middle(at):
            value = coef_linear * square_ref[at, :] + product(mapped_low[at, :], square_low[...])
            middle_ref[at, :] = value
            spare_low[at, :] = value.astype(LOW)

        row_loop(size, middle)

        def squared(at):
            value = coef_linear * middle_ref[at, :] + product(spare_low[at, :], mapped_low[...])
            square_ref[at, :] = value
            square_low[at, :] = value.astype(LOW)

        row_loop(size, squared)

    pick_rows(count, half, square_low, rows_low)
    pick_rows(count, half, square_ref, mapped_ref)
    pick_rows(count, half, gathered_ref, middle_ref)
    pick_rows(count, half, whole_ref, rows_own)

    def last(at):
        mapped = coef_cubic * mapped_ref[at, :] + coef_quintic * product(rows_low[at, :], square_low[...])
        value = coef_linear * middle_ref[at, :] + level * mapped + product(mapped.astype(LOW), gathered_low[...])
        rows_low[at, :] = value.astype(LOW)

    row_loop(size // 2, last)
    level = level * coef_linear

    @pl.loop(0, whole_ref.shape[1] // TILE)
    def _(i):
        at = pl.ds(pl.multiple_of(i * TILE, TILE), TILE)
        value = level * rows_own[:, at].astype(FULL) + product(rows_low[...], whole_ref[:, at])
        out_ref[:, at] = (value * scale).astype(LOW)


def orth_square_kernel(
    count, half, whole_ref, out_ref, square_ref, current_ref, square_low, mapped_low, first_low, second_low,
    rows_low, rows_own,
):
    size = whole_ref.shape[0]

    def start(at):
        square_ref[at, :] = product(whole_ref[at, :], whole_ref[...], (1, 1))

    row_loop(size, start)
    scale = 1.0 / (jnp.sqrt(trace_of(square_ref)) + 1e-07)

    def scaled(at):
        value = whole_ref[at, :].astype(FULL) * scale
        current_ref[at, :] = value
        first_low[at, :] = value.astype(LOW)
        value = square_ref[at, :] * (scale * scale)
        square_ref[at, :] = value
        square_low[at, :] = value.astype(LOW)

    row_loop(size, scaled)
    now, later = first_low, second_low
    for sweep in range(NS_STEPS):
        if sweep:
            def squared(at):
                value = product(now[at, :], now[...], (1, 1))
                square_ref[at, :] = value
                square_low[at, :] = value.astype(LOW)

            row_loop(size, squared)

        def mapping(at):
            value = coef_cubic * square_ref[at, :] + coef_quintic * product(square_low[at, :], square_low[...])
            mapped_low[at, :] = value.astype(LOW)

        row_loop(size, mapping)
        if sweep < NS_STEPS - 1:
            def step(at):
                value = coef_linear * current_ref[at, :] + product(mapped_low[at, :], now[...])
                current_ref[at, :] = value
                later[at, :] = value.astype(LOW)

            row_loop(size, step)
            now, later = later, now
    pick_rows(count, half, mapped_low, rows_low)
    pick_rows(count, half, current_ref, rows_own)

    @pl.loop(0, size // TILE)
    def _(i):
        at = pl.ds(pl.multiple_of(i * TILE, TILE), TILE)
        value = coef_linear * rows_own[:, at] + product(rows_low[...], now[:, at])
        out_ref[:, at] = value.astype(LOW)


def orth_call(kernel, scratch, count, whole):
    half, width = whole.shape[2:]
    size = count * 2 * half
    flat = whole.reshape(size, width)
    vmem = pl.BlockSpec(memory_space=pltpu.VMEM)
    result = pl.pallas_call(
        partial(kernel, count, half),
        in_specs=[vmem],
        out_specs=vmem,
        out_shape=jax.ShapeDtypeStruct((size // 2, width), LOW),
        scratch_shapes=scratch(size, width),
        compiler_params=pltpu.CompilerParams(vmem_limit_bytes=56 << 20),
    )(flat)
    return result.reshape(count, half, width)


def orth_wide(count, whole):
    def scratch(size, width):
        return (
            [pltpu.VMEM((size, size), FULL)] * 4
            + [pltpu.VMEM((size, size), LOW)] * 4
            + [pltpu.VMEM((size // 2, size), LOW), pltpu.VMEM((size // 2, width), LOW)]
        )

    return orth_call(orth_wide_kernel, scratch, count, whole)


def orth_square(count, whole):
    def scratch(size, width):
        return (
            [pltpu.VMEM((size, size), FULL)] * 2
            + [pltpu.VMEM((size, size), LOW)] * 4
            + [pltpu.VMEM((size // 2, size), LOW), pltpu.VMEM((size // 2, width), FULL)]
        )

    return orth_call(orth_square_kernel, scratch, count, whole)


def chosen_place(owners, mine, chip):
    chosen = (mine == owners[0][1]) & (chip == owners[0][0])
    for row, place in owners[1:]:
        chosen = chosen | ((mine == place) & (chip == row))
    return chosen


def orthogonal(whole, owners, method, mine, chip, count):
    half, width = whole.shape[2:]
    return lax.cond(
        chosen_place(owners, mine, chip),
        partial(method, count),
        lambda one: jnp.zeros((count, half, width), LOW),
        whole,
    )


def on_device(
    inputs,
    cotangent,
    lengths,
    mixer_weight,
    strength_weight,
    filter_weight,
    norm_gain,
    head_gain,
    output_weight,
    gate_up_weight,
    down_weight,
    mixer_moment,
    strength_moment,
    filter_moment,
    gain_moment,
    head_gain_moment,
    output_moment,
    gate_up_moment,
    down_moment,
):
    seq_count = lax.axis_size("seq")
    seq_index = lax.axis_index("seq")
    fsdp_count = lax.axis_size("fsdp")
    fsdp_index = lax.axis_index("fsdp")
    row_count, width = inputs.shape
    shard = width // fsdp_count
    heads_all = strength_weight.shape[1]

    wide_ff = tile_count(gate_up_weight.shape[2], seq_count) * HD
    core = seq_index % 2
    half = shard // 2
    groups = heads_all // GROUP
    span = GROUP * HD
    small_count = heads_all + 3 * CONV + 3
    top_near = core_swapped(cotangent)
    top_far = [chip_shifted(cotangent, k) for k in range(1, seq_count // 2)]
    square_own, ff_own, small_own = prepared(
        mixer_weight, output_weight, gate_up_weight, down_weight, strength_weight, filter_weight, norm_gain, head_gain,
        seq_count,
    )
    square_full, small_full = gathered_mixer(square_own, small_own, seq_count, fsdp_count)
    by_place = small_full.reshape(-1, fsdp_count, 128)
    small_wide = small_full if shard == 128 else by_place[:, :, :shard].reshape(-1, width)
    strength_full = small_wide[:heads_all]
    filters_wide = small_wide[heads_all : heads_all + 3 * CONV].reshape(3, CONV, width).astype(FULL)
    gains_wide = small_wide[heads_all + 3 * CONV : heads_all + 3 * CONV + 2].astype(FULL)
    head_part = head_gain.shape[0]
    head_gain_full = by_place[small_count - 1, :, :head_part].reshape(1, HD).astype(FULL)

    square_full, ff_own, top_near, top_far = lax.optimization_barrier((square_full, ff_own, top_near, top_far))
    top_parts = [cotangent, top_near] + [part for one in top_far for part in (one, core_swapped(one))]
    ff_full = lax.all_gather(ff_own, "fsdp", axis=0, tiled=True)
    mixer_full, output_full = square_full[:, : 3 * width], square_full[:, 3 * width :]
    ff_parts = [ff_full[:, j * wide_ff : (j + 1) * wide_ff] for j in range(3)]

    my_lengths = lax.dynamic_slice_in_dim(lengths, fsdp_index, 1, 0)[0]
    doc_ends = jnp.cumsum(my_lengths)

    def passed_docs(at):
        return (at[:, None] >= doc_ends[None, :]).astype(jnp.int32)

    own = seq_index * row_count + jnp.arange(row_count, dtype=jnp.int32)
    passed = passed_docs(own)
    segment = jnp.sum(passed, axis=1)
    doc_first = jnp.sum(passed * my_lengths[None, :], axis=1)
    block_start = own.reshape(-1, BLOCK)[:, 0]
    before = jnp.where(block_start == 0, -1, jnp.sum(passed_docs(block_start - 1), axis=1))
    blocked = segment.reshape(-1, BLOCK)
    carried = (blocked == before[:, None]).reshape(-1)
    trailing = (blocked == blocked[:, -1:]).reshape(-1)
    columns = [own - lag >= doc_first for lag in range(CONV)] + [carried, trailing, segment]
    meta = jnp.stack([one.astype(FULL) for one in columns] + [jnp.zeros((row_count,), FULL)], axis=1)
    meta_row = jnp.broadcast_to(segment.astype(FULL)[None, :], (8, row_count))

    residual_in = inputs.astype(FULL)
    scale_one = lax.rsqrt(jnp.mean(residual_in * residual_in, axis=-1, keepdims=True) + norm_eps)
    unit_one = residual_in * scale_one
    normed_low = (unit_one * gains_wide[0]).astype(LOW)
    projected = low_dot(normed_low, mixer_full, (1, 0)).astype(LOW)
    logits = low_dot(normed_low, strength_full, (1, 1))
    strength = jax.nn.sigmoid(logits).astype(LOW).astype(FULL)
    forth = [(i, i + 1) for i in range(seq_count - 1)]
    rim = lax.ppermute(projected[row_count - RIM :], "seq", forth)
    mixed, solve, weight, update, drift, local_out, effective, states, end, transfer = forward_blocks(
        projected, rim, filters_wide, strength, meta, meta_row
    )
    enter = exchanged(end, transfer, False, 4)
    delta_out, head_normed = head_outputs(local_out, effective, enter, head_gain_full)
    residual = residual_in + low_dot(head_normed, output_full, (1, 0))
    scale_two = lax.rsqrt(jnp.mean(residual * residual, axis=-1, keepdims=True) + norm_eps)
    unit_two = residual * scale_two
    normed_two = (unit_two * gains_wide[1]).astype(LOW)
    gate_full, up_full, down_full = ff_parts
    chips = seq_count // 2
    near_norm = jnp.concatenate([normed_two, core_swapped(normed_two)])
    far_straight = [chip_shifted(normed_two, k) for k in range(1, chips)]

    def spread_out(normed_part, top_part):
        gate = low_dot(normed_part, gate_full, (1, 0))
        up = low_dot(normed_part, up_full, (1, 0))
        gate_sigmoid = jax.nn.sigmoid(gate)
        gate_silu = gate * gate_sigmoid
        hidden = (gate_silu * up).astype(LOW)
        grad_hidden = low_dot(top_part, down_full, (1, 0))
        grad_gate = (grad_hidden * up * (gate_sigmoid * (1.0 + gate * (1.0 - gate_sigmoid)))).astype(LOW)
        grad_up = (grad_hidden * gate_silu).astype(LOW)
        return hidden, grad_gate, grad_up

    def grad_in(values):
        return low_dot(values[1], gate_full, (1, 1)) + low_dot(values[2], up_full, (1, 1))

    near_top, far_top = jnp.concatenate(top_parts[:2]), jnp.concatenate(top_parts[2:])
    near = spread_out(near_norm, near_top)
    far_straight, near = lax.optimization_barrier((far_straight, near))
    far_parts = [part for one in far_straight for part in (one, core_swapped(one))]
    near_grad = grad_in(near)
    near_back = core_swapped(near_grad[row_count:].astype(LOW))
    near_grad, far_parts = lax.optimization_barrier((near_grad, far_parts))
    far_norm = jnp.concatenate(far_parts)
    far = spread_out(far_norm, far_top)

    def picked(values, side):
        size = 2 * row_count
        return [
            tuple(one[i * size + side * row_count : i * size + (side + 1) * row_count] for one in values)
            for i in range(chips - 1)
        ]

    crossed = [core_swapped(grad_in(one).astype(LOW)) for one in picked(far, 1)]
    joint = [(grad_in(one) + other.astype(FULL)).astype(LOW) for one, other in zip(picked(far, 0), crossed)]
    ff_grads, back_parts = weight_grads(
        jnp.stack(joint), near_norm, near_top, far_norm, far_top, near, far, seq_count, 6
    )
    ff_part = lax.psum_scatter(ff_grads, "fsdp", scatter_dimension=0, tiled=True)
    back_parts = [near_back] + [back_parts[k] for k in range(chips - 1)]
    grad_normed_two = near_grad[:row_count] + sum(one.astype(FULL) for one in back_parts)
    back_two, grad_gain_two = norm_back(unit_two, scale_two, gains_wide[1], grad_normed_two)
    grad_residual = back_two + cotangent.astype(FULL)
    grad_attention = grad_residual.astype(LOW)
    grad_head_normed = low_dot(grad_attention, output_full, (1, 1)).astype(LOW)

    upstream, adjoint_local, grad_head_gain = head_back(
        grad_head_normed, delta_out, effective, head_gain_full
    )
    leave = exchanged(adjoint_local, transfer, True, 5)
    grad_projected, grad_strength, grad_filter, edge, lead = backward_blocks(
        projected, rim, filters_wide, strength, meta, meta_row, mixed, solve, weight, update, drift,
        upstream, states, enter, leave,
    )
    back = [(i + 1, i) for i in range(seq_count - 1)]
    incoming = lax.ppermute(lead.astype(LOW), "seq", back).astype(FULL)
    grad_projected = lax.dynamic_update_slice(
        grad_projected, (edge + incoming).astype(LOW), (row_count - 8, 0)
    )
    grad_strength = grad_strength.astype(LOW).astype(FULL)
    grad_logits = (grad_strength * strength * (1.0 - strength)).astype(LOW)
    def core_rows(values):
        by_core = values.reshape(row_count, fsdp_count, 2, half)
        return [
            lax.dynamic_slice_in_dim(by_core, at, 1, 2).reshape(row_count, width // 2) for at in (core, 1 - core)
        ]

    grad_mixer = [low_dot(one, grad_projected, (0, 0)) for one in core_rows(normed_low)]
    grad_output = [low_dot(one, grad_attention, (0, 0)) for one in core_rows(head_normed)]
    square_grads = jnp.concatenate(
        [
            (mine + core_swapped(other.astype(LOW)).astype(FULL)).astype(LOW)
            for mine, other in (grad_mixer, grad_output)
        ],
        axis=1,
    )
    near_hidden, far_hidden = near[0], far[0]
    square_grads, ff_part, grad_projected, grad_logits, near_hidden, far_hidden = lax.optimization_barrier(
        (square_grads, ff_part, grad_projected, grad_logits, near_hidden, far_hidden)
    )
    far_out, near_out = low_dot(far_hidden, down_full, (1, 1)), low_dot(near_hidden, down_full, (1, 1))
    out_crossed = [core_swapped(one[0].astype(LOW)) for one in picked((far_out,), 1)]
    out_joint = [(one[0] + other.astype(FULL)).astype(LOW) for one, other in zip(picked((far_out,), 0), out_crossed)]
    out_parts = [chip_shifted(one, -(k + 1)) for k, one in enumerate(out_joint)]
    out_near = near_out[:row_count] + core_swapped(near_out[row_count:].astype(LOW)).astype(FULL)
    square_part = lax.psum_scatter(square_grads, "fsdp", scatter_dimension=0, tiled=True)
    grad_strength_weight = low_dot(grad_logits, normed_low, (0, 0))
    grad_normed = low_dot(grad_logits, strength_full, (1, 0)) + low_dot(grad_projected, mixer_full, (1, 1))
    ff_stack = seq_stacked(ff_part)
    back_one, grad_gain_one = norm_back(unit_one, scale_one, gains_wide[0], grad_normed)
    input_grad = grad_residual + back_one

    head_row = jnp.pad(
        grad_head_gain.reshape(fsdp_count, head_part), ((0, 0), (0, shard - head_part))
    ).reshape(1, width)
    small_grads = jnp.concatenate(
        [
            grad_strength_weight,
            grad_filter.reshape(3 * CONV, width),
            grad_gain_one[None],
            grad_gain_two[None],
            head_row,
            jnp.zeros((-small_count % 8, width), FULL),
        ],
        axis=0,
    )
    small_pieces = small_grads.reshape(-1, fsdp_count, shard).transpose(1, 0, 2)

    ff_stack, input_grad, small_pieces = lax.optimization_barrier((ff_stack, input_grad, small_pieces))
    new_gate_up_moment, new_down_moment, wide_sent = wide_moments(gate_up_moment, down_moment, ff_stack, seq_count)
    owners = tuple(matrix_owners(fsdp_count))
    chip = seq_index // 2
    mixer_prior = lax.dynamic_slice_in_dim(mixer_moment, core * half, half, 1)
    output_prior = lax.dynamic_slice_in_dim(output_moment, core * half, half, 0)
    square_prior = jnp.concatenate(
        [mixer_prior[j, :, g * span : (g + 1) * span] for g in range(groups) for j in range(3)] + [output_prior], axis=1
    )
    block_output = residual + (out_near + sum(one.astype(FULL) for one in out_parts))
    wide_sent, square_prior, block_output = lax.optimization_barrier((wide_sent, square_prior, block_output))
    square_sum, small_own, square_all, wide_all = middle(
        square_part, square_prior, small_pieces, wide_sent, owners, 2, seq_count, fsdp_count
    )
    square_rows = orthogonal(square_all, owners[3:], orth_square, fsdp_index, chip, fsdp_count)
    wide_rows = orthogonal(wide_all, owners[:3], orth_wide, fsdp_index, chip, fsdp_count)
    wide_parts, square_parts = handed_back(wide_rows, square_rows, owners, 3, seq_count, fsdp_count)
    weights = (
        mixer_weight, output_weight, gate_up_weight, down_weight, strength_weight, filter_weight, norm_gain, head_gain
    )
    moments = (mixer_moment, output_moment, strength_moment, filter_moment, gain_moment, head_gain_moment)
    done = finished(
        wide_parts.reshape(3, shard, -1),
        square_parts.reshape(4, shard, width),
        square_sum.reshape(shard, -1),
        small_own,
        weights,
        moments,
    )
    head_pair = [one[0] for one in done[8:10]]
    return (
        (block_output, input_grad)
        + tuple(done[:8])
        + tuple(head_pair)
        + tuple(done[10:12])
        + (new_gate_up_moment, done[12], new_down_moment, done[13])
    )


def solution(mesh):
    return jax.shard_map(
        on_device,
        mesh=mesh,
        in_specs=(
            P(("seq", "fsdp"), None),
            P(("seq", "fsdp"), None),
            P(),
            P(None, "fsdp", None),
            P("fsdp", None),
            P(None, None, "fsdp"),
            P(None, "fsdp"),
            P("fsdp"),
            P("fsdp", None),
            P(None, "fsdp", None),
            P(None, "fsdp"),
            P(None, "fsdp", None),
            P("fsdp", None),
            P(None, None, "fsdp"),
            P(None, "fsdp"),
            P("fsdp"),
            P("fsdp", None),
            P(None, "fsdp", None),
            P(None, "fsdp"),
        ),
        out_specs=(
            P(("seq", "fsdp"), None),
            P(("seq", "fsdp"), None),
            P(None, "fsdp", None),
            P(None, "fsdp", None),
            P("fsdp", None),
            P("fsdp", None),
            P(None, None, "fsdp"),
            P(None, None, "fsdp"),
            P(None, "fsdp"),
            P(None, "fsdp"),
            P("fsdp"),
            P("fsdp"),
            P("fsdp", None),
            P("fsdp", None),
            P(None, "fsdp", None),
            P(None, "fsdp", None),
            P(None, "fsdp"),
            P(None, "fsdp"),
        ),
        check_vma=False,
    )
```
